128 devices in a mesh: tm: 32 (over x, z, core), band: 4 (over y).
Axes of the slice: x: 4, y: 4, z: 4, core: 2. Of those that a mesh axis runs over, the one named last changes fastest.
Arguments:
- section_in: bfloat16 [64, 32, 8, 512], P('tm', 'band'), may hold values from -6 to 6
- norm_gain: float32 [512], replicated, may hold values from 0.1 to 1.9
- conv_weight: bfloat16 [3, 3, 3, 512, 512], replicated, may hold values from -0.0546875 to 0.0546875
- conv_bias: float32 [512], replicated, may hold values from -2 to 2
- lengths: int32 [4], replicated, may hold values from 1 to 48, as said below
- embed_weight: bfloat16 [512, 3072], replicated, may hold values from -0.25 to 0.25
- embed_bias: float32 [3072], replicated, may hold values from -3 to 3
- mod_shift: float32 [3072], replicated, may hold values from -3 to 3
- mod_scale: float32 [3072], replicated, may hold values from -1.5 to 1.5
- qkv_weight: bfloat16 [3072, 3, 12, 128], P(None, None, 'band'), may hold values from -0.109375 to 0.109375
- q_gain: float32 [128], replicated, may hold values from 1.2 to 6, as said below
- k_gain: float32 [128], replicated, may hold values from 1.2 to 6, as said below
Outputs:
- section_out: bfloat16 [64, 32, 8, 512], P('tm', 'band')
- attended: bfloat16 [16384, 12, 128], P('tm', 'band')
The draws below stay inside these ranges and needn't reach their ends.
Inputs may be any that keep to these rules, and one draw needn't show every extreme that they name: `lengths`: whole frames of each clip; they sum to 64 and the longest clip has exactly 48 frames. `q_gain`: positive gains. `k_gain`: positive gains.
All inputs are finite; a program needn't handle non-finite values.
Results may differ from the reference program's by a relative error of at most 0.023.
The reference program's roundings to bfloat16 on the way count: a program that leaves them out, or rounds other values in their place, can miss the bound.
Values may be sent and summed in bfloat16 or wider, within the bound.
No kernel may reach another device: no remote copies, remote signals or barrier semaphores. Data moves between devices by JAX's collectives and lax.ppermute only.
A program may use at most 192 MiB of HBM per device.

```python
import jax
import jax.numpy as jnp
from jax import lax

CH = 512
D = 3072
HEADS = 12
HDIM = 128
WIDE = 8
FRAMES = 64
MAXF = 48
HEIGHT = 32
FRAME_TOK = 256
TOKENS = 16384


def draw_lengths(key, part):
    key = jax.random.fold_in(key, 13)
    cut_key, place_key = jax.random.split(key)
    remain = FRAMES - MAXF
    cuts = jax.random.permutation(cut_key, remain - 1)[:2].astype(jnp.int32) + 1
    lower_cut = jnp.minimum(cuts[0], cuts[1])
    upper_cut = jnp.maximum(cuts[0], cuts[1])
    others = jnp.stack([lower_cut, upper_cut - lower_cut, remain - upper_cut]).astype(jnp.int32)
    place = jax.random.randint(place_key, (), 0, 4).astype(jnp.int32)
    slots = jnp.arange(4, dtype=jnp.int32)
    before = others[jnp.clip(slots, 0, 2)]
    after = others[jnp.clip(slots - 1, 0, 2)]
    longest = jnp.full((4,), MAXF, jnp.int32)
    return jnp.where(slots < place, before, jnp.where(slots == place, longest, after)).astype(jnp.int32)


def draw_q_gain(key, part):
    key = jax.random.fold_in(key, 11)
    return jax.random.uniform(key, (HDIM,), jnp.float32, 1.2, 3.0)


def draw_k_gain(key, part):
    key = jax.random.fold_in(key, 12)
    return jax.random.uniform(key, (HDIM,), jnp.float32, 1.2, 3.0)


def steps_of(key, dims, pieces, smallest, top_value):
    def one(dim, parts):
        draws = jax.random.uniform(jax.random.fold_in(jax.random.fold_in(key, 6), dim), (parts,), jnp.float32, smallest / len(pieces), top_value / len(pieces))
        return jnp.repeat(jnp.exp(draws), dims[dim] // parts).reshape((-1,) + (1,) * (len(dims) - dim - 1))

    loudness = one(*pieces[0])
    for cut in pieces[1:]:
        loudness = loudness * one(*cut)
    return loudness


def bell_draw(key, shape, width, most, shards=(), held_as=jnp.bfloat16):
    array = jax.random.normal(key, shape, jnp.float32) * width
    if len(shards) > 0:
        array = steps_of(key, shape, shards, -0.22, 0.18) * array
    return jnp.clip(array, min=-most, max=most).astype(held_as)


def setup_inputs(seed: int = 0) -> dict:
    arg_keys = jax.random.split(jax.random.key(seed), 13)
    section_in = bell_draw(arg_keys[0], (FRAMES, HEIGHT, WIDE, CH), 1.0, 6.0, ((0, 32), (1, 4)))
    norm_gain = jnp.clip(1.0 + 0.18 * jax.random.normal(arg_keys[1], (CH,), jnp.float32), 0.1, 1.9)
    conv_weight = bell_draw(arg_keys[2], (3, 3, 3, CH, CH), (27 * CH) ** -0.5, 0.0546875)
    conv_bias = bell_draw(arg_keys[3], (CH,), 0.3, 2.0, (), jnp.float32)
    lengths = draw_lengths(jax.random.fold_in(arg_keys[12], 71), 0)
    embed_weight = bell_draw(arg_keys[5], (CH, D), CH ** -0.5, 0.25)
    embed_bias = bell_draw(arg_keys[6], (D,), 0.5, 3.0, (), jnp.float32)
    mod_shift = bell_draw(arg_keys[7], (D,), 0.5, 3.0, (), jnp.float32)
    mod_scale = bell_draw(arg_keys[8], (D,), 0.3, 1.5, (), jnp.float32)
    qkv_weight = bell_draw(arg_keys[9], (D, 3, HEADS, HDIM), D ** -0.5, 0.109375, ((2, 4),))
    q_gain = draw_q_gain(jax.random.fold_in(arg_keys[12], 71), 0)
    k_gain = draw_k_gain(jax.random.fold_in(arg_keys[12], 71), 0)
    return dict(section_in=section_in, norm_gain=norm_gain, conv_weight=conv_weight, conv_bias=conv_bias, lengths=lengths, embed_weight=embed_weight, embed_bias=embed_bias, mod_shift=mod_shift, mod_scale=mod_scale, qkv_weight=qkv_weight, q_gain=q_gain, k_gain=k_gain)


EPSILON = 1e-06

def clip_layout(frame_index, lengths):
    clip_ends = jnp.cumsum(lengths).astype(jnp.int32)
    starts = (clip_ends - lengths).astype(jnp.int32)
    member = (frame_index[:, None] >= clip_ends[None, :]).astype(jnp.int32)
    clip_id = lax.optimization_barrier(jnp.sum(member, axis=1)).astype(jnp.int32)
    labels = jnp.arange(lengths.shape[0], dtype=jnp.int32)
    clip_first = lax.optimization_barrier(jnp.sum(jnp.where(clip_id[:, None] == labels[None, :], starts[None, :], 0), axis=1)).astype(jnp.int32)
    return (clip_id, clip_first)

def rms_scale(values, gain):
    mean_square = lax.optimization_barrier(jnp.mean(values * values, axis=-1, keepdims=True))
    return values * lax.rsqrt(mean_square + EPSILON) * gain

def modulate(token_block, embed_weight, embed_bias, mod_shift, mod_scale):
    embedded = jnp.dot(token_block, embed_weight, preferred_element_type=jnp.float32) + embed_bias
    center = embedded - lax.optimization_barrier(jnp.mean(embedded, axis=-1, keepdims=True))
    spread = lax.optimization_barrier(jnp.mean(center * center, axis=-1, keepdims=True))
    normal = center * lax.rsqrt(spread + EPSILON)
    return (normal * (1.0 + mod_scale) + mod_shift).astype(jnp.bfloat16)

def reference(section_in, norm_gain, conv_weight, conv_bias, lengths, embed_weight, embed_bias, mod_shift, mod_scale, qkv_weight, q_gain, k_gain):
    frame_index = jnp.arange(FRAMES, dtype=jnp.int32)
    clip_id, clip_first = clip_layout(frame_index, lengths)
    inputs = section_in.astype(jnp.float32)
    active = jax.nn.silu(rms_scale(inputs, norm_gain)).astype(jnp.bfloat16)
    padded = jnp.pad(active, ((0, 0), (1, 1), (1, 1), (0, 0)))
    conv_sum = jnp.zeros((FRAMES * HEIGHT * WIDE, CH), jnp.float32)
    for tap_time in range(3):
        source = jnp.maximum(frame_index - 2 + tap_time, clip_first).astype(jnp.int32)
        tapped = padded[source]
        for tap_row in range(3):
            for tap_col in range(3):
                tap_piece = tapped[:, tap_row:tap_row + HEIGHT, tap_col:tap_col + WIDE].reshape(-1, CH)
                conv_sum = conv_sum + jnp.dot(tap_piece, conv_weight[tap_time, tap_row, tap_col], preferred_element_type=jnp.float32)
    section_out = (inputs + conv_bias + conv_sum.reshape(FRAMES, HEIGHT, WIDE, CH)).astype(jnp.bfloat16)
    frame_tokens = section_out.reshape(FRAMES, FRAME_TOK, CH)
    flat_weight = qkv_weight.reshape(D, 3 * HEADS * HDIM)

    def project(token_block):
        modulated = modulate(token_block, embed_weight, embed_bias, mod_shift, mod_scale)
        projected = jnp.dot(modulated, flat_weight, preferred_element_type=jnp.float32).reshape(FRAME_TOK, 3, HEADS, HDIM)
        queries = rms_scale(projected[:, 0], q_gain).astype(jnp.bfloat16)
        key_rows = rms_scale(projected[:, 1], k_gain).astype(jnp.bfloat16)
        values = projected[:, 2].astype(jnp.bfloat16)
        return (queries, key_rows, values)
    queries, key_rows, values = lax.map(project, frame_tokens)
    all_keys = key_rows.reshape(TOKENS, HEADS, HDIM).astype(jnp.float32)
    all_values = values.reshape(TOKENS, HEADS, HDIM).astype(jnp.float32)
    key_clip = jnp.repeat(clip_id, FRAME_TOK)
    score_scale = 1.0 / HDIM ** 0.5

    def attend(frame_at):
        same_clip = (key_clip == clip_id[frame_at])[None, None, :]
        scores = jnp.einsum('qhd,khd->hqk', queries[frame_at].astype(jnp.float32), all_keys) * score_scale
        masked = jnp.where(same_clip, scores, -1e+30)
        row_peak = lax.optimization_barrier(jnp.max(masked, axis=-1, keepdims=True))
        weights = jnp.where(same_clip, jnp.exp(masked - row_peak), 0.0)
        weight_sum = lax.optimization_barrier(jnp.sum(weights, axis=-1))
        rounded = lax.optimization_barrier(weights.astype(jnp.bfloat16))
        mixed_rows = jnp.einsum('hqk,khd->qhd', rounded.astype(jnp.float32), all_values)
        return (mixed_rows / jnp.transpose(weight_sum)[:, :, None]).astype(jnp.bfloat16)
    attended = lax.map(attend, jnp.arange(FRAMES, dtype=jnp.int32)).reshape(TOKENS, HEADS, HDIM)
    return (section_out, attended)
```

```python
import functools

import jax
import jax.numpy as jnp
from jax import lax
from jax.experimental import pallas as pl
from jax.experimental.pallas import tpu as pltpu
from jax.sharding import PartitionSpec as P

EPSILON = 1e-06
LOG2E = 1.4426950408889634
NONE = -1e30
NX, NZ, NC, NB = 4, 4, 2, 4
HD = 128
HEADS = 3
SHARD = 128
FRAME = 256
OWN = 512
KEYS = 4096
F32 = jnp.float32
BF16 = jnp.bfloat16
VMEM_LIMIT = 56 * 1024 * 1024


def params():
    return pltpu.CompilerParams(vmem_limit_bytes=VMEM_LIMIT)


def split_bf16(value, count):
    parts = []
    for _ in range(count):
        part = value.astype(BF16).astype(F32)
        parts.append(part)
        value = value - part
    return parts


def tm_index(x, z, c):
    return (x * NZ + z) * NC + c


def shift_tm(block, dx=0, dz=0, swap=False):
    route = []
    for x in range(NX):
        for z in range(NZ):
            for c in range(NC):
                target = tm_index((x + dx) % NX, (z + dz) % NZ, 1 - c if swap else c)
                route.append((tm_index(x, z, c), target))
    return lax.ppermute(block, "tm", route)


def shift_band(block, db):
    return lax.ppermute(block, "band", [(i, (i + db) % NB) for i in range(NB)])


def halo(block, dt, db):
    count = lax.axis_size("tm")
    route = []
    for t in range(count):
        for b in range(NB):
            if t + dt < count and 0 <= b + db < NB:
                route.append((t * NB + b, (t + dt) * NB + b + db))
    return lax.ppermute(block, ("tm", "band"), route)


def fold_kernel(embed_ref, bias_ref, shift_ref, scale_ref, qkv_ref, out_ref, rows_ref, left, total):
    step = pl.program_id(0)
    width = left.shape[1]
    chunk = qkv_ref.shape[1]

    @pl.when(step == 0)
    def _():
        gain = 1.0 + scale_ref[...]
        for lo in range(0, 512, 64):
            weight = embed_ref[lo : lo + 64, :].astype(F32)
            centred = weight - jnp.mean(weight, axis=-1, keepdims=True)
            left[lo : lo + 64, :] = (centred * gain).astype(BF16)
        bias = bias_ref[...]
        bias = (bias - jnp.mean(bias, axis=-1, keepdims=True)) * gain
        extra = jnp.zeros((16, width), F32)
        place = lax.broadcasted_iota(jnp.int32, (16, width), 0)
        for at, part in enumerate(split_bf16(bias, 3) + split_bf16(shift_ref[...], 3)):
            extra = jnp.where(place == at, part, extra)
        left[512:528, :] = extra.astype(BF16)

    columns = pl.ds(pl.multiple_of(step * chunk, chunk), chunk)
    right = jnp.concatenate([qkv_ref[i] for i in range(9)], axis=1)
    part = jnp.dot(left[:, columns], right, preferred_element_type=F32)

    @pl.when(step == 0)
    def _():
        total[...] = part

    @pl.when(step > 0)
    def _():
        total[...] += part

    @pl.when(step == pl.num_programs(0) - 1)
    def _():
        out_ref[...] = total[0:512, :].astype(BF16)
        rows = total[512:528, :]
        place = lax.broadcasted_iota(jnp.int32, (8, 1152), 0)
        bias = rows[0:1] + rows[1:2] + rows[2:3]
        moved = rows[3:4] + rows[4:5] + rows[5:6]
        rows_ref[...] = jnp.where(place == 0, bias, jnp.where(place == 1, moved, 0.0))


def fold(embed_weight, embed_bias, mod_shift, mod_scale, qkv):
    chunk = 512
    steps = qkv.shape[1] // chunk
    row = pl.BlockSpec((1, 3072), lambda k: (0, 0))
    return pl.pallas_call(
        fold_kernel,
        grid=(steps,),
        in_specs=[
            pl.BlockSpec((512, 3072), lambda k: (0, 0)),
            row,
            row,
            row,
            pl.BlockSpec((9, chunk, HD), lambda k: (0, k, 0)),
        ],
        out_specs=[
            pl.BlockSpec((512, 1152), lambda k: (0, 0)),
            pl.BlockSpec((8, 1152), lambda k: (0, 0)),
        ],
        out_shape=[
            jax.ShapeDtypeStruct((512, 1152), BF16),
            jax.ShapeDtypeStruct((8, 1152), F32),
        ],
        scratch_shapes=[pltpu.VMEM((528, 3072), BF16), pltpu.VMEM((528, 1152), F32)],
        compiler_params=params(),
        cost_estimate=pl.CostEstimate(
            flops=2 * 528 * 3072 * 1152, bytes_accessed=12000000, transcendentals=0
        ),
    )(embed_weight, embed_bias[None], mod_shift[None], mod_scale[None], qkv)


def conv_kernel(
    slots_ref,
    cur_ref,
    prev_ref,
    up_cur_ref,
    down_cur_ref,
    up_prev_ref,
    down_prev_ref,
    gain_ref,
    bias_ref,
    embed_ref,
    embed_bias_ref,
    weight_ref,
    out_ref,
    send_ref,
    act,
    total,
):
    step = pl.program_id(0)

    @pl.when(step == 0)
    def _():
        total[...] = jnp.zeros_like(total)
        place = lax.broadcasted_iota(jnp.int32, (80, 512), 0) % 8
        for slot in range(4):
            up, mid, down = (
                (up_prev_ref, prev_ref, down_prev_ref)
                if slot < 2
                else (up_cur_ref, cur_ref, down_cur_ref)
            )
            at = slot % 2
            cells = jnp.concatenate(
                [
                    up[at, 0].astype(F32),
                    mid[at].astype(F32).reshape(64, 512),
                    down[at, 0].astype(F32),
                ],
                axis=0,
            )
            mean_square = jnp.mean(cells * cells, axis=-1, keepdims=True)
            scaled = cells * lax.rsqrt(mean_square + EPSILON) * gain_ref[...]
            active = (scaled * jax.nn.sigmoid(scaled)).astype(BF16).astype(F32)
            act[0, slot] = jnp.where(place == 0, 0.0, pltpu.roll(active, 1, 0))
            act[1, slot] = active
            act[2, slot] = jnp.where(place == 7, 0.0, pltpu.roll(active, 79, 0))

    tap_time = step // 3
    rows = pl.ds(pl.multiple_of((step % 3) * 8, 8), 64)
    part = total[...]
    for tap_col in range(3):
        piece = jnp.concatenate(
            [act[tap_col, slots_ref[i * 3 + tap_time], rows, :] for i in range(2)], axis=0
        ).astype(BF16)
        part = part + jnp.dot(piece, weight_ref[0, 0, tap_col], preferred_element_type=F32)
    total[...] = part

    @pl.when(step == pl.num_programs(0) - 1)
    def _():
        inputs = cur_ref[...].astype(F32).reshape(SHARD, 512)
        section = (inputs + bias_ref[...] + total[...]).astype(BF16)
        out_ref[...] = section.reshape(out_ref.shape)
        send_ref[0:SHARD, :] = section
        embedded = (
            jnp.dot(section, embed_ref[...], preferred_element_type=F32) + embed_bias_ref[...]
        )
        center = embedded - jnp.mean(embedded, axis=-1, keepdims=True)
        spread = jnp.mean(center * center, axis=-1, keepdims=True)
        scale = lax.rsqrt(spread + EPSILON)
        across = jnp.transpose(jnp.broadcast_to(scale, (SHARD, SHARD)))[0:16]
        high, low = split_bf16(across, 2)
        tail = jnp.concatenate([high, low, jnp.zeros((16, 256), F32)], axis=1)
        place = lax.broadcasted_iota(jnp.int32, (16, 512), 0)
        send_ref[SHARD : SHARD + 16, :] = jnp.where(place == 0, tail, 0.0).astype(BF16)


def conv(slots, pieces, norm_gain, conv_bias, embed_weight, embed_bias, conv_weight):
    def whole(shape):
        return pl.BlockSpec(shape, lambda k, s: (0,) * len(shape))

    return pl.pallas_call(
        conv_kernel,
        grid_spec=pltpu.PrefetchScalarGridSpec(
            num_scalar_prefetch=1,
            grid=(9,),
            in_specs=[whole(piece.shape) for piece in pieces]
            + [
                whole((1, 512)),
                whole((1, 512)),
                whole((512, 3072)),
                whole((1, 3072)),
                pl.BlockSpec((1, 1, 3, 512, 512), lambda k, s: (k // 3, k % 3, 0, 0, 0)),
            ],
            out_specs=[whole((2, 8, 8, 512)), whole((SHARD + 16, 512))],
            scratch_shapes=[pltpu.VMEM((3, 4, 80, 512), F32), pltpu.VMEM((SHARD, 512), F32)],
        ),
        out_shape=[
            jax.ShapeDtypeStruct((2, 8, 8, 512), BF16),
            jax.ShapeDtypeStruct((SHARD + 16, 512), BF16),
        ],
        compiler_params=params(),
        cost_estimate=pl.CostEstimate(
            flops=2 * 128 * 13824 * 512, bytes_accessed=18000000, transcendentals=0
        ),
    )(slots, *pieces, norm_gain[None], conv_bias[None], embed_weight, embed_bias[None], conv_weight)


def normed(values, gain):
    mean_square = jnp.mean(values * values, axis=-1, keepdims=True)
    return (values * lax.rsqrt(mean_square + EPSILON) * gain).astype(BF16)


def query_kernel(band_ref, s0, s1, s3, s2, weight_ref, rows_ref, gain_ref, q_ref, xr_ref):
    band = band_ref[0]
    place = lax.broadcasted_iota(jnp.int32, (16, 512), 0)
    tail = jnp.zeros((16, 512), F32)
    for back, ref in ((0, s0), (1, s1), (3, s3), (2, s2)):
        source = lax.rem(band + (NB - back), NB)
        cells = ref[0:SHARD, :]
        extra = ref[SHARD : SHARD + 16, :].astype(F32)
        tail = jnp.where(place == source, extra[0:1, :], tail)
        across = extra[0:1, 0:HD] + extra[0:1, HD : 2 * HD]
        scale = jnp.transpose(jnp.broadcast_to(across, (HD, HD)))
        projected = jnp.dot(cells, weight_ref[...], preferred_element_type=F32) + rows_ref[0:1, :]
        for head in range(HEADS):
            lanes = slice(head * HD, (head + 1) * HD)
            values = normed(projected[:, lanes] * scale + rows_ref[1:2, lanes], gain_ref[...])
            for i in range(2):
                rows = pl.ds(pl.multiple_of(i * FRAME + source * 64, 64), 64)
                q_ref[head, rows, :] = values[i * 64 : (i + 1) * 64]
        for i in range(2):
            rows = pl.ds(pl.multiple_of(i * FRAME + source * 64, 64), 64)
            xr_ref[rows, :] = cells[i * 64 : (i + 1) * 64]
    xr_ref[OWN : OWN + 16, :] = tail.astype(BF16)


def queries_of(band, shards, weight, rows, gain):
    smem = pl.BlockSpec(memory_space=pltpu.SMEM)
    vmem = pl.BlockSpec(memory_space=pltpu.VMEM)
    return pl.pallas_call(
        query_kernel,
        in_specs=[smem] + [vmem] * 7,
        out_specs=[vmem, vmem],
        out_shape=[
            jax.ShapeDtypeStruct((HEADS, OWN, HD), BF16),
            jax.ShapeDtypeStruct((OWN + 16, 512), BF16),
        ],
        compiler_params=params(),
        cost_estimate=pl.CostEstimate(
            flops=2 * 512 * 512 * 384, bytes_accessed=2000000, transcendentals=0
        ),
    )(band, *shards, weight, rows, gain[None])


def attend_kernel(
    info_ref, q0, q1, q3, q2, a0, a1, a3, a2, b0, b1, b3, b2, weight_ref, rows_ref, gain_ref,
    o0, o1, o3, o2, key_t, value_x, total, peak,
):
    x_here, core = info_ref[16], info_ref[17]
    value_x[:, :, HD : 2 * HD] = jnp.ones((HEADS, KEYS, HD), BF16)
    for swap, refs in ((0, (a0, a1, a3, a2)), (1, (b0, b1, b3, b2))):
        for back, ref in zip((0, 1, 3, 2), refs):
            source = lax.rem(x_here + (NX - back), NX)
            core_at = core if swap == 0 else 1 - core
            extra = ref[OWN : OWN + 16, :].astype(F32)
            across = extra[:, 0:HD] + extra[:, HD : 2 * HD]
            down = jnp.transpose(
                jnp.concatenate([across, jnp.zeros((HD - 16, HD), F32)], axis=0)
            )
            for i in range(2):
                scale = jnp.concatenate(
                    [down[i * 64 : (i + 1) * 64, b : b + 1] for b in range(NB)], axis=0
                )
                projected = (
                    jnp.dot(
                        ref[i * FRAME : (i + 1) * FRAME, :],
                        weight_ref[...],
                        preferred_element_type=F32,
                    )
                    + rows_ref[0:1, :]
                ) * scale + rows_ref[1:2, :]
                start = pl.multiple_of((source * 4 + core_at * 2 + i) * FRAME, FRAME)
                for head in range(HEADS):
                    keys = normed(projected[:, head * HD : (head + 1) * HD], gain_ref[...])
                    key_t[head, :, pl.ds(start, FRAME)] = jnp.transpose(keys)
                    value_x[head, pl.ds(start, FRAME), 0:HD] = projected[
                        :, (HEADS + head) * HD : (HEADS + head + 1) * HD
                    ].astype(BF16)

    factor = LOG2E / HD**0.5

    for group, (q_ref, o_ref) in enumerate(((q0, o0), (q1, o1), (q3, o3), (q2, o2))):

        def one_frame(i, carry, group=group, q_ref=q_ref, o_ref=o_ref):
            first = info_ref[group * 4 + i * 2]
            count = info_ref[group * 4 + i * 2 + 1]
            base = pl.multiple_of(i * FRAME, FRAME)
            total[...] = jnp.zeros_like(total)
            peak[...] = jnp.full_like(peak, NONE)

            def block(start, size):
                for head in range(HEADS):
                    scores = (
                        jnp.dot(
                            q_ref[head, pl.ds(base, FRAME), :],
                            key_t[head, :, pl.ds(start, size)],
                            preferred_element_type=F32,
                        )
                        * factor
                    )
                    old = peak[head][:, 0:1]
                    new = jnp.maximum(old, jnp.max(scores, axis=-1, keepdims=True))
                    weights = jnp.exp2(scores - new).astype(BF16)
                    mixed = jnp.dot(
                        weights,
                        value_x[head, pl.ds(start, size), :],
                        preferred_element_type=F32,
                    )
                    total[head] = total[head] * jnp.exp2(old - new) + mixed
                    peak[head] = jnp.broadcast_to(new, (FRAME, HD))

            def wide(j, c):
                block(pl.multiple_of((first + j * 4) * FRAME, FRAME), 4 * FRAME)
                return c

            def narrow(j, c):
                block(pl.multiple_of((first + j) * FRAME, FRAME), FRAME)
                return c

            wides = count // 4
            lax.fori_loop(0, wides, wide, 0)
            lax.fori_loop(wides * 4, count, narrow, 0)
            lane = lax.broadcasted_iota(jnp.int32, (FRAME, HD), 1)
            marks = jnp.zeros((FRAME, HD), F32)
            for head in range(HEADS):
                weight_sum = total[head, :, HD : 2 * HD]
                some = weight_sum > 0.0
                safe = jnp.where(some, weight_sum, 1.0)
                o_ref[pl.ds(pl.multiple_of(head * OWN + base, FRAME), FRAME), :] = (
                    total[head, :, 0:HD] / safe
                ).astype(BF16)
                level = jnp.where(some, peak[head] + jnp.log2(safe), NONE)
                for at, part in enumerate(split_bf16(level, 3)):
                    marks = jnp.where(lane == head * 3 + at, part, marks)
            for half in range(2):
                rows = pl.ds(
                    pl.multiple_of(HEADS * OWN + (i * 2 + half) * 16, 16), 16
                )
                o_ref[rows, :] = jnp.transpose(marks[half * HD : (half + 1) * HD])[0:16].astype(
                    BF16
                )
            return carry

        lax.fori_loop(0, 2, one_frame, 0)


def attend(info, queries, near, far, weight, rows, gain):
    smem = pl.BlockSpec(memory_space=pltpu.SMEM)
    vmem = pl.BlockSpec(memory_space=pltpu.VMEM)
    out = jax.ShapeDtypeStruct((HEADS * OWN + 64, HD), BF16)
    return pl.pallas_call(
        attend_kernel,
        in_specs=[smem] + [vmem] * 15,
        out_specs=[vmem] * 4,
        out_shape=[out] * 4,
        scratch_shapes=[
            pltpu.VMEM((HEADS, HD, KEYS), BF16),
            pltpu.VMEM((HEADS, KEYS, 2 * HD), BF16),
            pltpu.VMEM((HEADS, FRAME, 2 * HD), F32),
            pltpu.VMEM((HEADS, FRAME, HD), F32),
        ],
        compiler_params=params(),
        cost_estimate=pl.CostEstimate(
            flops=40000000000, bytes_accessed=10000000, transcendentals=0
        ),
    )(info, *queries, *near, *far, weight, rows, gain[None])


def merge_kernel(p0, p1, p2, p3, out_ref):
    for at in range(4):
        base = HEADS * OWN + at * 16
        columns = []
        for ref in (p0, p1, p2, p3):
            marks = ref[base : base + 16, :].astype(F32)
            columns.append(
                jnp.transpose(jnp.concatenate([marks, jnp.zeros((HD - 16, HD), F32)], axis=0))
            )
        for head in range(HEADS):
            rows = slice(head * OWN + at * HD, head * OWN + (at + 1) * HD)
            levels = [
                mark[:, head * 3 : head * 3 + 1]
                + mark[:, head * 3 + 1 : head * 3 + 2]
                + mark[:, head * 3 + 2 : head * 3 + 3]
                for mark in columns
            ]
            top = functools.reduce(jnp.maximum, levels)
            shares = [jnp.exp2(level - top) for level in levels]
            weight_sum = functools.reduce(jnp.add, shares)
            mixed = functools.reduce(
                jnp.add,
                [
                    ref[rows, :].astype(F32) * share
                    for ref, share in zip((p0, p1, p2, p3), shares)
                ],
            )
            out_ref[head, at * HD : (at + 1) * HD, :] = (mixed / weight_sum).astype(BF16)


def merge(parts):
    vmem = pl.BlockSpec(memory_space=pltpu.VMEM)
    return pl.pallas_call(
        merge_kernel,
        in_specs=[vmem] * 4,
        out_specs=vmem,
        out_shape=jax.ShapeDtypeStruct((HEADS, OWN, HD), BF16),
        compiler_params=params(),
    )(*parts)


def frame_bounds(frames, lengths):
    ends = jnp.cumsum(lengths)
    starts = ends - lengths
    inside = (frames[:, None] >= starts[None, :]) & (frames[:, None] < ends[None, :])
    first = jnp.sum(jnp.where(inside, starts[None, :], 0), axis=1)
    last = jnp.sum(jnp.where(inside, ends[None, :], 0), axis=1)
    return first, last


def per_device(
    section_in,
    norm_gain,
    conv_weight,
    conv_bias,
    lengths,
    embed_weight,
    embed_bias,
    mod_shift,
    mod_scale,
    qkv_weight,
    q_gain,
    k_gain,
):
    place = lax.axis_index("tm")
    band = lax.axis_index("band")
    x_here, z_here, core = place // (NZ * NC), place // NC % NZ, place % NC
    top, bottom = section_in[:, 0:1], section_in[:, 7:8]
    pieces = (
        section_in,
        halo(section_in, 1, 0),
        halo(bottom, 0, 1),
        halo(top, 0, -1),
        halo(bottom, 1, 1),
        halo(top, 1, -1),
    )
    qkv = jnp.transpose(qkv_weight, (1, 2, 0, 3)).reshape(9, 3072, HD)
    folded, rows = fold(embed_weight, embed_bias, mod_shift, mod_scale, qkv)

    own = place * 2 + jnp.arange(2, dtype=jnp.int32)
    own_first, _ = frame_bounds(own, lengths)
    taps = jnp.arange(3, dtype=jnp.int32)
    slots = jnp.maximum(own[:, None] - 2 + taps[None, :], own_first[:, None]) - (place * 2 - 2)
    section_out, send = conv(
        slots.reshape(-1).astype(jnp.int32),
        pieces,
        norm_gain,
        conv_bias,
        embed_weight,
        embed_bias,
        conv_weight,
    )
    shards = (send, shift_band(send, 1), shift_band(send, 3), shift_band(send, 2))
    query, xr = queries_of(
        band[None].astype(jnp.int32), shards, folded[:, 0:384], rows[:, 0:384], q_gain
    )
    queries = (query, shift_tm(query, dz=1), shift_tm(query, dz=3), shift_tm(query, dz=2))
    near = (xr, shift_tm(xr, dx=1), shift_tm(xr, dx=3), shift_tm(xr, dx=2))
    far = tuple(shift_tm(part, swap=True) for part in near)

    back = jnp.array([0, 1, 3, 2], jnp.int32)
    group_z = (z_here - back) % NZ
    query_frames = (
        x_here * 16 + group_z[:, None] * 4 + core * 2 + jnp.arange(2, dtype=jnp.int32)[None, :]
    ).reshape(-1)
    first, last = frame_bounds(query_frames, lengths)
    slot = jnp.arange(16, dtype=jnp.int32)
    key_frames = slot // 4 * 16 + z_here * 4 + slot % 4
    begin = jnp.sum((key_frames[None, :] < first[:, None]).astype(jnp.int32), axis=1)
    end = jnp.sum((key_frames[None, :] < last[:, None]).astype(jnp.int32), axis=1)
    info = jnp.concatenate(
        [
            jnp.stack([begin, end - begin], axis=1).reshape(-1),
            jnp.stack([x_here, core]),
        ]
    ).astype(jnp.int32)
    o0, o1, o3, o2 = attend(
        info, queries, near, far, folded[:, 384:1152], rows[:, 384:1152], k_gain
    )
    parts = (o0, shift_tm(o1, dz=3), shift_tm(o3, dz=1), shift_tm(o2, dz=2))
    attended = jnp.transpose(merge(parts), (1, 0, 2))
    return (section_out, attended)


def solution(mesh):
    return jax.shard_map(
        per_device,
        mesh=mesh,
        in_specs=(
            P("tm", "band", None, None),
            P(),
            P(),
            P(),
            P(),
            P(),
            P(),
            P(),
            P(),
            P(None, None, "band", None),
            P(),
            P(),
        ),
        out_specs=(P("tm", "band", None, None), P("tm", "band", None)),
        check_vma=False,
    )
```

```python
import functools

import jax
import jax.numpy as jnp
from jax import lax
from jax.experimental import pallas as pl
from jax.experimental.pallas import tpu as pltpu
from jax.sharding import PartitionSpec as P

EPSILON = 1e-06
NONE = -1e30
NX, NZ, NC, NB = 4, 4, 2, 4
HD = 128
FACTOR = 1.4426950408889634 / HD**0.5
HEADS = 3
SHARD = 128
FRAME = 256
OWN = 512
KEYS = 4096
F32 = jnp.float32
BF16 = jnp.bfloat16
MIB = 1024 * 1024


def params(mib):
    return pltpu.CompilerParams(vmem_limit_bytes=mib * MIB)


def fetch(sources, targets, sems, base=0):
    copies = [
        pltpu.make_async_copy(source, target, sems.at[base + at])
        for at, (source, target) in enumerate(zip(sources, targets))
    ]
    for copy in copies:
        copy.start()
    return copies


SMEM = pl.BlockSpec(memory_space=pltpu.SMEM)
VMEM = pl.BlockSpec(memory_space=pltpu.VMEM)
HBM = pl.BlockSpec(memory_space=pltpu.HBM)
ANY = pl.BlockSpec(memory_space=pl.ANY)


def pinned(*arrays):
    return [pltpu.with_memory_space_constraint(array, pltpu.HBM) for array in arrays]


def in_vmem(*arrays):
    return [pltpu.with_memory_space_constraint(array, pltpu.VMEM) for array in arrays]


def clip_of_frame(info_ref, frame):
    first, last, end = 0, 0, 0
    for clip in range(4):
        start, end = end, end + info_ref[clip]
        inside = (frame >= start) & (frame < end)
        first = jnp.where(inside, start, first)
        last = jnp.where(inside, end, last)
    return first, last


def place_of(info_ref):
    place = info_ref[4]
    return place // (NZ * NC), place // NC % NZ, place % NC


def split_bf16(value, count):
    parts = []
    for _ in range(count):
        part = value.astype(BF16).astype(F32)
        parts.append(part)
        value = value - part
    return parts


def together(*arrays):
    count = len(arrays)

    def kernel(*refs):
        pass

    return pl.pallas_call(
        kernel,
        in_specs=[ANY] * count,
        out_specs=[ANY] * count,
        out_shape=[jax.ShapeDtypeStruct(array.shape, array.dtype) for array in arrays],
        input_output_aliases={i: i for i in range(count)},
    )(*arrays)


def tm_index(x, z, c):
    return (x * NZ + z) * NC + c


def shift_tm(block, dx=0, dz=0, swap=False):
    route = []
    for x in range(NX):
        for z in range(NZ):
            for c in range(NC):
                target = tm_index((x + dx) % NX, (z + dz) % NZ, 1 - c if swap else c)
                route.append((tm_index(x, z, c), target))
    return lax.ppermute(block, "tm", route)


def shift_band(block, db):
    return lax.ppermute(block, "band", [(i, (i + db) % NB) for i in range(NB)])


def halo(block, dt, db):
    count = lax.axis_size("tm")
    route = []
    for t in range(count):
        for b in range(NB):
            if t + dt < count and 0 <= b + db < NB:
                route.append((t * NB + b, (t + dt) * NB + b + db))
    return lax.ppermute(block, ("tm", "band"), route)


def fold_kernel(
    embed_ref, bias_ref, shift_ref, scale_ref, gain_ref, qkv_ref, wq_ref, wk_ref, wv_ref, rows_ref, cols_ref,
    left,
):
    width = left.shape[1]
    gain = 1.0 + scale_ref[...]
    for lo in range(0, 512, 64):
        weight = embed_ref[lo : lo + 64, :].astype(F32)
        centred = weight - jnp.mean(weight, axis=-1, keepdims=True)
        left[lo : lo + 64, :] = (centred * gain).astype(BF16)
    bias = bias_ref[...]
    bias = (bias - jnp.mean(bias, axis=-1, keepdims=True)) * gain
    extra = jnp.zeros((16, width), F32)
    place = lax.broadcasted_iota(jnp.int32, (16, width), 0)
    for at, part in enumerate(split_bf16(bias, 3) + split_bf16(shift_ref[...], 3)):
        extra = jnp.where(place == at, part, extra)
    left[512:528, :] = extra.astype(BF16)
    where = lax.broadcasted_iota(jnp.int32, (8, HD), 0)
    cols_ref[2, 0:HD, :] = jnp.transpose(jnp.broadcast_to(gain_ref[...], (HD, HD)))
    for pair in ((0, 1), (2, 3), (4, 5), (6, 7), (8,)):
        right = jnp.concatenate([qkv_ref[i] for i in pair], axis=1)
        both = jnp.dot(left[...], right, preferred_element_type=F32)
        for at, block in enumerate(pair):
            part = both[:, at * HD : (at + 1) * HD]
            head = slice(block % HEADS * HD, (block % HEADS + 1) * HD)
            offset = part[512:513] + part[513:514] + part[514:515]
            moved = part[515:516] + part[516:517] + part[517:518]
            rows_ref[:, block * HD : (block + 1) * HD] = jnp.where(
                where == 0, offset, jnp.where(where == 1, moved, 0.0)
            )
            if block // HEADS == 0:
                wq_ref[:, head] = part[0:512].astype(BF16)
            elif block // HEADS == 1:
                wk_ref[head, :] = jnp.transpose(part[0:512]).astype(BF16)
                cols_ref[0, head, :] = jnp.transpose(jnp.broadcast_to(offset, (HD, HD)))
                cols_ref[1, head, :] = jnp.transpose(jnp.broadcast_to(moved, (HD, HD)))
            else:
                wv_ref[:, head] = part[0:512].astype(BF16)


def fold(embed_weight, embed_bias, mod_shift, mod_scale, k_gain, qkv):
    return pl.pallas_call(
        fold_kernel,
        in_specs=[VMEM] * 6,
        out_specs=[VMEM] * 5,
        out_shape=[
            jax.ShapeDtypeStruct((512, 384), BF16),
            jax.ShapeDtypeStruct((384, 512), BF16),
            jax.ShapeDtypeStruct((512, 384), BF16),
            jax.ShapeDtypeStruct((8, 1152), F32),
            jax.ShapeDtypeStruct((3, 384, HD), F32),
        ],
        scratch_shapes=[pltpu.VMEM((528, 3072), BF16)],
        compiler_params=params(16),
        cost_estimate=pl.CostEstimate(
            flops=2 * 528 * 3072 * 1152, bytes_accessed=12000000, transcendentals=0
        ),
    )(
        *in_vmem(embed_weight),
        embed_bias[None],
        mod_shift[None],
        mod_scale[None],
        k_gain[None],
        *in_vmem(qkv),
    )


def conv_kernel(
    info_ref,
    cur_ref,
    prev_ref,
    gain_ref,
    bias_ref,
    embed_bias_ref,
    weight_hbm,
    embed_hbm,
    qkv_hbm,
    out_ref,
    send_ref,
    embed_out,
    qkv_out,
    act,
    embed_ref,
    weight_ref,
    sems,
):
    taps = [(t, r) for t in range(3) for r in range(3)]
    weight_copies = fetch(
        [weight_hbm.at[tap] for tap in taps], [weight_ref.at[tap] for tap in taps], sems, 3
    )
    copies = fetch((embed_hbm, embed_hbm, qkv_hbm), (embed_ref, embed_out, qkv_out), sems)
    first_frame = info_ref[4] * 2
    slots = []
    for i in range(2):
        clip_first, _ = clip_of_frame(info_ref, first_frame + i)
        slots.append(
            [jnp.maximum(first_frame + i - 2 + t, clip_first) - first_frame + 2 for t in range(3)]
        )
    place = lax.broadcasted_iota(jnp.int32, (80, 512), 0) % 8
    for slot in range(4):
        cells = (prev_ref if slot < 2 else cur_ref)[slot % 2].astype(F32).reshape(80, 512)
        mean_square = jnp.mean(cells * cells, axis=-1, keepdims=True)
        scaled = cells * lax.rsqrt(mean_square + EPSILON) * gain_ref[...]
        active = (scaled * jax.nn.sigmoid(scaled)).astype(BF16).astype(F32)
        act[0, slot] = jnp.where(place == 0, 0.0, pltpu.roll(active, 1, 0))
        act[1, slot] = active
        act[2, slot] = jnp.where(place == 7, 0.0, pltpu.roll(active, 79, 0))
    inputs = jnp.concatenate(
        [cur_ref[i, 1:9].astype(F32).reshape(64, 512) for i in range(2)], axis=0
    )
    total = inputs + bias_ref[...]
    for tap_time in range(3):
        for tap_row in range(3):
            weight_copies[tap_time * 3 + tap_row].wait()
            for tap_col in range(3):
                piece = jnp.concatenate(
                    [
                        act[tap_col, slots[i][tap_time], tap_row * 8 : tap_row * 8 + 64, :]
                        for i in range(2)
                    ],
                    axis=0,
                ).astype(BF16)
                total = total + jnp.dot(
                    piece, weight_ref[tap_time, tap_row, tap_col], preferred_element_type=F32
                )
    section = total.astype(BF16)
    out_ref[...] = section.reshape(out_ref.shape)
    send_ref[0:SHARD, :] = section
    copies[0].wait()
    embedded = jnp.dot(section, embed_ref[...], preferred_element_type=F32) + embed_bias_ref[...]
    center = embedded - jnp.mean(embedded, axis=-1, keepdims=True)
    spread = jnp.mean(center * center, axis=-1, keepdims=True)
    scale = lax.rsqrt(spread + EPSILON)
    across = jnp.transpose(jnp.broadcast_to(scale, (SHARD, SHARD)))[0:16]
    high, low = split_bf16(across, 2)
    tail = jnp.concatenate([high, low, jnp.zeros((16, 256), F32)], axis=1)
    place = lax.broadcasted_iota(jnp.int32, (16, 512), 0)
    send_ref[SHARD : SHARD + 16, :] = jnp.where(place == 0, tail, 0.0).astype(BF16)
    for copy in copies[1:]:
        copy.wait()


def conv(info, cur, prev, norm_gain, conv_bias, embed_weight, embed_bias, conv_weight, qkv):
    return pl.pallas_call(
        conv_kernel,
        in_specs=[SMEM] + [VMEM] * 5 + [HBM] * 3,
        out_specs=[VMEM] * 2 + [ANY] * 2,
        out_shape=[
            jax.ShapeDtypeStruct((2, 8, 8, 512), BF16),
            jax.ShapeDtypeStruct((SHARD + 16, 512), BF16),
            jax.ShapeDtypeStruct(embed_weight.shape, BF16),
            jax.ShapeDtypeStruct(qkv.shape, BF16),
        ],
        scratch_shapes=[
            pltpu.VMEM((3, 4, 80, 512), F32),
            pltpu.VMEM((512, 3072), BF16),
            pltpu.VMEM(conv_weight.shape, BF16),
            pltpu.SemaphoreType.DMA((12,)),
        ],
        compiler_params=params(34),
        cost_estimate=pl.CostEstimate(
            flops=2 * 128 * 13824 * 512, bytes_accessed=18000000, transcendentals=0
        ),
    )(
        info,
        *in_vmem(cur, prev),
        norm_gain[None],
        conv_bias[None],
        embed_bias[None],
        *pinned(conv_weight, embed_weight, qkv),
    )


def normed(values, gain):
    mean_square = jnp.mean(values * values, axis=-1, keepdims=True)
    return (values * lax.rsqrt(mean_square + EPSILON) * gain).astype(BF16)


def query_kernel(
    band_ref, s0, s1, s3, s2, weight_ref, rows_ref, gain_ref, q_ref, xr_ref
):
    band = band_ref[5]
    across = []
    sources = []
    for back, ref in ((0, s0), (1, s1), (3, s3), (2, s2)):
        source = lax.rem(band + (NB - back), NB)
        sources.append(source)
        cells = ref[0:SHARD, :]
        extra = ref[SHARD : SHARD + 16, :].astype(F32)[0:1]
        across.append(extra)
        scale = jnp.transpose(jnp.broadcast_to(extra[:, 0:HD] + extra[:, HD : 2 * HD], (HD, HD)))
        projected = (
            jnp.dot(cells, weight_ref[...], preferred_element_type=F32) + rows_ref[0:1, 0:384]
        )
        for head in range(HEADS):
            lanes = slice(head * HD, (head + 1) * HD)
            values = normed(projected[:, lanes] * scale + rows_ref[1:2, lanes], gain_ref[...])
            for i in range(2):
                rows = pl.ds(pl.multiple_of(i * FRAME + source * 64, 64), 64)
                q_ref[head, rows, :] = values[i * 64 : (i + 1) * 64]
        for i in range(2):
            rows = pl.ds(pl.multiple_of(i * FRAME + source * 64, 64), 64)
            xr_ref[rows, :] = cells[i * 64 : (i + 1) * 64]
    lines = []
    for term in range(2):
        pieces = []
        for i in range(2):
            for b in range(NB):
                lanes = slice(term * HD + i * 64, term * HD + (i + 1) * 64)
                piece = across[0][:, lanes]
                for source, extra in zip(sources[1:], across[1:]):
                    piece = jnp.where(source == b, extra[:, lanes], piece)
                pieces.append(piece)
        lines.append(jnp.concatenate(pieces, axis=1))
    place = lax.broadcasted_iota(jnp.int32, (16, 512), 0)
    tail = jnp.where(place == 0, lines[0], jnp.where(place == 1, lines[1], 0.0))
    xr_ref[OWN : OWN + 16, :] = tail.astype(BF16)


def queries_of(band, shards, weight, rows, gain):
    return pl.pallas_call(
        query_kernel,
        in_specs=[SMEM] + [VMEM] * 7,
        out_specs=[VMEM, VMEM],
        out_shape=[
            jax.ShapeDtypeStruct((HEADS, OWN, HD), BF16),
            jax.ShapeDtypeStruct((OWN + 16, 512), BF16),
        ],
        compiler_params=params(8),
        cost_estimate=pl.CostEstimate(
            flops=2 * 512 * 512 * 384, bytes_accessed=2000000, transcendentals=0
        ),
    )(band, *in_vmem(*shards, weight, rows), gain[None] * FACTOR)


def store_rows(o_ref, base, results):
    lane = lax.broadcasted_iota(jnp.int32, (FRAME, HD), 1)
    marks = jnp.zeros((FRAME, HD), F32)
    for head, (mixed, peak, weight_sum) in enumerate(results):
        some = weight_sum > 0.0
        safe = jnp.where(some, weight_sum, 1.0)
        o_ref[pl.ds(pl.multiple_of(head * OWN + base, FRAME), FRAME), :] = (mixed / safe).astype(
            BF16
        )
        level = jnp.where(some, peak + jnp.log2(safe), NONE)
        marks = jnp.where(lane == head, level, marks)
    for half in range(2):
        turned = jnp.transpose(marks[half * HD : (half + 1) * HD])[0:8]
        first, second, third = split_bf16(turned, 3)
        at = pl.multiple_of(HEADS * OWN + (base // HD + half) * 32, 32)
        tail = jnp.concatenate([first, second, third, jnp.zeros((8, HD), F32)], axis=0)
        o_ref[pl.ds(at, 32), :] = tail.astype(BF16)


LONG = 12


def attend_group(info_ref, group, q_ref, o_ref, key_t, value, total, peak, weigh):
    x_here, z_here, core = place_of(info_ref)
    group_frame = x_here * 16 + lax.rem(z_here + NZ - group, NZ) * 4 + core * 2

    def bounds(i):
        ends = []
        for edge in clip_of_frame(info_ref, group_frame + i):
            inside = [jnp.clip(edge - 16 * x - 4 * z_here, 0, 4) for x in range(NX)]
            ends.append(inside[0] + inside[1] + inside[2] + inside[3])
        return ends[0], ends[1] - ends[0]

    first0, count0 = bounds(0)
    first1, count1 = bounds(1)
    full = (count0 == LONG) & (count1 == LONG) & (first0 == first1)

    @pl.when(full)
    def _():
        start = pl.multiple_of(first0 * FRAME, FRAME)
        units = [(head, base) for base in (0, FRAME) for head in range(HEADS)]

        def scores_of(unit):
            head, base = unit
            return jnp.dot(
                q_ref[head, base : base + FRAME, :],
                key_t[head, :, pl.ds(start, LONG * FRAME)],
                preferred_element_type=F32,
            )

        scores = scores_of(units[0])
        results = []
        for n, (head, base) in enumerate(units):
            ahead = scores_of(units[n + 1]) if n + 1 < len(units) else None
            top = jnp.max(scores, axis=-1, keepdims=True)
            weights = jnp.exp2(scores - top)
            weight_sum = jnp.sum(weights, axis=-1, keepdims=True)
            mixed = jnp.dot(
                weights.astype(BF16),
                value[head, pl.ds(start, LONG * FRAME), :],
                preferred_element_type=F32,
            )
            results.append((mixed, top, weight_sum))
            if head == HEADS - 1:
                store_rows(o_ref, base, results)
                results = []
            scores = ahead

    @pl.when(jnp.logical_not(full))
    def _():
        def one_frame(i, carry):
            first = jnp.where(i == 0, first0, first1)
            count = jnp.where(i == 0, count0, count1)
            base = pl.multiple_of(i * FRAME, FRAME)
            total[...] = jnp.zeros_like(total)
            weigh[...] = jnp.zeros_like(weigh)
            peak[...] = jnp.full_like(peak, NONE)

            def block(start, size):
                for head in range(HEADS):
                    scores = jnp.dot(
                        q_ref[head, pl.ds(base, FRAME), :],
                        key_t[head, :, pl.ds(start, size)],
                        preferred_element_type=F32,
                    )
                    old = peak[head][:, 0:1]
                    new = jnp.maximum(old, jnp.max(scores, axis=-1, keepdims=True))
                    fade = jnp.exp2(old - new)
                    weights = jnp.exp2(scores - new)
                    mixed = jnp.dot(
                        weights.astype(BF16),
                        value[head, pl.ds(start, size), :],
                        preferred_element_type=F32,
                    )
                    total[head] = total[head] * fade + mixed
                    weigh[head] = weigh[head] * fade + jnp.sum(weights, axis=-1, keepdims=True)
                    peak[head] = jnp.broadcast_to(new, (FRAME, HD))

            def wide(j, c):
                block(pl.multiple_of((first + j * 4) * FRAME, FRAME), 4 * FRAME)
                return c

            def narrow(j, c):
                block(pl.multiple_of((first + j) * FRAME, FRAME), FRAME)
                return c

            wides = count // 4
            lax.fori_loop(0, wides, wide, 0)
            lax.fori_loop(wides * 4, count, narrow, 0)
            store_rows(
                o_ref,
                base,
                [(total[h], peak[h][:, 0:1], weigh[h][:, 0:1]) for h in range(HEADS)],
            )
            return carry

        lax.fori_loop(0, 2, one_frame, 0)


def project_block(ref, start, wk_ref, wv_ref, rows_ref, cols_ref, key_t, value):
    cells = ref[0:OWN, :]
    extra = ref[OWN : OWN + 16, :].astype(F32)
    scale = extra[0:1] + extra[1:2]
    keys = lax.dot_general(
        wk_ref[...], cells, (((1,), (1,)), ((), ())), preferred_element_type=F32
    )
    for head in range(HEADS):
        lanes = slice(head * HD, (head + 1) * HD)
        offset = jnp.concatenate([cols_ref[0, lanes, :]] * 4, axis=1)
        moved = jnp.concatenate([cols_ref[1, lanes, :]] * 4, axis=1)
        gain = jnp.concatenate([cols_ref[2, 0:HD, :]] * 4, axis=1)
        part = (keys[lanes] + offset) * scale + moved
        mean_square = jnp.mean(part * part, axis=0, keepdims=True)
        key_t[head, :, pl.ds(start, OWN)] = (
            part * lax.rsqrt(mean_square + EPSILON) * gain
        ).astype(BF16)
    down = jnp.concatenate(
        [
            jnp.transpose(jnp.broadcast_to(scale[:, j * HD : (j + 1) * HD], (HD, HD)))
            for j in range(4)
        ],
        axis=0,
    )
    values = jnp.dot(cells, wv_ref[...], preferred_element_type=F32) + rows_ref[0:1, 768:1152]
    for head in range(HEADS):
        lanes = slice(head * HD, (head + 1) * HD)
        value[head, pl.ds(start, OWN), :] = (
            values[:, lanes] * down + rows_ref[1:2, 768 + head * HD : 768 + (head + 1) * HD]
        ).astype(BF16)


def first_kernel(
    info_ref, q_hbm, a0, b0, a1, b1, a3, b3, a2, b2, wk_hbm, wv_hbm, rows_hbm, cols_hbm,
    o2, key_out, value_out, key_t, value, blocks, q2, wk_ref, wv_ref, rows_ref, cols_ref,
    total, peak, weigh, sems,
):
    x_here, _, core = place_of(info_ref)
    weight_copies = fetch(
        (wk_hbm, wv_hbm, rows_hbm, cols_hbm), (wk_ref, wv_ref, rows_ref, cols_ref), sems
    )
    sources = (a0, b0, a1, b1, a3, b3, a2, b2)
    block_copies = fetch(sources, [blocks.at[i] for i in range(8)], sems, 4)
    (query_copy,) = fetch([q_hbm], [q2], sems, 12)
    for copy in weight_copies:
        copy.wait()
    for at in range(8):
        if at % 4 == 0:
            for copy in block_copies[at : at + 4]:
                copy.wait()
        source = lax.rem(x_here + (NX - (0, 1, 3, 2)[at // 2]), NX)
        core_at = core if at % 2 == 0 else 1 - core
        start = pl.multiple_of((source * 2 + core_at) * OWN, OWN)
        project_block(blocks.at[at], start, wk_ref, wv_ref, rows_ref, cols_ref, key_t, value)
    copies = fetch((key_t, value), (key_out, value_out), sems, 13)
    query_copy.wait()
    attend_group(info_ref, 2, q2, o2, key_t, value, total, peak, weigh)
    for copy in copies:
        copy.wait()


def state():
    return [
        pltpu.VMEM((HEADS, FRAME, HD), F32),
        pltpu.VMEM((HEADS, FRAME, HD), F32),
        pltpu.VMEM((HEADS, FRAME, HD), F32),
    ]


PARTIAL = jax.ShapeDtypeStruct((HEADS * OWN + 128, HD), BF16)


def attend_first(info, query, near, far, wk, wv, rows, cols):
    return pl.pallas_call(
        first_kernel,
        in_specs=[SMEM] + [ANY] * 9 + [HBM] * 4,
        out_specs=[VMEM, ANY, ANY],
        out_shape=[
            PARTIAL,
            jax.ShapeDtypeStruct((HEADS, HD, KEYS), BF16),
            jax.ShapeDtypeStruct((HEADS, KEYS, HD), BF16),
        ],
        scratch_shapes=[
            pltpu.VMEM((HEADS, HD, KEYS), BF16),
            pltpu.VMEM((HEADS, KEYS, HD), BF16),
            pltpu.VMEM((8, OWN + 16, 512), BF16),
            pltpu.VMEM((HEADS, OWN, HD), BF16),
            pltpu.VMEM((384, 512), BF16),
            pltpu.VMEM((512, 384), BF16),
            pltpu.VMEM((8, 1152), F32),
            pltpu.VMEM((3, 384, HD), F32),
        ]
        + state()
        + [pltpu.SemaphoreType.DMA((15,))],
        compiler_params=params(42),
        cost_estimate=pl.CostEstimate(
            flops=15000000000, bytes_accessed=10000000, transcendentals=0
        ),
    )(
        info,
        query,
        *[block for pair in zip(near, far) for block in pair],
        *pinned(wk, wv, rows, cols),
    )


def next_kernel(groups, info_ref, key_t, value, *refs):
    count = len(groups)
    sources, refs = refs[:count], refs[-(2 * count + 4) :]
    outs, queries, scratch, sems = refs[:count], refs[count : 2 * count], refs[-4:-1], refs[-1]
    for copy in fetch(sources, queries, sems):
        copy.wait()
    for group, q_ref, o_ref in zip(groups, queries, outs):
        attend_group(info_ref, group, q_ref, o_ref, key_t, value, *scratch)


def attend_next(groups, info, queries, key_t, value, *after):
    key_t, value = [
        pltpu.with_memory_space_constraint(array, pltpu.VMEM) for array in (key_t, value)
    ]
    return pl.pallas_call(
        functools.partial(next_kernel, groups),
        in_specs=[SMEM, VMEM, VMEM] + [ANY] * (len(groups) + len(after)),
        out_specs=[VMEM] * len(groups),
        out_shape=[PARTIAL] * len(groups),
        scratch_shapes=[pltpu.VMEM((HEADS, OWN, HD), BF16)] * len(groups)
        + state()
        + [pltpu.SemaphoreType.DMA((len(groups),))],
        compiler_params=params(42),
        cost_estimate=pl.CostEstimate(
            flops=8000000000 * len(groups), bytes_accessed=8000000, transcendentals=0
        ),
    )(info, key_t, value, *queries, *after)


def merge_kernel(p0, p1, p2, p3, out_ref):
    parts = (p0, p1, p2, p3)
    for at in range(4):
        base = HEADS * OWN + at * 32
        levels = []
        for ref in parts:
            marks = ref[base : base + 32, :].astype(F32)
            levels.append(marks[0:8] + marks[8:16] + marks[16:24])
        top = functools.reduce(jnp.maximum, levels)
        shares = [jnp.exp2(level - top) for level in levels]
        weight_sum = functools.reduce(jnp.add, shares)
        stacked = jnp.concatenate([share / weight_sum for share in shares], axis=0)
        columns = jnp.transpose(
            jnp.concatenate([stacked, jnp.zeros((HD - 32, HD), F32)], axis=0)
        )
        for head in range(HEADS):
            rows = slice(head * OWN + at * HD, head * OWN + (at + 1) * HD)
            mixed = functools.reduce(
                jnp.add,
                [
                    ref[rows, :].astype(F32) * columns[:, i * 8 + head : i * 8 + head + 1]
                    for i, ref in enumerate(parts)
                ],
            )
            out_ref[head, at * HD : (at + 1) * HD, :] = mixed.astype(BF16)


def merge(parts):
    return pl.pallas_call(
        merge_kernel,
        in_specs=[VMEM] * 4,
        out_specs=VMEM,
        out_shape=jax.ShapeDtypeStruct((HEADS, OWN, HD), BF16),
        compiler_params=params(8),
    )(*in_vmem(*parts))


def per_device(
    section_in,
    norm_gain,
    conv_weight,
    conv_bias,
    lengths,
    embed_weight,
    embed_bias,
    mod_shift,
    mod_scale,
    qkv_weight,
    q_gain,
    k_gain,
):
    info = jnp.concatenate(
        [lengths, jnp.stack([lax.axis_index("tm"), lax.axis_index("band")])]
    ).astype(jnp.int32)
    above = halo(section_in[:, 7:8], 0, 1)
    below = halo(section_in[:, 0:1], 0, -1)
    cur = jnp.concatenate([above, section_in, below], axis=1)
    prev = halo(cur, 1, 0)
    qkv = jnp.transpose(qkv_weight, (1, 2, 0, 3)).reshape(9, 3072, HD)
    section_out, send, embed_near, qkv_near = conv(
        info, cur, prev, norm_gain, conv_bias, embed_weight, embed_bias, conv_weight, qkv
    )
    wq, wk, wv, rows, cols = fold(
        embed_near, embed_bias, mod_shift, mod_scale, k_gain, qkv_near
    )
    shards = (send, shift_band(send, 1), shift_band(send, 3), shift_band(send, 2))
    query, xr = queries_of(
        info, shards, wq, rows, q_gain
    )
    far_own = shift_tm(xr, swap=True)
    a1, a3 = shift_tm(xr, dx=1), shift_tm(xr, dx=3)
    a2, q1, q3, q2 = together(
        shift_tm(xr, dx=2),
        shift_tm(query, dz=1),
        shift_tm(query, dz=3),
        shift_tm(query, dz=2),
    )
    near = (xr, a1, a3, a2)
    far = (far_own,) + tuple(shift_tm(part, swap=True) for part in near[1:])
    o2, key_t, value = attend_first(info, q2, near, far, wk, wv, rows, cols)
    p2 = shift_tm(o2, dz=2)
    o1, o3 = attend_next((1, 3), info, (q1, q3), key_t, value)
    p1, p3 = shift_tm(o1, dz=3), shift_tm(o3, dz=1)
    (o0,) = attend_next((0,), info, (query,), key_t, value, p2)
    parts = (o0, p1, p3, p2)
    attended = jnp.transpose(merge(parts), (1, 0, 2))
    return (section_out, attended)


def solution(mesh):
    return jax.shard_map(
        per_device,
        mesh=mesh,
        in_specs=(
            P("tm", "band", None, None),
            P(),
            P(),
            P(),
            P(),
            P(),
            P(),
            P(),
            P(),
            P(None, None, "band", None),
            P(),
            P(),
        ),
        out_specs=(P("tm", "band", None, None), P("tm", "band", None)),
        check_vma=False,
    )
```

```python
import functools

import jax
import jax.numpy as jnp
from jax import lax
from jax.experimental import pallas as pl
from jax.experimental.pallas import tpu as pltpu
from jax.sharding import PartitionSpec as P

EPSILON = 1e-06
NONE = -1e30
NX, NZ, NC, NB = 4, 4, 2, 4
HD = 128
FACTOR = 1.4426950408889634 / HD**0.5
HEADS = 3
SHARD = 128
FRAME = 256
OWN = 512
KEYS = 4096
F32 = jnp.float32
BF16 = jnp.bfloat16
MIB = 1024 * 1024


def params(mib):
    return pltpu.CompilerParams(vmem_limit_bytes=mib * MIB)


def fetch(sources, targets, sems, base=0):
    copies = [
        pltpu.make_async_copy(source, target, sems.at[base + at])
        for at, (source, target) in enumerate(zip(sources, targets))
    ]
    for copy in copies:
        copy.start()
    return copies


SMEM = pl.BlockSpec(memory_space=pltpu.SMEM)
VMEM = pl.BlockSpec(memory_space=pltpu.VMEM)
HBM = pl.BlockSpec(memory_space=pltpu.HBM)
ANY = pl.BlockSpec(memory_space=pl.ANY)


def pinned(*arrays):
    return [pltpu.with_memory_space_constraint(array, pltpu.HBM) for array in arrays]


def in_vmem(*arrays):
    return [pltpu.with_memory_space_constraint(array, pltpu.VMEM) for array in arrays]


def clip_of_frame(info_ref, frame):
    first, last, end = 0, 0, 0
    for clip in range(4):
        start, end = end, end + info_ref[clip]
        inside = (frame >= start) & (frame < end)
        first = jnp.where(inside, start, first)
        last = jnp.where(inside, end, last)
    return first, last


def place_of(info_ref):
    place = info_ref[4]
    return place // (NZ * NC), place // NC % NZ, place % NC


def split_bf16(value, count):
    parts = []
    for _ in range(count):
        part = value.astype(BF16).astype(F32)
        parts.append(part)
        value = value - part
    return parts


def after(array, *others):
    def kernel(source, *refs):
        (copy,) = fetch([source], [refs[-2]], refs[-1])
        copy.wait()

    return pl.pallas_call(
        kernel,
        in_specs=[ANY] * (1 + len(others)),
        out_specs=ANY,
        out_shape=jax.ShapeDtypeStruct(array.shape, array.dtype),
        scratch_shapes=[pltpu.SemaphoreType.DMA((1,))],
        compiler_params=params(2),
    )(array, *others)


def tm_index(x, z, c):
    return (x * NZ + z) * NC + c


def shift_tm(block, dx=0, dz=0, swap=False):
    route = []
    for x in range(NX):
        for z in range(NZ):
            for c in range(NC):
                target = tm_index((x + dx) % NX, (z + dz) % NZ, 1 - c if swap else c)
                route.append((tm_index(x, z, c), target))
    return lax.ppermute(block, "tm", route)


def shift_band(block, db):
    return lax.ppermute(block, "band", [(i, (i + db) % NB) for i in range(NB)])


def halo(block, dt, db):
    count = lax.axis_size("tm")
    route = []
    for t in range(count):
        for b in range(NB):
            if t + dt < count and 0 <= b + db < NB:
                route.append((t * NB + b, (t + dt) * NB + b + db))
    return lax.ppermute(block, ("tm", "band"), route)


def fold_kernel(
    embed_ref, bias_ref, shift_ref, scale_ref, gain_ref, qkv_ref, wq_ref, wk_ref, wv_ref, rows_ref, cols_ref,
    left,
):
    width = left.shape[1]
    gain = 1.0 + scale_ref[...]
    for lo in range(0, 512, 64):
        weight = embed_ref[lo : lo + 64, :].astype(F32)
        centred = weight - jnp.mean(weight, axis=-1, keepdims=True)
        left[lo : lo + 64, :] = (centred * gain).astype(BF16)
    bias = bias_ref[...]
    bias = (bias - jnp.mean(bias, axis=-1, keepdims=True)) * gain
    extra = jnp.zeros((16, width), F32)
    place = lax.broadcasted_iota(jnp.int32, (16, width), 0)
    for at, part in enumerate(split_bf16(bias, 3) + split_bf16(shift_ref[...], 3)):
        extra = jnp.where(place == at, part, extra)
    left[512:528, :] = extra.astype(BF16)
    where = lax.broadcasted_iota(jnp.int32, (8, HD), 0)
    cols_ref[2, 0:HD, :] = jnp.transpose(jnp.broadcast_to(gain_ref[...], (HD, HD)))
    for pair in ((0, 1), (2, 3), (4, 5), (6, 7), (8,)):
        right = jnp.concatenate([qkv_ref[i] for i in pair], axis=1)
        both = jnp.dot(left[...], right, preferred_element_type=F32)
        for at, block in enumerate(pair):
            part = both[:, at * HD : (at + 1) * HD]
            head = slice(block % HEADS * HD, (block % HEADS + 1) * HD)
            offset = part[512:513] + part[513:514] + part[514:515]
            moved = part[515:516] + part[516:517] + part[517:518]
            rows_ref[:, block * HD : (block + 1) * HD] = jnp.where(
                where == 0, offset, jnp.where(where == 1, moved, 0.0)
            )
            if block // HEADS == 0:
                wq_ref[:, head] = part[0:512].astype(BF16)
            elif block // HEADS == 1:
                wk_ref[head, :] = jnp.transpose(part[0:512]).astype(BF16)
                cols_ref[0, head, :] = jnp.transpose(jnp.broadcast_to(offset, (HD, HD)))
                cols_ref[1, head, :] = jnp.transpose(jnp.broadcast_to(moved, (HD, HD)))
            else:
                wv_ref[:, head] = part[0:512].astype(BF16)


def fold(embed_weight, embed_bias, mod_shift, mod_scale, k_gain, qkv):
    return pl.pallas_call(
        fold_kernel,
        in_specs=[VMEM] * 6,
        out_specs=[VMEM] * 5,
        out_shape=[
            jax.ShapeDtypeStruct((512, 384), BF16),
            jax.ShapeDtypeStruct((384, 512), BF16),
            jax.ShapeDtypeStruct((512, 384), BF16),
            jax.ShapeDtypeStruct((8, 1152), F32),
            jax.ShapeDtypeStruct((3, 384, HD), F32),
        ],
        scratch_shapes=[pltpu.VMEM((528, 3072), BF16)],
        compiler_params=params(16),
        cost_estimate=pl.CostEstimate(
            flops=2 * 528 * 3072 * 1152, bytes_accessed=12000000, transcendentals=0
        ),
    )(
        *in_vmem(embed_weight),
        embed_bias[None],
        mod_shift[None],
        mod_scale[None],
        k_gain[None],
        *in_vmem(qkv),
    )


def activate(cells, gain, act, slot, place):
    mean_square = jnp.mean(cells * cells, axis=-1, keepdims=True)
    scaled = cells * lax.rsqrt(mean_square + EPSILON) * gain
    active = (scaled * jax.nn.sigmoid(scaled)).astype(BF16).astype(F32)
    act[0, slot] = jnp.where(place == 0, 0.0, pltpu.roll(active, 1, 0))
    act[1, slot] = active
    act[2, slot] = jnp.where(place == 7, 0.0, pltpu.roll(active, 79, 0))


def newest_kernel(
    cur_ref, gain_hbm, weight_hbm, embed_hbm, qkv_hbm, part_ref, embed_out, qkv_out,
    act, gain_ref, weight_ref, sems,
):
    (gain_copy,) = fetch([gain_hbm], [gain_ref], sems)
    weight_copies = fetch(
        [weight_hbm.at[2, r] for r in range(3)], [weight_ref.at[r] for r in range(3)], sems, 1
    )
    copies = fetch((embed_hbm, qkv_hbm), (embed_out, qkv_out), sems, 4)
    place = lax.broadcasted_iota(jnp.int32, (80, 512), 0) % 8
    gain_copy.wait()
    for slot in range(2):
        activate(cur_ref[slot].astype(F32).reshape(80, 512), gain_ref[...], act, slot, place)
    total = jnp.zeros((SHARD, 512), F32)
    for tap_row in range(3):
        weight_copies[tap_row].wait()
        for tap_col in range(3):
            piece = jnp.concatenate(
                [act[tap_col, i, tap_row * 8 : tap_row * 8 + 64, :] for i in range(2)], axis=0
            ).astype(BF16)
            total = total + jnp.dot(
                piece, weight_ref[tap_row, tap_col], preferred_element_type=F32
            )
    part_ref[...] = total
    for copy in copies:
        copy.wait()


def conv_newest(cur, norm_gain, conv_weight, embed_weight, qkv):
    return pl.pallas_call(
        newest_kernel,
        in_specs=[VMEM] + [HBM] * 4,
        out_specs=[VMEM] + [ANY] * 2,
        out_shape=[
            jax.ShapeDtypeStruct((SHARD, 512), F32),
            jax.ShapeDtypeStruct(embed_weight.shape, BF16),
            jax.ShapeDtypeStruct(qkv.shape, BF16),
        ],
        scratch_shapes=[
            pltpu.VMEM((3, 2, 80, 512), F32),
            pltpu.VMEM((1, 512), F32),
            pltpu.VMEM((3, 3, 512, 512), BF16),
            pltpu.SemaphoreType.DMA((6,)),
        ],
        compiler_params=params(16),
        cost_estimate=pl.CostEstimate(
            flops=2 * 128 * 4608 * 512, bytes_accessed=15000000, transcendentals=0
        ),
    )(*in_vmem(cur), *pinned(norm_gain[None], conv_weight, embed_weight, qkv))


def conv_kernel(
    info_ref, cur_ref, prev_ref, part_ref, embed_ref, gain_hbm, bias_hbm, embed_bias_hbm, weight_hbm,
    out_ref, send_ref,
    act, gain_ref, bias_ref, embed_bias_ref, weight_ref, sems,
):
    copies = fetch(
        (gain_hbm, bias_hbm, embed_bias_hbm), (gain_ref, bias_ref, embed_bias_ref), sems
    )
    taps = [(t, r) for t in range(2) for r in range(3)]
    weight_copies = fetch(
        [weight_hbm.at[tap] for tap in taps], [weight_ref.at[tap] for tap in taps], sems, 3
    )
    first_frame = info_ref[4] * 2
    slots = []
    for i in range(2):
        clip_first, _ = clip_of_frame(info_ref, first_frame + i)
        slots.append(
            [jnp.maximum(first_frame + i - 2 + t, clip_first) - first_frame + 2 for t in range(2)]
        )
    place = lax.broadcasted_iota(jnp.int32, (80, 512), 0) % 8
    for copy in copies:
        copy.wait()
    for slot in range(4):
        cells = (prev_ref if slot < 2 else cur_ref)[slot % 2].astype(F32).reshape(80, 512)
        activate(cells, gain_ref[...], act, slot, place)
    inputs = jnp.concatenate(
        [cur_ref[i, 1:9].astype(F32).reshape(64, 512) for i in range(2)], axis=0
    )
    total = inputs + bias_ref[...] + part_ref[...]
    for at, (tap_time, tap_row) in enumerate(taps):
        weight_copies[at].wait()
        for tap_col in range(3):
            piece = jnp.concatenate(
                [
                    act[tap_col, slots[i][tap_time], tap_row * 8 : tap_row * 8 + 64, :]
                    for i in range(2)
                ],
                axis=0,
            ).astype(BF16)
            total = total + jnp.dot(
                piece, weight_ref[tap_time, tap_row, tap_col], preferred_element_type=F32
            )
    section = total.astype(BF16)
    out_ref[...] = section.reshape(out_ref.shape)
    send_ref[0:SHARD, :] = section
    embedded = jnp.dot(section, embed_ref[...], preferred_element_type=F32) + embed_bias_ref[...]
    center = embedded - jnp.mean(embedded, axis=-1, keepdims=True)
    spread = jnp.mean(center * center, axis=-1, keepdims=True)
    scale = lax.rsqrt(spread + EPSILON)
    across = jnp.transpose(jnp.broadcast_to(scale, (SHARD, SHARD)))[0:16]
    high, low = split_bf16(across, 2)
    tail = jnp.concatenate([high, low, jnp.zeros((16, 256), F32)], axis=1)
    place = lax.broadcasted_iota(jnp.int32, (16, 512), 0)
    send_ref[SHARD : SHARD + 16, :] = jnp.where(place == 0, tail, 0.0).astype(BF16)


def conv(info, cur, prev, part, norm_gain, conv_bias, embed_near, embed_bias, conv_weight):
    return pl.pallas_call(
        conv_kernel,
        in_specs=[SMEM] + [VMEM] * 4 + [HBM] * 4,
        out_specs=[VMEM] * 2,
        out_shape=[
            jax.ShapeDtypeStruct((2, 8, 8, 512), BF16),
            jax.ShapeDtypeStruct((SHARD + 16, 512), BF16),
        ],
        scratch_shapes=[
            pltpu.VMEM((3, 4, 80, 512), F32),
            pltpu.VMEM((1, 512), F32),
            pltpu.VMEM((1, 512), F32),
            pltpu.VMEM((1, 3072), F32),
            pltpu.VMEM((2, 3, 3, 512, 512), BF16),
            pltpu.SemaphoreType.DMA((9,)),
        ],
        compiler_params=params(24),
        cost_estimate=pl.CostEstimate(
            flops=2 * 128 * 13824 * 512, bytes_accessed=12000000, transcendentals=0
        ),
    )(
        info,
        *in_vmem(cur, prev, part, embed_near),
        *pinned(norm_gain[None], conv_bias[None], embed_bias[None], conv_weight),
    )


def normed(values, gain):
    mean_square = jnp.mean(values * values, axis=-1, keepdims=True)
    return (values * lax.rsqrt(mean_square + EPSILON) * gain).astype(BF16)


def query_kernel(
    band_ref, s0, s1, s3, s2, weight_ref, rows_ref, gain_ref, q_ref, xr_ref
):
    band = band_ref[5]
    across = []
    sources = []
    for back, ref in ((0, s0), (1, s1), (3, s3), (2, s2)):
        source = lax.rem(band + (NB - back), NB)
        sources.append(source)
        cells = ref[0:SHARD, :]
        extra = ref[SHARD : SHARD + 16, :].astype(F32)[0:1]
        across.append(extra)
        scale = jnp.transpose(jnp.broadcast_to(extra[:, 0:HD] + extra[:, HD : 2 * HD], (HD, HD)))
        projected = (
            jnp.dot(cells, weight_ref[...], preferred_element_type=F32) + rows_ref[0:1, 0:384]
        )
        for head in range(HEADS):
            lanes = slice(head * HD, (head + 1) * HD)
            values = normed(projected[:, lanes] * scale + rows_ref[1:2, lanes], gain_ref[...])
            for i in range(2):
                rows = pl.ds(pl.multiple_of(i * FRAME + source * 64, 64), 64)
                q_ref[head, rows, :] = values[i * 64 : (i + 1) * 64]
        for i in range(2):
            rows = pl.ds(pl.multiple_of(i * FRAME + source * 64, 64), 64)
            xr_ref[rows, :] = cells[i * 64 : (i + 1) * 64]
    lines = []
    for term in range(2):
        pieces = []
        for i in range(2):
            for b in range(NB):
                lanes = slice(term * HD + i * 64, term * HD + (i + 1) * 64)
                piece = across[0][:, lanes]
                for source, extra in zip(sources[1:], across[1:]):
                    piece = jnp.where(source == b, extra[:, lanes], piece)
                pieces.append(piece)
        lines.append(jnp.concatenate(pieces, axis=1))
    place = lax.broadcasted_iota(jnp.int32, (16, 512), 0)
    tail = jnp.where(place == 0, lines[0], jnp.where(place == 1, lines[1], 0.0))
    xr_ref[OWN : OWN + 16, :] = tail.astype(BF16)


def queries_of(band, shards, weight, rows, gain):
    return pl.pallas_call(
        query_kernel,
        in_specs=[SMEM] + [VMEM] * 7,
        out_specs=[VMEM, VMEM],
        out_shape=[
            jax.ShapeDtypeStruct((HEADS, OWN, HD), BF16),
            jax.ShapeDtypeStruct((OWN + 16, 512), BF16),
        ],
        compiler_params=params(8),
        cost_estimate=pl.CostEstimate(
            flops=2 * 512 * 512 * 384, bytes_accessed=2000000, transcendentals=0
        ),
    )(band, *in_vmem(*shards, weight, rows), gain[None] * FACTOR)


def store_rows(o_ref, base, results):
    lane = lax.broadcasted_iota(jnp.int32, (FRAME, HD), 1)
    marks = jnp.zeros((FRAME, HD), F32)
    for head, (mixed, peak, weight_sum) in enumerate(results):
        some = weight_sum > 0.0
        safe = jnp.where(some, weight_sum, 1.0)
        o_ref[pl.ds(pl.multiple_of(head * OWN + base, FRAME), FRAME), :] = (mixed / safe).astype(
            BF16
        )
        level = jnp.where(some, peak + jnp.log2(safe), NONE)
        marks = jnp.where(lane == head, level, marks)
    for half in range(2):
        turned = jnp.transpose(marks[half * HD : (half + 1) * HD])[0:8]
        first, second, third = split_bf16(turned, 3)
        at = pl.multiple_of(HEADS * OWN + (base // HD + half) * 32, 32)
        tail = jnp.concatenate([first, second, third, jnp.zeros((8, HD), F32)], axis=0)
        o_ref[pl.ds(at, 32), :] = tail.astype(BF16)


LONG = 12
SHORT = 4


def attend_group(info_ref, group, q_ref, o_ref, key_t, value):
    x_here, z_here, core = place_of(info_ref)
    group_frame = x_here * 16 + lax.rem(z_here + NZ - group, NZ) * 4 + core * 2

    def bounds(i):
        ends = []
        for edge in clip_of_frame(info_ref, group_frame + i):
            inside = [jnp.clip(edge - 16 * x - 4 * z_here, 0, 4) for x in range(NX)]
            ends.append(inside[0] + inside[1] + inside[2] + inside[3])
        return ends[0], ends[1] - ends[0]

    first0, count0 = bounds(0)
    first1, count1 = bounds(1)
    full = (count0 == LONG) & (count1 == LONG) & (first0 == first1)

    def rows_of(start, frames, bases, shown=None):
        width = frames * FRAME
        start = pl.multiple_of(start * FRAME, FRAME)
        units = [(head, base) for base in bases for head in range(HEADS)]

        def scores_of(unit):
            head, base = unit
            return jnp.dot(
                q_ref[head, pl.ds(base, FRAME), :],
                key_t[head, :, pl.ds(start, width)],
                preferred_element_type=F32,
            )

        scores = scores_of(units[0])
        results = []
        for n, (head, base) in enumerate(units):
            ahead = scores_of(units[n + 1]) if n + 1 < len(units) else None
            if shown is not None:
                scores = jnp.where(shown, scores, NONE)
            top = jnp.max(scores, axis=-1, keepdims=True)
            weights = jnp.exp2(scores - top)
            if shown is not None:
                weights = jnp.where(shown, weights, 0.0)
            weight_sum = jnp.sum(weights, axis=-1, keepdims=True)
            mixed = jnp.dot(
                weights.astype(BF16),
                value[head, pl.ds(start, width), :],
                preferred_element_type=F32,
            )
            results.append((mixed, top, weight_sum))
            if head == HEADS - 1:
                store_rows(o_ref, base, results)
                results = []
            scores = ahead

    @pl.when(full)
    def _():
        rows_of(first0, LONG, (0, FRAME))

    @pl.when(jnp.logical_not(full))
    def _():
        def one_frame(i, carry):
            first = jnp.where(i == 0, first0, first1)
            count = jnp.where(i == 0, count0, count1)
            base = pl.multiple_of(i * FRAME, FRAME)

            @pl.when(count == LONG)
            def _():
                rows_of(first, LONG, (base,))

            @pl.when(count != LONG)
            def _():
                start = jnp.minimum(first, KEYS // FRAME - SHORT)
                lane = lax.broadcasted_iota(jnp.int32, (FRAME, SHORT * FRAME), 1)
                low = (first - start) * FRAME
                rows_of(start, SHORT, (base,), (lane >= low) & (lane < low + count * FRAME))

            return carry

        lax.fori_loop(0, 2, one_frame, 0)


def project_block(ref, start, wk_ref, wv_ref, rows_ref, cols_ref, key_t, value):
    cells = ref[0:OWN, :]
    extra = ref[OWN : OWN + 16, :].astype(F32)
    scale = extra[0:1] + extra[1:2]
    keys = lax.dot_general(
        wk_ref[...], cells, (((1,), (1,)), ((), ())), preferred_element_type=F32
    )
    for head in range(HEADS):
        lanes = slice(head * HD, (head + 1) * HD)
        offset = jnp.concatenate([cols_ref[0, lanes, :]] * 4, axis=1)
        moved = jnp.concatenate([cols_ref[1, lanes, :]] * 4, axis=1)
        gain = jnp.concatenate([cols_ref[2, 0:HD, :]] * 4, axis=1)
        part = (keys[lanes] + offset) * scale + moved
        mean_square = jnp.mean(part * part, axis=0, keepdims=True)
        key_t[head, :, pl.ds(start, OWN)] = (
            part * lax.rsqrt(mean_square + EPSILON) * gain
        ).astype(BF16)
    down = jnp.concatenate(
        [
            jnp.transpose(jnp.broadcast_to(scale[:, j * HD : (j + 1) * HD], (HD, HD)))
            for j in range(4)
        ],
        axis=0,
    )
    values = jnp.dot(cells, wv_ref[...], preferred_element_type=F32) + rows_ref[0:1, 768:1152]
    for head in range(HEADS):
        lanes = slice(head * HD, (head + 1) * HD)
        value[head, pl.ds(start, OWN), :] = (
            values[:, lanes] * down + rows_ref[1:2, 768 + head * HD : 768 + (head + 1) * HD]
        ).astype(BF16)


def first_kernel(
    info_ref, q_hbm, a0, b0, a1, b1, a3, b3, a2, b2, wk_hbm, wv_hbm, rows_hbm, cols_hbm,
    o2, key_out, value_out, key_t, value, blocks, q2, wk_ref, wv_ref, rows_ref, cols_ref,
    sems,
):
    x_here, _, core = place_of(info_ref)
    weight_copies = fetch(
        (wk_hbm, wv_hbm, rows_hbm, cols_hbm), (wk_ref, wv_ref, rows_ref, cols_ref), sems
    )
    sources = (a0, b0, a1, b1, a3, b3, a2, b2)
    block_copies = fetch(sources, [blocks.at[i] for i in range(8)], sems, 4)
    (query_copy,) = fetch([q_hbm], [q2], sems, 12)
    for copy in weight_copies:
        copy.wait()
    for at in range(8):
        if at % 4 == 0:
            for copy in block_copies[at : at + 4]:
                copy.wait()
        source = lax.rem(x_here + (NX - (0, 1, 3, 2)[at // 2]), NX)
        core_at = core if at % 2 == 0 else 1 - core
        start = pl.multiple_of((source * 2 + core_at) * OWN, OWN)
        project_block(blocks.at[at], start, wk_ref, wv_ref, rows_ref, cols_ref, key_t, value)
    copies = fetch((key_t, value), (key_out, value_out), sems, 13)
    query_copy.wait()
    attend_group(info_ref, 2, q2, o2, key_t, value)
    for copy in copies:
        copy.wait()


PARTIAL = jax.ShapeDtypeStruct((HEADS * OWN + 128, HD), BF16)


def attend_first(info, query, near, far, wk, wv, rows, cols):
    return pl.pallas_call(
        first_kernel,
        in_specs=[SMEM] + [ANY] * 13,
        out_specs=[VMEM, ANY, ANY],
        out_shape=[
            PARTIAL,
            jax.ShapeDtypeStruct((HEADS, HD, KEYS), BF16),
            jax.ShapeDtypeStruct((HEADS, KEYS, HD), BF16),
        ],
        scratch_shapes=[
            pltpu.VMEM((HEADS, HD, KEYS), BF16),
            pltpu.VMEM((HEADS, KEYS, HD), BF16),
            pltpu.VMEM((8, OWN + 16, 512), BF16),
            pltpu.VMEM((HEADS, OWN, HD), BF16),
            pltpu.VMEM((384, 512), BF16),
            pltpu.VMEM((512, 384), BF16),
            pltpu.VMEM((8, 1152), F32),
            pltpu.VMEM((3, 384, HD), F32),
            pltpu.SemaphoreType.DMA((15,)),
        ],
        compiler_params=params(42),
        cost_estimate=pl.CostEstimate(
            flops=15000000000, bytes_accessed=10000000, transcendentals=0
        ),
    )(
        info,
        query,
        *[block for pair in zip(near, far) for block in pair],
        wk,
        wv,
        rows,
        cols,
    )


def next_kernel(groups, info_ref, key_t, value, *refs):
    count = len(groups)
    sources, refs = refs[:count], refs[-(2 * count + 1) :]
    outs, queries, sems = refs[:count], refs[count : 2 * count], refs[-1]
    for copy in fetch(sources, queries, sems):
        copy.wait()
    for group, q_ref, o_ref in zip(groups, queries, outs):
        attend_group(info_ref, group, q_ref, o_ref, key_t, value)


def attend_next(groups, info, queries, key_t, value, *needed):
    key_t, value = [
        pltpu.with_memory_space_constraint(array, pltpu.VMEM) for array in (key_t, value)
    ]
    return pl.pallas_call(
        functools.partial(next_kernel, groups),
        in_specs=[SMEM, VMEM, VMEM] + [ANY] * (len(groups) + len(needed)),
        out_specs=[VMEM] * len(groups),
        out_shape=[PARTIAL] * len(groups),
        scratch_shapes=[pltpu.VMEM((HEADS, OWN, HD), BF16)] * len(groups)
        + [pltpu.SemaphoreType.DMA((len(groups),))],
        compiler_params=params(42),
        cost_estimate=pl.CostEstimate(
            flops=8000000000 * len(groups), bytes_accessed=8000000, transcendentals=0
        ),
    )(info, key_t, value, *queries, *needed)


def merge_kernel(p0, p1, p2, p3, out_ref):
    parts = (p0, p1, p2, p3)
    for at in range(4):
        base = HEADS * OWN + at * 32
        levels = []
        for ref in parts:
            marks = ref[base : base + 32, :].astype(F32)
            levels.append(marks[0:8] + marks[8:16] + marks[16:24])
        top = functools.reduce(jnp.maximum, levels)
        shares = [jnp.exp2(level - top) for level in levels]
        weight_sum = functools.reduce(jnp.add, shares)
        stacked = jnp.concatenate([share / weight_sum for share in shares], axis=0)
        columns = jnp.transpose(
            jnp.concatenate([stacked, jnp.zeros((HD - 32, HD), F32)], axis=0)
        )
        for head in range(HEADS):
            rows = slice(head * OWN + at * HD, head * OWN + (at + 1) * HD)
            mixed = functools.reduce(
                jnp.add,
                [
                    ref[rows, :].astype(F32) * columns[:, i * 8 + head : i * 8 + head + 1]
                    for i, ref in enumerate(parts)
                ],
            )
            out_ref[head, at * HD : (at + 1) * HD, :] = mixed.astype(BF16)


def merge(parts):
    return pl.pallas_call(
        merge_kernel,
        in_specs=[VMEM] * 4,
        out_specs=VMEM,
        out_shape=jax.ShapeDtypeStruct((HEADS, OWN, HD), BF16),
        compiler_params=params(8),
    )(*in_vmem(*parts))


def per_device(
    section_in,
    norm_gain,
    conv_weight,
    conv_bias,
    lengths,
    embed_weight,
    embed_bias,
    mod_shift,
    mod_scale,
    qkv_weight,
    q_gain,
    k_gain,
):
    info = jnp.concatenate(
        [lengths, jnp.stack([lax.axis_index("tm"), lax.axis_index("band")])]
    ).astype(jnp.int32)
    above = halo(section_in[:, 7:8], 0, 1)
    below = halo(section_in[:, 0:1], 0, -1)
    cur = jnp.concatenate([above, section_in, below], axis=1)
    prev = halo(cur, 1, 0)
    qkv = jnp.transpose(qkv_weight, (1, 2, 0, 3)).reshape(9, 3072, HD)
    part, embed_near, qkv_near = conv_newest(cur, norm_gain, conv_weight, embed_weight, qkv)
    section_out, send = conv(
        info, cur, prev, part, norm_gain, conv_bias, embed_near, embed_bias, conv_weight
    )
    wq, wk, wv, rows, cols = fold(
        embed_near, embed_bias, mod_shift, mod_scale, k_gain, qkv_near
    )
    shards = (send, shift_band(send, 1), shift_band(send, 3), shift_band(send, 2))
    query, xr = queries_of(
        info, shards, wq, rows, q_gain
    )
    far_own = shift_tm(xr, swap=True)
    a1, a3 = shift_tm(xr, dx=1), shift_tm(xr, dx=3)
    q1, q3, q2 = shift_tm(query, dz=1), shift_tm(query, dz=3), shift_tm(query, dz=2)
    a2 = after(shift_tm(xr, dx=2), q1, q3, q2)
    near = (xr, a1, a3, a2)
    far = (far_own,) + tuple(shift_tm(part, swap=True) for part in near[1:])
    o2, key_t, value = attend_first(info, q2, near, far, wk, wv, rows, cols)
    p2 = shift_tm(o2, dz=2)
    o1, o3 = attend_next((1, 3), info, (q1, q3), key_t, value)
    p1, p3 = shift_tm(o1, dz=3), shift_tm(o3, dz=1)
    (o0,) = attend_next((0,), info, (query,), key_t, value, p2)
    parts = (o0, p1, p3, p2)
    attended = jnp.transpose(merge(parts), (1, 0, 2))
    return (section_out, attended)


def solution(mesh):
    return jax.shard_map(
        per_device,
        mesh=mesh,
        in_specs=(
            P("tm", "band", None, None),
            P(),
            P(),
            P(),
            P(),
            P(),
            P(),
            P(),
            P(),
            P(None, None, "band", None),
            P(),
            P(),
        ),
        out_specs=(P("tm", "band", None, None), P("tm", "band", None)),
        check_vma=False,
    )
```

```python
import functools

import jax
import jax.numpy as jnp
from jax import lax
from jax.experimental import pallas as pl
from jax.experimental.pallas import tpu as pltpu
from jax.sharding import PartitionSpec as P

EPSILON = 1e-06
NONE = -1e30
NX, NZ, NC, NB = 4, 4, 2, 4
HD = 128
FACTOR = 1.4426950408889634 / HD**0.5
HEADS = 3
SHARD = 128
FRAME = 256
OWN = 512
KEYS = 4096
F32 = jnp.float32
BF16 = jnp.bfloat16
MIB = 1024 * 1024


def params(mib):
    return pltpu.CompilerParams(vmem_limit_bytes=mib * MIB)


def fetch(sources, targets, sems, base=0):
    copies = [
        pltpu.make_async_copy(source, target, sems.at[base + at])
        for at, (source, target) in enumerate(zip(sources, targets))
    ]
    for copy in copies:
        copy.start()
    return copies


SMEM = pl.BlockSpec(memory_space=pltpu.SMEM)
VMEM = pl.BlockSpec(memory_space=pltpu.VMEM)
HBM = pl.BlockSpec(memory_space=pltpu.HBM)
ANY = pl.BlockSpec(memory_space=pl.ANY)


def pinned(*arrays):
    return [pltpu.with_memory_space_constraint(array, pltpu.HBM) for array in arrays]


def in_vmem(*arrays):
    return [pltpu.with_memory_space_constraint(array, pltpu.VMEM) for array in arrays]


def clip_of_frame(info_ref, frame):
    first, last, end = 0, 0, 0
    for clip in range(4):
        start, end = end, end + info_ref[clip]
        inside = (frame >= start) & (frame < end)
        first = jnp.where(inside, start, first)
        last = jnp.where(inside, end, last)
    return first, last


def place_of(info_ref):
    place = info_ref[4]
    return place // (NZ * NC), place // NC % NZ, place % NC


def split_bf16(value, count):
    parts = []
    for _ in range(count):
        part = value.astype(BF16).astype(F32)
        parts.append(part)
        value = value - part
    return parts


def after(array, *others):
    def kernel(source, *refs):
        (copy,) = fetch([source], [refs[-2]], refs[-1])
        copy.wait()

    return pl.pallas_call(
        kernel,
        in_specs=[ANY] * (1 + len(others)),
        out_specs=ANY,
        out_shape=jax.ShapeDtypeStruct(array.shape, array.dtype),
        scratch_shapes=[pltpu.SemaphoreType.DMA((1,))],
        compiler_params=params(2),
    )(array, *others)


def tm_index(x, z, c):
    return (x * NZ + z) * NC + c


def shift_tm(block, dx=0, dz=0, swap=False):
    route = []
    for x in range(NX):
        for z in range(NZ):
            for c in range(NC):
                target = tm_index((x + dx) % NX, (z + dz) % NZ, 1 - c if swap else c)
                route.append((tm_index(x, z, c), target))
    return lax.ppermute(block, "tm", route)


def shift_band(block, db):
    return lax.ppermute(block, "band", [(i, (i + db) % NB) for i in range(NB)])


def halo(block, dt, db):
    count = lax.axis_size("tm")
    route = []
    for t in range(count):
        for b in range(NB):
            if t + dt < count and 0 <= b + db < NB:
                route.append((t * NB + b, (t + dt) * NB + b + db))
    return lax.ppermute(block, ("tm", "band"), route)


def fold_kernel(
    embed_ref, bias_ref, shift_ref, scale_ref, gain_ref, qkv_ref, wq_ref, wk_ref, wv_ref, rows_ref, cols_ref,
    left,
):
    width = left.shape[1]
    gain = 1.0 + scale_ref[...]
    for lo in range(0, 512, 64):
        weight = embed_ref[lo : lo + 64, :].astype(F32)
        centred = weight - jnp.mean(weight, axis=-1, keepdims=True)
        left[lo : lo + 64, :] = (centred * gain).astype(BF16)
    bias = bias_ref[...]
    bias = (bias - jnp.mean(bias, axis=-1, keepdims=True)) * gain
    extra = jnp.zeros((16, width), F32)
    place = lax.broadcasted_iota(jnp.int32, (16, width), 0)
    for at, part in enumerate(split_bf16(bias, 3) + split_bf16(shift_ref[...], 3)):
        extra = jnp.where(place == at, part, extra)
    left[512:528, :] = extra.astype(BF16)
    where = lax.broadcasted_iota(jnp.int32, (8, HD), 0)
    cols_ref[2, 0:HD, :] = jnp.transpose(jnp.broadcast_to(gain_ref[...], (HD, HD)))
    for pair in ((0, 1), (2, 3), (4, 5), (6, 7), (8,)):
        right = jnp.concatenate([qkv_ref[i] for i in pair], axis=1)
        both = jnp.dot(left[...], right, preferred_element_type=F32)
        for at, block in enumerate(pair):
            part = both[:, at * HD : (at + 1) * HD]
            head = slice(block % HEADS * HD, (block % HEADS + 1) * HD)
            offset = part[512:513] + part[513:514] + part[514:515]
            moved = part[515:516] + part[516:517] + part[517:518]
            rows_ref[:, block * HD : (block + 1) * HD] = jnp.where(
                where == 0, offset, jnp.where(where == 1, moved, 0.0)
            )
            if block // HEADS == 0:
                wq_ref[:, head] = part[0:512].astype(BF16)
            elif block // HEADS == 1:
                wk_ref[head, :] = jnp.transpose(part[0:512]).astype(BF16)
                cols_ref[0, head, :] = jnp.transpose(jnp.broadcast_to(offset, (HD, HD)))
                cols_ref[1, head, :] = jnp.transpose(jnp.broadcast_to(moved, (HD, HD)))
            else:
                wv_ref[:, head] = part[0:512].astype(BF16)


def fold(embed_weight, embed_bias, mod_shift, mod_scale, k_gain, qkv):
    return pl.pallas_call(
        fold_kernel,
        in_specs=[VMEM] * 6,
        out_specs=[VMEM] * 5,
        out_shape=[
            jax.ShapeDtypeStruct((512, 384), BF16),
            jax.ShapeDtypeStruct((384, 512), BF16),
            jax.ShapeDtypeStruct((512, 384), BF16),
            jax.ShapeDtypeStruct((8, 1152), F32),
            jax.ShapeDtypeStruct((3, 384, HD), F32),
        ],
        scratch_shapes=[pltpu.VMEM((528, 3072), BF16)],
        compiler_params=params(16),
        cost_estimate=pl.CostEstimate(
            flops=2 * 528 * 3072 * 1152, bytes_accessed=12000000, transcendentals=0
        ),
    )(
        *in_vmem(embed_weight),
        embed_bias[None],
        mod_shift[None],
        mod_scale[None],
        k_gain[None],
        *in_vmem(qkv),
    )


def activate(cells, gain, act, slot, place):
    mean_square = jnp.mean(cells * cells, axis=-1, keepdims=True)
    scaled = cells * lax.rsqrt(mean_square + EPSILON) * gain
    active = (scaled * jax.nn.sigmoid(scaled)).astype(BF16).astype(F32)
    act[0, slot] = jnp.where(place == 0, 0.0, pltpu.roll(active, 1, 0))
    act[1, slot] = active
    act[2, slot] = jnp.where(place == 7, 0.0, pltpu.roll(active, 79, 0))


def newest_kernel(
    cur_ref, gain_hbm, weight_hbm, embed_hbm, qkv_hbm, part_ref, embed_out, qkv_out,
    act, gain_ref, weight_ref, sems,
):
    (gain_copy,) = fetch([gain_hbm], [gain_ref], sems)
    weight_copies = fetch(
        [weight_hbm.at[2, r] for r in range(3)], [weight_ref.at[r] for r in range(3)], sems, 1
    )
    copies = fetch((embed_hbm, qkv_hbm), (embed_out, qkv_out), sems, 4)
    place = lax.broadcasted_iota(jnp.int32, (80, 512), 0) % 8
    gain_copy.wait()
    for slot in range(2):
        activate(cur_ref[slot].astype(F32).reshape(80, 512), gain_ref[...], act, slot, place)
    total = jnp.zeros((SHARD, 512), F32)
    for tap_row in range(3):
        weight_copies[tap_row].wait()
        for tap_col in range(3):
            piece = jnp.concatenate(
                [act[tap_col, i, tap_row * 8 : tap_row * 8 + 64, :] for i in range(2)], axis=0
            ).astype(BF16)
            total = total + jnp.dot(
                piece, weight_ref[tap_row, tap_col], preferred_element_type=F32
            )
    part_ref[...] = total
    for copy in copies:
        copy.wait()


def conv_newest(cur, norm_gain, conv_weight, embed_weight, qkv):
    return pl.pallas_call(
        newest_kernel,
        in_specs=[VMEM] + [HBM] * 4,
        out_specs=[VMEM] + [ANY] * 2,
        out_shape=[
            jax.ShapeDtypeStruct((SHARD, 512), F32),
            jax.ShapeDtypeStruct(embed_weight.shape, BF16),
            jax.ShapeDtypeStruct(qkv.shape, BF16),
        ],
        scratch_shapes=[
            pltpu.VMEM((3, 2, 80, 512), F32),
            pltpu.VMEM((1, 512), F32),
            pltpu.VMEM((3, 3, 512, 512), BF16),
            pltpu.SemaphoreType.DMA((6,)),
        ],
        compiler_params=params(16),
        cost_estimate=pl.CostEstimate(
            flops=2 * 128 * 4608 * 512, bytes_accessed=15000000, transcendentals=0
        ),
    )(*in_vmem(cur), *pinned(norm_gain[None], conv_weight, embed_weight, qkv))


def conv_kernel(
    info_ref, cur_ref, prev_ref, part_ref, embed_ref, gain_hbm, bias_hbm, embed_bias_hbm, weight_hbm,
    out_ref, send_ref,
    act, gain_ref, bias_ref, embed_bias_ref, weight_ref, sems,
):
    copies = fetch(
        (gain_hbm, bias_hbm, embed_bias_hbm), (gain_ref, bias_ref, embed_bias_ref), sems
    )
    taps = [(t, r) for t in range(2) for r in range(3)]
    weight_copies = fetch(
        [weight_hbm.at[tap] for tap in taps], [weight_ref.at[tap] for tap in taps], sems, 3
    )
    first_frame = info_ref[4] * 2
    slots = []
    for i in range(2):
        clip_first, _ = clip_of_frame(info_ref, first_frame + i)
        slots.append(
            [jnp.maximum(first_frame + i - 2 + t, clip_first) - first_frame + 2 for t in range(2)]
        )
    place = lax.broadcasted_iota(jnp.int32, (80, 512), 0) % 8
    for copy in copies:
        copy.wait()
    for slot in range(4):
        cells = (prev_ref if slot < 2 else cur_ref)[slot % 2].astype(F32).reshape(80, 512)
        activate(cells, gain_ref[...], act, slot, place)
    inputs = jnp.concatenate(
        [cur_ref[i, 1:9].astype(F32).reshape(64, 512) for i in range(2)], axis=0
    )
    total = inputs + bias_ref[...] + part_ref[...]
    for at, (tap_time, tap_row) in enumerate(taps):
        weight_copies[at].wait()
        for tap_col in range(3):
            piece = jnp.concatenate(
                [
                    act[tap_col, slots[i][tap_time], tap_row * 8 : tap_row * 8 + 64, :]
                    for i in range(2)
                ],
                axis=0,
            ).astype(BF16)
            total = total + jnp.dot(
                piece, weight_ref[tap_time, tap_row, tap_col], preferred_element_type=F32
            )
    section = total.astype(BF16)
    out_ref[...] = section.reshape(out_ref.shape)
    send_ref[0:SHARD, :] = section
    embedded = jnp.dot(section, embed_ref[...], preferred_element_type=F32) + embed_bias_ref[...]
    center = embedded - jnp.mean(embedded, axis=-1, keepdims=True)
    spread = jnp.mean(center * center, axis=-1, keepdims=True)
    scale = lax.rsqrt(spread + EPSILON)
    across = jnp.transpose(jnp.broadcast_to(scale, (SHARD, SHARD)))[0:16]
    high, low = split_bf16(across, 2)
    tail = jnp.concatenate([high, low, jnp.zeros((16, 256), F32)], axis=1)
    place = lax.broadcasted_iota(jnp.int32, (16, 512), 0)
    send_ref[SHARD : SHARD + 16, :] = jnp.where(place == 0, tail, 0.0).astype(BF16)


def conv(info, cur, prev, part, norm_gain, conv_bias, embed_near, embed_bias, conv_weight):
    return pl.pallas_call(
        conv_kernel,
        in_specs=[SMEM] + [VMEM] * 4 + [HBM] * 4,
        out_specs=[VMEM] * 2,
        out_shape=[
            jax.ShapeDtypeStruct((2, 8, 8, 512), BF16),
            jax.ShapeDtypeStruct((SHARD + 16, 512), BF16),
        ],
        scratch_shapes=[
            pltpu.VMEM((3, 4, 80, 512), F32),
            pltpu.VMEM((1, 512), F32),
            pltpu.VMEM((1, 512), F32),
            pltpu.VMEM((1, 3072), F32),
            pltpu.VMEM((2, 3, 3, 512, 512), BF16),
            pltpu.SemaphoreType.DMA((9,)),
        ],
        compiler_params=params(24),
        cost_estimate=pl.CostEstimate(
            flops=2 * 128 * 13824 * 512, bytes_accessed=12000000, transcendentals=0
        ),
    )(
        info,
        *in_vmem(cur, prev, part, embed_near),
        *pinned(norm_gain[None], conv_bias[None], embed_bias[None], conv_weight),
    )


def normed(values, gain):
    mean_square = jnp.mean(values * values, axis=-1, keepdims=True)
    return (values * lax.rsqrt(mean_square + EPSILON) * gain).astype(BF16)


def query_kernel(
    band_ref, s0, s1, s3, s2, weight_ref, rows_ref, gain_ref, q_ref, xr_ref
):
    band = band_ref[5]
    across = []
    sources = []
    for back, ref in ((0, s0), (1, s1), (3, s3), (2, s2)):
        source = lax.rem(band + (NB - back), NB)
        sources.append(source)
        cells = ref[0:SHARD, :]
        extra = ref[SHARD : SHARD + 16, :].astype(F32)[0:1]
        across.append(extra)
        scale = jnp.transpose(jnp.broadcast_to(extra[:, 0:HD] + extra[:, HD : 2 * HD], (HD, HD)))
        projected = (
            jnp.dot(cells, weight_ref[...], preferred_element_type=F32) + rows_ref[0:1, 0:384]
        )
        for head in range(HEADS):
            lanes = slice(head * HD, (head + 1) * HD)
            values = normed(projected[:, lanes] * scale + rows_ref[1:2, lanes], gain_ref[...])
            for i in range(2):
                rows = pl.ds(pl.multiple_of(i * FRAME + source * 64, 64), 64)
                q_ref[head, rows, :] = values[i * 64 : (i + 1) * 64]
        for i in range(2):
            rows = pl.ds(pl.multiple_of(i * FRAME + source * 64, 64), 64)
            xr_ref[rows, :] = cells[i * 64 : (i + 1) * 64]
    lines = []
    for term in range(2):
        pieces = []
        for i in range(2):
            for b in range(NB):
                lanes = slice(term * HD + i * 64, term * HD + (i + 1) * 64)
                piece = across[0][:, lanes]
                for source, extra in zip(sources[1:], across[1:]):
                    piece = jnp.where(source == b, extra[:, lanes], piece)
                pieces.append(piece)
        lines.append(jnp.concatenate(pieces, axis=1))
    place = lax.broadcasted_iota(jnp.int32, (16, 512), 0)
    tail = jnp.where(place == 0, lines[0], jnp.where(place == 1, lines[1], 0.0))
    xr_ref[OWN : OWN + 16, :] = tail.astype(BF16)


def queries_of(band, shards, weight, rows, gain):
    return pl.pallas_call(
        query_kernel,
        in_specs=[SMEM] + [VMEM] * 7,
        out_specs=[VMEM, VMEM],
        out_shape=[
            jax.ShapeDtypeStruct((HEADS, OWN, HD), BF16),
            jax.ShapeDtypeStruct((OWN + 16, 512), BF16),
        ],
        compiler_params=params(8),
        cost_estimate=pl.CostEstimate(
            flops=2 * 512 * 512 * 384, bytes_accessed=2000000, transcendentals=0
        ),
    )(band, *in_vmem(*shards, weight, rows), gain[None] * FACTOR)


def store_rows(o_ref, base, results):
    lane = lax.broadcasted_iota(jnp.int32, (FRAME, HD), 1)
    marks = jnp.zeros((FRAME, HD), F32)
    for head, (mixed, peak, weight_sum) in enumerate(results):
        some = weight_sum > 0.0
        safe = jnp.where(some, weight_sum, 1.0)
        o_ref[pl.ds(pl.multiple_of(head * OWN + base, FRAME), FRAME), :] = (mixed / safe).astype(
            BF16
        )
        level = jnp.where(some, peak + jnp.log2(safe), NONE)
        marks = jnp.where(lane == head, level, marks)
    for half in range(2):
        turned = jnp.transpose(marks[half * HD : (half + 1) * HD])[0:8]
        first, second, third = split_bf16(turned, 3)
        at = pl.multiple_of(HEADS * OWN + (base // HD + half) * 32, 32)
        tail = jnp.concatenate([first, second, third, jnp.zeros((8, HD), F32)], axis=0)
        o_ref[pl.ds(at, 32), :] = tail.astype(BF16)


LONG = 12
SHORT = 4


def attend_group(info_ref, group, q_ref, o_ref, key_t, value):
    x_here, z_here, core = place_of(info_ref)
    group_frame = x_here * 16 + lax.rem(z_here + NZ - group, NZ) * 4 + core * 2

    def bounds(i):
        ends = []
        for edge in clip_of_frame(info_ref, group_frame + i):
            inside = [jnp.clip(edge - 16 * x - 4 * z_here, 0, 4) for x in range(NX)]
            ends.append(inside[0] + inside[1] + inside[2] + inside[3])
        return ends[0], ends[1] - ends[0]

    def rows_of(start, frames, base, shown=None):
        width = frames * FRAME
        start = pl.multiple_of(start * FRAME, FRAME)

        def scores_of(head):
            return jnp.dot(
                q_ref[head, pl.ds(base, FRAME), :],
                key_t[head, :, pl.ds(start, width)],
                preferred_element_type=F32,
            )

        scores = scores_of(0)
        results = []
        for head in range(HEADS):
            ahead = scores_of(head + 1) if head + 1 < HEADS else None
            if shown is not None:
                scores = jnp.where(shown, scores, NONE)
            top = jnp.max(scores, axis=-1, keepdims=True)
            weights = jnp.exp2(scores - top)
            if shown is not None:
                weights = jnp.where(shown, weights, 0.0)
            weight_sum = jnp.sum(weights, axis=-1, keepdims=True)
            mixed = jnp.dot(
                weights.astype(BF16),
                value[head, pl.ds(start, width), :],
                preferred_element_type=F32,
            )
            results.append((mixed, top, weight_sum))
            scores = ahead
        store_rows(o_ref, base, results)

    def one_frame(i, carry):
        first, count = bounds(i)
        base = pl.multiple_of(i * FRAME, FRAME)

        @pl.when(count == LONG)
        def _():
            rows_of(first, LONG, base)

        @pl.when(count != LONG)
        def _():
            start = jnp.minimum(first, KEYS // FRAME - SHORT)
            lane = lax.broadcasted_iota(jnp.int32, (FRAME, SHORT * FRAME), 1)
            low = (first - start) * FRAME
            rows_of(start, SHORT, base, (lane >= low) & (lane < low + count * FRAME))

        return carry

    lax.fori_loop(0, 2, one_frame, 0)


def project_block(ref, start, wk_ref, wv_ref, rows_ref, cols_ref, key_t, value):
    cells = ref[0:OWN, :]
    extra = ref[OWN : OWN + 16, :].astype(F32)
    scale = extra[0:1] + extra[1:2]
    keys = lax.dot_general(
        wk_ref[...], cells, (((1,), (1,)), ((), ())), preferred_element_type=F32
    )
    for head in range(HEADS):
        lanes = slice(head * HD, (head + 1) * HD)
        offset = jnp.concatenate([cols_ref[0, lanes, :]] * 4, axis=1)
        moved = jnp.concatenate([cols_ref[1, lanes, :]] * 4, axis=1)
        gain = jnp.concatenate([cols_ref[2, 0:HD, :]] * 4, axis=1)
        part = (keys[lanes] + offset) * scale + moved
        mean_square = jnp.mean(part * part, axis=0, keepdims=True)
        key_t[head, :, pl.ds(start, OWN)] = (
            part * lax.rsqrt(mean_square + EPSILON) * gain
        ).astype(BF16)
    down = jnp.concatenate(
        [
            jnp.transpose(jnp.broadcast_to(scale[:, j * HD : (j + 1) * HD], (HD, HD)))
            for j in range(4)
        ],
        axis=0,
    )
    values = jnp.dot(cells, wv_ref[...], preferred_element_type=F32) + rows_ref[0:1, 768:1152]
    for head in range(HEADS):
        lanes = slice(head * HD, (head + 1) * HD)
        value[head, pl.ds(start, OWN), :] = (
            values[:, lanes] * down + rows_ref[1:2, 768 + head * HD : 768 + (head + 1) * HD]
        ).astype(BF16)


def first_kernel(
    info_ref, q_hbm, a0, b0, a1, b1, a3, b3, a2, b2, wk_hbm, wv_hbm, rows_hbm, cols_hbm,
    o2, key_out, value_out, key_t, value, blocks, q2, wk_ref, wv_ref, rows_ref, cols_ref,
    sems,
):
    x_here, _, core = place_of(info_ref)
    weight_copies = fetch(
        (wk_hbm, wv_hbm, rows_hbm, cols_hbm), (wk_ref, wv_ref, rows_ref, cols_ref), sems
    )
    sources = (a0, b0, a1, b1, a3, b3, a2, b2)
    block_copies = fetch(sources, [blocks.at[i] for i in range(8)], sems, 4)
    (query_copy,) = fetch([q_hbm], [q2], sems, 12)
    for copy in weight_copies:
        copy.wait()
    for at in range(8):
        if at % 4 == 0:
            for copy in block_copies[at : at + 4]:
                copy.wait()
        source = lax.rem(x_here + (NX - (0, 1, 3, 2)[at // 2]), NX)
        core_at = core if at % 2 == 0 else 1 - core
        start = pl.multiple_of((source * 2 + core_at) * OWN, OWN)
        project_block(blocks.at[at], start, wk_ref, wv_ref, rows_ref, cols_ref, key_t, value)
    copies = fetch((key_t, value), (key_out, value_out), sems, 13)
    query_copy.wait()
    attend_group(info_ref, 2, q2, o2, key_t, value)
    for copy in copies:
        copy.wait()


PARTIAL = jax.ShapeDtypeStruct((HEADS * OWN + 128, HD), BF16)


def attend_first(info, query, near, far, wk, wv, rows, cols):
    return pl.pallas_call(
        first_kernel,
        in_specs=[SMEM] + [ANY] * 13,
        out_specs=[VMEM, ANY, ANY],
        out_shape=[
            PARTIAL,
            jax.ShapeDtypeStruct((HEADS, HD, KEYS), BF16),
            jax.ShapeDtypeStruct((HEADS, KEYS, HD), BF16),
        ],
        scratch_shapes=[
            pltpu.VMEM((HEADS, HD, KEYS), BF16),
            pltpu.VMEM((HEADS, KEYS, HD), BF16),
            pltpu.VMEM((8, OWN + 16, 512), BF16),
            pltpu.VMEM((HEADS, OWN, HD), BF16),
            pltpu.VMEM((384, 512), BF16),
            pltpu.VMEM((512, 384), BF16),
            pltpu.VMEM((8, 1152), F32),
            pltpu.VMEM((3, 384, HD), F32),
            pltpu.SemaphoreType.DMA((15,)),
        ],
        compiler_params=params(34),
        cost_estimate=pl.CostEstimate(
            flops=15000000000, bytes_accessed=10000000, transcendentals=0
        ),
    )(
        info,
        query,
        *[block for pair in zip(near, far) for block in pair],
        wk,
        wv,
        rows,
        cols,
    )


def next_kernel(groups, info_ref, key_t, value, *refs):
    count = len(groups)
    sources, refs = refs[:count], refs[-(count + 3) :]
    outs, queries, partial, sems = refs[:count], refs[count], refs[count + 1], refs[count + 2]
    for copy in fetch(sources, [queries.at[n] for n in range(count)], sems):
        copy.wait()

    def one_group(n, carry):
        group = groups[0] + n * 2
        attend_group(info_ref, group, queries.at[n], partial.at[n], key_t, value)
        return carry

    lax.fori_loop(0, count, one_group, 0)
    for copy in fetch([partial.at[n] for n in range(count)], outs, sems, count):
        copy.wait()


def attend_next(groups, info, queries, key_t, value, *needed):
    key_t, value = [
        pltpu.with_memory_space_constraint(array, pltpu.VMEM) for array in (key_t, value)
    ]
    return pl.pallas_call(
        functools.partial(next_kernel, groups),
        in_specs=[SMEM, VMEM, VMEM] + [ANY] * (len(groups) + len(needed)),
        out_specs=[ANY] * len(groups),
        out_shape=[PARTIAL] * len(groups),
        scratch_shapes=[
            pltpu.VMEM((len(groups), HEADS, OWN, HD), BF16),
            pltpu.VMEM((len(groups), *PARTIAL.shape), BF16),
            pltpu.SemaphoreType.DMA((2 * len(groups),)),
        ],
        compiler_params=params(28),
        cost_estimate=pl.CostEstimate(
            flops=8000000000 * len(groups), bytes_accessed=8000000, transcendentals=0
        ),
    )(info, key_t, value, *queries, *needed)


def merge_kernel(p0, p1, p2, p3, out_ref):
    parts = (p0, p1, p2, p3)
    for at in range(4):
        base = HEADS * OWN + at * 32
        levels = []
        for ref in parts:
            marks = ref[base : base + 32, :].astype(F32)
            levels.append(marks[0:8] + marks[8:16] + marks[16:24])
        top = functools.reduce(jnp.maximum, levels)
        shares = [jnp.exp2(level - top) for level in levels]
        weight_sum = functools.reduce(jnp.add, shares)
        stacked = jnp.concatenate([share / weight_sum for share in shares], axis=0)
        columns = jnp.transpose(
            jnp.concatenate([stacked, jnp.zeros((HD - 32, HD), F32)], axis=0)
        )
        for head in range(HEADS):
            rows = slice(head * OWN + at * HD, head * OWN + (at + 1) * HD)
            mixed = functools.reduce(
                jnp.add,
                [
                    ref[rows, :].astype(F32) * columns[:, i * 8 + head : i * 8 + head + 1]
                    for i, ref in enumerate(parts)
                ],
            )
            out_ref[head, at * HD : (at + 1) * HD, :] = mixed.astype(BF16)


def merge(parts):
    return pl.pallas_call(
        merge_kernel,
        in_specs=[VMEM] * 4,
        out_specs=VMEM,
        out_shape=jax.ShapeDtypeStruct((HEADS, OWN, HD), BF16),
        compiler_params=params(8),
    )(*in_vmem(*parts))


def per_device(
    section_in,
    norm_gain,
    conv_weight,
    conv_bias,
    lengths,
    embed_weight,
    embed_bias,
    mod_shift,
    mod_scale,
    qkv_weight,
    q_gain,
    k_gain,
):
    info = jnp.concatenate(
        [lengths, jnp.stack([lax.axis_index("tm"), lax.axis_index("band")])]
    ).astype(jnp.int32)
    above = halo(section_in[:, 7:8], 0, 1)
    below = halo(section_in[:, 0:1], 0, -1)
    cur = jnp.concatenate([above, section_in, below], axis=1)
    prev = halo(cur, 1, 0)
    qkv = jnp.transpose(qkv_weight, (1, 2, 0, 3)).reshape(9, 3072, HD)
    part, embed_near, qkv_near = conv_newest(cur, norm_gain, conv_weight, embed_weight, qkv)
    section_out, send = conv(
        info, cur, prev, part, norm_gain, conv_bias, embed_near, embed_bias, conv_weight
    )
    wq, wk, wv, rows, cols = fold(
        embed_near, embed_bias, mod_shift, mod_scale, k_gain, qkv_near
    )
    shards = (send, shift_band(send, 1), shift_band(send, 3), shift_band(send, 2))
    query, xr = queries_of(
        info, shards, wq, rows, q_gain
    )
    far_own = shift_tm(xr, swap=True)
    a1, a3 = shift_tm(xr, dx=1), shift_tm(xr, dx=3)
    q1, q3, q2 = shift_tm(query, dz=1), shift_tm(query, dz=3), shift_tm(query, dz=2)
    a2 = after(shift_tm(xr, dx=2), q1, q3, q2)
    near = (xr, a1, a3, a2)
    far = (far_own,) + tuple(shift_tm(part, swap=True) for part in near[1:])
    o2, key_t, value = attend_first(info, q2, near, far, wk, wv, rows, cols)
    p2 = shift_tm(o2, dz=2)
    o1, o3 = attend_next((1, 3), info, (q1, q3), key_t, value)
    p1, p3 = shift_tm(o1, dz=3), shift_tm(o3, dz=1)
    (o0,) = attend_next((0,), info, (query,), key_t, value, p2)
    parts = (o0, p1, p3, p2)
    attended = jnp.transpose(merge(parts), (1, 0, 2))
    return (section_out, attended)


def solution(mesh):
    return jax.shard_map(
        per_device,
        mesh=mesh,
        in_specs=(
            P("tm", "band", None, None),
            P(),
            P(),
            P(),
            P(),
            P(),
            P(),
            P(),
            P(),
            P(None, None, "band", None),
            P(),
            P(),
        ),
        out_specs=(P("tm", "band", None, None), P("tm", "band", None)),
        check_vma=False,
    )
```

```python
import functools

import jax
import jax.numpy as jnp
from jax import lax
from jax.experimental import pallas as pl
from jax.experimental.pallas import tpu as pltpu
from jax.sharding import PartitionSpec as P

EPSILON = 1e-06
NONE = -1e30
NX, NZ, NC, NB = 4, 4, 2, 4
HD = 128
FACTOR = 1.4426950408889634 / HD**0.5
HEADS = 3
SHARD = 128
FRAME = 256
OWN = 512
KEYS = 4096
F32 = jnp.float32
BF16 = jnp.bfloat16
MIB = 1024 * 1024


def params(mib):
    return pltpu.CompilerParams(vmem_limit_bytes=mib * MIB)


def fetch(sources, targets, sems, base=0):
    copies = [
        pltpu.make_async_copy(source, target, sems.at[base + at])
        for at, (source, target) in enumerate(zip(sources, targets))
    ]
    for copy in copies:
        copy.start()
    return copies


SMEM = pl.BlockSpec(memory_space=pltpu.SMEM)
VMEM = pl.BlockSpec(memory_space=pltpu.VMEM)
HBM = pl.BlockSpec(memory_space=pltpu.HBM)
ANY = pl.BlockSpec(memory_space=pl.ANY)


def pinned(*arrays):
    return [pltpu.with_memory_space_constraint(array, pltpu.HBM) for array in arrays]


def in_vmem(*arrays):
    return [pltpu.with_memory_space_constraint(array, pltpu.VMEM) for array in arrays]


def clip_of_frame(info_ref, frame):
    first, last, end = 0, 0, 0
    for clip in range(4):
        start, end = end, end + info_ref[clip]
        inside = (frame >= start) & (frame < end)
        first = jnp.where(inside, start, first)
        last = jnp.where(inside, end, last)
    return first, last


def place_of(info_ref):
    place = info_ref[4]
    return place // (NZ * NC), place // NC % NZ, place % NC


def split_bf16(value, count):
    parts = []
    for _ in range(count):
        part = value.astype(BF16).astype(F32)
        parts.append(part)
        value = value - part
    return parts


def after(array, *others):
    def kernel(source, *refs):
        (copy,) = fetch([source], [refs[-2]], refs[-1])
        copy.wait()

    return pl.pallas_call(
        kernel,
        in_specs=[ANY] * (1 + len(others)),
        out_specs=ANY,
        out_shape=jax.ShapeDtypeStruct(array.shape, array.dtype),
        scratch_shapes=[pltpu.SemaphoreType.DMA((1,))],
        compiler_params=params(2),
    )(array, *others)


def tm_index(x, z, c):
    return (x * NZ + z) * NC + c


def shift_tm(block, dx=0, dz=0, swap=False):
    route = []
    for x in range(NX):
        for z in range(NZ):
            for c in range(NC):
                target = tm_index((x + dx) % NX, (z + dz) % NZ, 1 - c if swap else c)
                route.append((tm_index(x, z, c), target))
    return lax.ppermute(block, "tm", route)


def shift_band(block, db):
    return lax.ppermute(block, "band", [(i, (i + db) % NB) for i in range(NB)])


def halo(block, dt, db):
    count = lax.axis_size("tm")
    route = []
    for t in range(count):
        for b in range(NB):
            if t + dt < count and 0 <= b + db < NB:
                route.append((t * NB + b, (t + dt) * NB + b + db))
    return lax.ppermute(block, ("tm", "band"), route)


def fold_kernel(
    embed_ref, bias_ref, shift_ref, scale_ref, gain_ref, qkv_ref, wq_ref, wk_ref, wv_ref, rows_ref, cols_ref,
    left,
):
    width = left.shape[1]
    gain = 1.0 + scale_ref[...]
    for lo in range(0, 512, 64):
        weight = embed_ref[lo : lo + 64, :].astype(F32)
        centred = weight - jnp.mean(weight, axis=-1, keepdims=True)
        left[lo : lo + 64, :] = (centred * gain).astype(BF16)
    bias = bias_ref[...]
    bias = (bias - jnp.mean(bias, axis=-1, keepdims=True)) * gain
    extra = jnp.zeros((16, width), F32)
    place = lax.broadcasted_iota(jnp.int32, (16, width), 0)
    for at, part in enumerate(split_bf16(bias, 3) + split_bf16(shift_ref[...], 3)):
        extra = jnp.where(place == at, part, extra)
    left[512:528, :] = extra.astype(BF16)
    where = lax.broadcasted_iota(jnp.int32, (8, HD), 0)
    cols_ref[2, 0:HD, :] = jnp.transpose(jnp.broadcast_to(gain_ref[...], (HD, HD)))
    for pair in ((0, 1), (2, 3), (4, 5), (6, 7), (8,)):
        right = jnp.concatenate([qkv_ref[i] for i in pair], axis=1)
        both = jnp.dot(left[...], right, preferred_element_type=F32)
        for at, block in enumerate(pair):
            part = both[:, at * HD : (at + 1) * HD]
            head = slice(block % HEADS * HD, (block % HEADS + 1) * HD)
            offset = part[512:513] + part[513:514] + part[514:515]
            moved = part[515:516] + part[516:517] + part[517:518]
            rows_ref[:, block * HD : (block + 1) * HD] = jnp.where(
                where == 0, offset, jnp.where(where == 1, moved, 0.0)
            )
            if block // HEADS == 0:
                wq_ref[:, head] = part[0:512].astype(BF16)
            elif block // HEADS == 1:
                wk_ref[head, :] = jnp.transpose(part[0:512]).astype(BF16)
                cols_ref[0, head, :] = jnp.transpose(jnp.broadcast_to(offset, (HD, HD)))
                cols_ref[1, head, :] = jnp.transpose(jnp.broadcast_to(moved, (HD, HD)))
            else:
                wv_ref[:, head] = part[0:512].astype(BF16)


def fold(embed_weight, embed_bias, mod_shift, mod_scale, k_gain, qkv):
    return pl.pallas_call(
        fold_kernel,
        in_specs=[VMEM] * 6,
        out_specs=[VMEM] * 5,
        out_shape=[
            jax.ShapeDtypeStruct((512, 384), BF16),
            jax.ShapeDtypeStruct((384, 512), BF16),
            jax.ShapeDtypeStruct((512, 384), BF16),
            jax.ShapeDtypeStruct((8, 1152), F32),
            jax.ShapeDtypeStruct((3, 384, HD), F32),
        ],
        scratch_shapes=[pltpu.VMEM((528, 3072), BF16)],
        compiler_params=params(16),
        cost_estimate=pl.CostEstimate(
            flops=2 * 528 * 3072 * 1152, bytes_accessed=12000000, transcendentals=0
        ),
    )(
        *in_vmem(embed_weight),
        embed_bias[None],
        mod_shift[None],
        mod_scale[None],
        k_gain[None],
        *in_vmem(qkv),
    )


def activate(cells, gain, act, slot, place):
    mean_square = jnp.mean(cells * cells, axis=-1, keepdims=True)
    scaled = cells * lax.rsqrt(mean_square + EPSILON) * gain
    active = (scaled * jax.nn.sigmoid(scaled)).astype(BF16).astype(F32)
    act[0, slot] = jnp.where(place == 0, 0.0, pltpu.roll(active, 1, 0))
    act[1, slot] = active
    act[2, slot] = jnp.where(place == 7, 0.0, pltpu.roll(active, 79, 0))


def newest_kernel(
    cur_ref, gain_hbm, weight_hbm, embed_hbm, qkv_hbm, part_ref, embed_out, qkv_out,
    act, gain_ref, weight_ref, sems,
):
    (gain_copy,) = fetch([gain_hbm], [gain_ref], sems)
    weight_copies = fetch(
        [weight_hbm.at[2, r] for r in range(3)], [weight_ref.at[r] for r in range(3)], sems, 1
    )
    copies = fetch((embed_hbm, qkv_hbm), (embed_out, qkv_out), sems, 4)
    place = lax.broadcasted_iota(jnp.int32, (80, 512), 0) % 8
    gain_copy.wait()
    for slot in range(2):
        activate(cur_ref[slot].astype(F32).reshape(80, 512), gain_ref[...], act, slot, place)
    total = jnp.zeros((SHARD, 512), F32)
    for tap_row in range(3):
        weight_copies[tap_row].wait()
        for tap_col in range(3):
            piece = jnp.concatenate(
                [act[tap_col, i, tap_row * 8 : tap_row * 8 + 64, :] for i in range(2)], axis=0
            ).astype(BF16)
            total = total + jnp.dot(
                piece, weight_ref[tap_row, tap_col], preferred_element_type=F32
            )
    part_ref[...] = total
    for copy in copies:
        copy.wait()


def conv_newest(cur, norm_gain, conv_weight, embed_weight, qkv):
    return pl.pallas_call(
        newest_kernel,
        in_specs=[VMEM] + [HBM] * 4,
        out_specs=[VMEM] + [ANY] * 2,
        out_shape=[
            jax.ShapeDtypeStruct((SHARD, 512), F32),
            jax.ShapeDtypeStruct(embed_weight.shape, BF16),
            jax.ShapeDtypeStruct(qkv.shape, BF16),
        ],
        scratch_shapes=[
            pltpu.VMEM((3, 2, 80, 512), F32),
            pltpu.VMEM((1, 512), F32),
            pltpu.VMEM((3, 3, 512, 512), BF16),
            pltpu.SemaphoreType.DMA((6,)),
        ],
        compiler_params=params(16),
        cost_estimate=pl.CostEstimate(
            flops=2 * 128 * 4608 * 512, bytes_accessed=15000000, transcendentals=0
        ),
    )(*in_vmem(cur), *pinned(norm_gain[None], conv_weight, embed_weight, qkv))


def conv_kernel(
    info_ref, cur_ref, prev_ref, part_ref, embed_ref, gain_hbm, bias_hbm, embed_bias_hbm, weight_hbm,
    out_ref, send_ref,
    act, gain_ref, bias_ref, embed_bias_ref, weight_ref, sems,
):
    copies = fetch(
        (gain_hbm, bias_hbm, embed_bias_hbm), (gain_ref, bias_ref, embed_bias_ref), sems
    )
    taps = [(t, r) for t in range(2) for r in range(3)]
    weight_copies = fetch(
        [weight_hbm.at[tap] for tap in taps], [weight_ref.at[tap] for tap in taps], sems, 3
    )
    first_frame = info_ref[4] * 2
    slots = []
    for i in range(2):
        clip_first, _ = clip_of_frame(info_ref, first_frame + i)
        slots.append(
            [jnp.maximum(first_frame + i - 2 + t, clip_first) - first_frame + 2 for t in range(2)]
        )
    place = lax.broadcasted_iota(jnp.int32, (80, 512), 0) % 8
    for copy in copies:
        copy.wait()
    for slot in range(4):
        cells = (prev_ref if slot < 2 else cur_ref)[slot % 2].astype(F32).reshape(80, 512)
        activate(cells, gain_ref[...], act, slot, place)
    inputs = jnp.concatenate(
        [cur_ref[i, 1:9].astype(F32).reshape(64, 512) for i in range(2)], axis=0
    )
    total = inputs + bias_ref[...] + part_ref[...]
    for at, (tap_time, tap_row) in enumerate(taps):
        weight_copies[at].wait()
        for tap_col in range(3):
            piece = jnp.concatenate(
                [
                    act[tap_col, slots[i][tap_time], tap_row * 8 : tap_row * 8 + 64, :]
                    for i in range(2)
                ],
                axis=0,
            ).astype(BF16)
            total = total + jnp.dot(
                piece, weight_ref[tap_time, tap_row, tap_col], preferred_element_type=F32
            )
    section = total.astype(BF16)
    out_ref[...] = section.reshape(out_ref.shape)
    send_ref[0:SHARD, :] = section
    embedded = jnp.dot(section, embed_ref[...], preferred_element_type=F32) + embed_bias_ref[...]
    center = embedded - jnp.mean(embedded, axis=-1, keepdims=True)
    spread = jnp.mean(center * center, axis=-1, keepdims=True)
    scale = lax.rsqrt(spread + EPSILON)
    across = jnp.transpose(jnp.broadcast_to(scale, (SHARD, SHARD)))[0:16]
    high, low = split_bf16(across, 2)
    tail = jnp.concatenate([high, low, jnp.zeros((16, 256), F32)], axis=1)
    place = lax.broadcasted_iota(jnp.int32, (16, 512), 0)
    send_ref[SHARD : SHARD + 16, :] = jnp.where(place == 0, tail, 0.0).astype(BF16)


def conv(info, cur, prev, part, norm_gain, conv_bias, embed_near, embed_bias, conv_weight):
    return pl.pallas_call(
        conv_kernel,
        in_specs=[SMEM] + [VMEM] * 4 + [HBM] * 4,
        out_specs=[VMEM] * 2,
        out_shape=[
            jax.ShapeDtypeStruct((2, 8, 8, 512), BF16),
            jax.ShapeDtypeStruct((SHARD + 16, 512), BF16),
        ],
        scratch_shapes=[
            pltpu.VMEM((3, 4, 80, 512), F32),
            pltpu.VMEM((1, 512), F32),
            pltpu.VMEM((1, 512), F32),
            pltpu.VMEM((1, 3072), F32),
            pltpu.VMEM((2, 3, 3, 512, 512), BF16),
            pltpu.SemaphoreType.DMA((9,)),
        ],
        compiler_params=params(24),
        cost_estimate=pl.CostEstimate(
            flops=2 * 128 * 13824 * 512, bytes_accessed=12000000, transcendentals=0
        ),
    )(
        info,
        *in_vmem(cur, prev, part, embed_near),
        *pinned(norm_gain[None], conv_bias[None], embed_bias[None], conv_weight),
    )


def normed(values, gain):
    mean_square = jnp.mean(values * values, axis=-1, keepdims=True)
    return (values * lax.rsqrt(mean_square + EPSILON) * gain).astype(BF16)


def gather_rows(shards, first_row, band, out_ref):
    across = []
    sources = []
    for back, ref in zip((0, 1, 3, 2), shards):
        source = lax.rem(band + (NB - back), NB)
        sources.append(source)
        across.append(ref[first_row + SHARD : first_row + SHARD + 16, :].astype(F32)[0:1])
        for i in range(2):
            rows = pl.ds(pl.multiple_of(i * FRAME + source * 64, 64), 64)
            out_ref[rows, :] = ref[first_row + i * 64 : first_row + (i + 1) * 64, :]
    lines = []
    for term in range(2):
        pieces = []
        for i in range(2):
            for b in range(NB):
                lanes = slice(term * HD + i * 64, term * HD + (i + 1) * 64)
                piece = across[0][:, lanes]
                for source, extra in zip(sources[1:], across[1:]):
                    piece = jnp.where(source == b, extra[:, lanes], piece)
                pieces.append(piece)
        lines.append(jnp.concatenate(pieces, axis=1))
    place = lax.broadcasted_iota(jnp.int32, (16, 512), 0)
    tail = jnp.where(place == 0, lines[0], jnp.where(place == 1, lines[1], 0.0))
    out_ref[OWN : OWN + 16, :] = tail.astype(BF16)
    return sources, across


def query_kernel(
    band_ref, s0, s1, s3, s2, x_near, x_far, weight_ref, rows_ref, gain_ref, q_ref, xr_ref, pair_ref
):
    shards = (s0, s1, s3, s2)
    pair_ref[0 : SHARD + 16, :] = x_near[...]
    pair_ref[SHARD + 16 : 2 * (SHARD + 16), :] = x_far[...]
    sources, across = gather_rows(shards, 0, band_ref[5], xr_ref)
    for ref, source, extra in zip(shards, sources, across):
        scale = jnp.transpose(jnp.broadcast_to(extra[:, 0:HD] + extra[:, HD : 2 * HD], (HD, HD)))
        projected = (
            jnp.dot(ref[0:SHARD, :], weight_ref[...], preferred_element_type=F32)
            + rows_ref[0:1, 0:384]
        )
        for head in range(HEADS):
            lanes = slice(head * HD, (head + 1) * HD)
            values = normed(projected[:, lanes] * scale + rows_ref[1:2, lanes], gain_ref[...])
            for i in range(2):
                rows = pl.ds(pl.multiple_of(i * FRAME + source * 64, 64), 64)
                q_ref[head, rows, :] = values[i * 64 : (i + 1) * 64]


def queries_of(info, shards, across, weight, rows, gain):
    return pl.pallas_call(
        query_kernel,
        in_specs=[SMEM] + [VMEM] * 9,
        out_specs=[VMEM] * 3,
        out_shape=[
            jax.ShapeDtypeStruct((HEADS, OWN, HD), BF16),
            jax.ShapeDtypeStruct((OWN + 16, 512), BF16),
            jax.ShapeDtypeStruct((2 * (SHARD + 16), 512), BF16),
        ],
        compiler_params=params(8),
        cost_estimate=pl.CostEstimate(
            flops=2 * 512 * 512 * 384, bytes_accessed=2000000, transcendentals=0
        ),
    )(info, *in_vmem(*shards, *across, weight, rows), gain[None] * FACTOR)


def store_rows(o_ref, base, results):
    lane = lax.broadcasted_iota(jnp.int32, (FRAME, HD), 1)
    marks = jnp.zeros((FRAME, HD), F32)
    for head, (mixed, peak, weight_sum) in enumerate(results):
        some = weight_sum > 0.0
        safe = jnp.where(some, weight_sum, 1.0)
        o_ref[pl.ds(pl.multiple_of(head * OWN + base, FRAME), FRAME), :] = (mixed / safe).astype(
            BF16
        )
        level = jnp.where(some, peak + jnp.log2(safe), NONE)
        marks = jnp.where(lane == head, level, marks)
    for half in range(2):
        turned = jnp.transpose(marks[half * HD : (half + 1) * HD])[0:8]
        first, second, third = split_bf16(turned, 3)
        at = pl.multiple_of(HEADS * OWN + (base // HD + half) * 32, 32)
        tail = jnp.concatenate([first, second, third, jnp.zeros((8, HD), F32)], axis=0)
        o_ref[pl.ds(at, 32), :] = tail.astype(BF16)


LONG = 12
SHORT = 4


def attend_group(info_ref, group, q_ref, o_ref, key_t, value):
    x_here, z_here, core = place_of(info_ref)
    group_frame = x_here * 16 + lax.rem(z_here + NZ - group, NZ) * 4 + core * 2

    def bounds(i):
        ends = []
        for edge in clip_of_frame(info_ref, group_frame + i):
            inside = [jnp.clip(edge - 16 * x - 4 * z_here, 0, 4) for x in range(NX)]
            ends.append(inside[0] + inside[1] + inside[2] + inside[3])
        return ends[0], ends[1] - ends[0]

    def rows_of(start, frames, base, shown=None):
        width = frames * FRAME
        start = pl.multiple_of(start * FRAME, FRAME)

        def scores_of(head):
            return jnp.dot(
                q_ref[head, pl.ds(base, FRAME), :],
                key_t[head, :, pl.ds(start, width)],
                preferred_element_type=F32,
            )

        scores = scores_of(0)
        results = []
        for head in range(HEADS):
            ahead = scores_of(head + 1) if head + 1 < HEADS else None
            if shown is not None:
                scores = jnp.where(shown, scores, NONE)
            top = jnp.max(scores, axis=-1, keepdims=True)
            weights = jnp.exp2(scores - top)
            if shown is not None:
                weights = jnp.where(shown, weights, 0.0)
            weight_sum = jnp.sum(weights, axis=-1, keepdims=True)
            mixed = jnp.dot(
                weights.astype(BF16),
                value[head, pl.ds(start, width), :],
                preferred_element_type=F32,
            )
            results.append((mixed, top, weight_sum))
            scores = ahead
        store_rows(o_ref, base, results)

    def one_frame(i, carry):
        first, count = bounds(i)
        base = pl.multiple_of(i * FRAME, FRAME)

        @pl.when(count == LONG)
        def _():
            rows_of(first, LONG, base)

        @pl.when(count != LONG)
        def _():
            start = jnp.minimum(first, KEYS // FRAME - SHORT)
            lane = lax.broadcasted_iota(jnp.int32, (FRAME, SHORT * FRAME), 1)
            low = (first - start) * FRAME
            rows_of(start, SHORT, base, (lane >= low) & (lane < low + count * FRAME))

        return carry

    lax.fori_loop(0, 2, one_frame, 0)


def project_block(ref, start, wk_ref, wv_ref, rows_ref, cols_ref, key_t, value):
    cells = ref[0:OWN, :]
    extra = ref[OWN : OWN + 16, :].astype(F32)
    scale = extra[0:1] + extra[1:2]
    keys = lax.dot_general(
        wk_ref[...], cells, (((1,), (1,)), ((), ())), preferred_element_type=F32
    )
    for head in range(HEADS):
        lanes = slice(head * HD, (head + 1) * HD)
        offset = jnp.concatenate([cols_ref[0, lanes, :]] * 4, axis=1)
        moved = jnp.concatenate([cols_ref[1, lanes, :]] * 4, axis=1)
        gain = jnp.concatenate([cols_ref[2, 0:HD, :]] * 4, axis=1)
        part = (keys[lanes] + offset) * scale + moved
        mean_square = jnp.mean(part * part, axis=0, keepdims=True)
        key_t[head, :, pl.ds(start, OWN)] = (
            part * lax.rsqrt(mean_square + EPSILON) * gain
        ).astype(BF16)
    down = jnp.concatenate(
        [
            jnp.transpose(jnp.broadcast_to(scale[:, j * HD : (j + 1) * HD], (HD, HD)))
            for j in range(4)
        ],
        axis=0,
    )
    values = jnp.dot(cells, wv_ref[...], preferred_element_type=F32) + rows_ref[0:1, 768:1152]
    for head in range(HEADS):
        lanes = slice(head * HD, (head + 1) * HD)
        value[head, pl.ds(start, OWN), :] = (
            values[:, lanes] * down + rows_ref[1:2, 768 + head * HD : 768 + (head + 1) * HD]
        ).astype(BF16)


def first_kernel(
    info_ref, q_hbm, a0, b0, a1, b1, a3, b3, g0, g1, g3, g2, wk_hbm, wv_hbm, rows_hbm, cols_hbm,
    o2, key_out, value_out, key_t, value, blocks, pairs, q2, wk_ref, wv_ref, rows_ref, cols_ref,
    sems,
):
    x_here, _, core = place_of(info_ref)
    weight_copies = fetch(
        (wk_hbm, wv_hbm, rows_hbm, cols_hbm), (wk_ref, wv_ref, rows_ref, cols_ref), sems
    )
    block_copies = fetch((a0, b0, a1, b1, a3, b3), [blocks.at[i] for i in range(6)], sems, 4)
    pair_copies = fetch((g0, g1, g3, g2), [pairs.at[i] for i in range(4)], sems, 10)
    (query_copy,) = fetch([q_hbm], [q2], sems, 14)
    for copy in weight_copies:
        copy.wait()
    for at in range(8):
        if at == 0:
            for copy in block_copies:
                copy.wait()
        if at == 4:
            for copy in pair_copies:
                copy.wait()
            for swap in range(2):
                gather_rows(
                    [pairs.at[i] for i in range(4)],
                    swap * (SHARD + 16),
                    info_ref[5],
                    blocks.at[6 + swap],
                )
        source = lax.rem(x_here + (NX - (0, 1, 3, 2)[at // 2]), NX)
        core_at = core if at % 2 == 0 else 1 - core
        start = pl.multiple_of((source * 2 + core_at) * OWN, OWN)
        project_block(blocks.at[at], start, wk_ref, wv_ref, rows_ref, cols_ref, key_t, value)
    copies = fetch((key_t, value), (key_out, value_out), sems, 15)
    query_copy.wait()
    attend_group(info_ref, 2, q2, o2, key_t, value)
    for copy in copies:
        copy.wait()


PARTIAL = jax.ShapeDtypeStruct((HEADS * OWN + 128, HD), BF16)


def attend_first(info, query, near, far, pairs, wk, wv, rows, cols):
    return pl.pallas_call(
        first_kernel,
        in_specs=[SMEM] + [ANY] * 15,
        out_specs=[VMEM, ANY, ANY],
        out_shape=[
            PARTIAL,
            jax.ShapeDtypeStruct((HEADS, HD, KEYS), BF16),
            jax.ShapeDtypeStruct((HEADS, KEYS, HD), BF16),
        ],
        scratch_shapes=[
            pltpu.VMEM((HEADS, HD, KEYS), BF16),
            pltpu.VMEM((HEADS, KEYS, HD), BF16),
            pltpu.VMEM((8, OWN + 16, 512), BF16),
            pltpu.VMEM((4, 2 * (SHARD + 16), 512), BF16),
            pltpu.VMEM((HEADS, OWN, HD), BF16),
            pltpu.VMEM((384, 512), BF16),
            pltpu.VMEM((512, 384), BF16),
            pltpu.VMEM((8, 1152), F32),
            pltpu.VMEM((3, 384, HD), F32),
            pltpu.SemaphoreType.DMA((17,)),
        ],
        compiler_params=params(34),
        cost_estimate=pl.CostEstimate(
            flops=15000000000, bytes_accessed=10000000, transcendentals=0
        ),
    )(
        info,
        query,
        *[block for pair in zip(near, far) for block in pair],
        *pairs,
        wk,
        wv,
        rows,
        cols,
    )


def next_kernel(groups, info_ref, key_t, value, *refs):
    count = len(groups)
    sources, refs = refs[:count], refs[-(count + 3) :]
    outs, queries, partial, sems = refs[:count], refs[count], refs[count + 1], refs[count + 2]
    for copy in fetch(sources, [queries.at[n] for n in range(count)], sems):
        copy.wait()

    def one_group(n, carry):
        group = groups[0] + n * 2
        attend_group(info_ref, group, queries.at[n], partial.at[n], key_t, value)
        return carry

    lax.fori_loop(0, count, one_group, 0)
    for copy in fetch([partial.at[n] for n in range(count)], outs, sems, count):
        copy.wait()


def attend_next(groups, info, queries, key_t, value, *needed):
    key_t, value = [
        pltpu.with_memory_space_constraint(array, pltpu.VMEM) for array in (key_t, value)
    ]
    return pl.pallas_call(
        functools.partial(next_kernel, groups),
        in_specs=[SMEM, VMEM, VMEM] + [ANY] * (len(groups) + len(needed)),
        out_specs=[ANY] * len(groups),
        out_shape=[PARTIAL] * len(groups),
        scratch_shapes=[
            pltpu.VMEM((len(groups), HEADS, OWN, HD), BF16),
            pltpu.VMEM((len(groups), *PARTIAL.shape), BF16),
            pltpu.SemaphoreType.DMA((2 * len(groups),)),
        ],
        compiler_params=params(28),
        cost_estimate=pl.CostEstimate(
            flops=8000000000 * len(groups), bytes_accessed=8000000, transcendentals=0
        ),
    )(info, key_t, value, *queries, *needed)


def merge_kernel(p0, p1, p2, p3, out_ref):
    parts = (p0, p1, p2, p3)
    for at in range(4):
        base = HEADS * OWN + at * 32
        levels = []
        for ref in parts:
            marks = ref[base : base + 32, :].astype(F32)
            levels.append(marks[0:8] + marks[8:16] + marks[16:24])
        top = functools.reduce(jnp.maximum, levels)
        shares = [jnp.exp2(level - top) for level in levels]
        weight_sum = functools.reduce(jnp.add, shares)
        stacked = jnp.concatenate([share / weight_sum for share in shares], axis=0)
        columns = jnp.transpose(
            jnp.concatenate([stacked, jnp.zeros((HD - 32, HD), F32)], axis=0)
        )
        for head in range(HEADS):
            rows = slice(head * OWN + at * HD, head * OWN + (at + 1) * HD)
            mixed = functools.reduce(
                jnp.add,
                [
                    ref[rows, :].astype(F32) * columns[:, i * 8 + head : i * 8 + head + 1]
                    for i, ref in enumerate(parts)
                ],
            )
            out_ref[head, at * HD : (at + 1) * HD, :] = mixed.astype(BF16)


def merge(parts):
    return pl.pallas_call(
        merge_kernel,
        in_specs=[VMEM] * 4,
        out_specs=VMEM,
        out_shape=jax.ShapeDtypeStruct((HEADS, OWN, HD), BF16),
        compiler_params=params(8),
    )(*in_vmem(*parts))


def per_device(
    section_in,
    norm_gain,
    conv_weight,
    conv_bias,
    lengths,
    embed_weight,
    embed_bias,
    mod_shift,
    mod_scale,
    qkv_weight,
    q_gain,
    k_gain,
):
    info = jnp.concatenate(
        [lengths, jnp.stack([lax.axis_index("tm"), lax.axis_index("band")])]
    ).astype(jnp.int32)
    above = halo(section_in[:, 7:8], 0, 1)
    below = halo(section_in[:, 0:1], 0, -1)
    cur = jnp.concatenate([above, section_in, below], axis=1)
    prev = halo(cur, 1, 0)
    qkv = jnp.transpose(qkv_weight, (1, 2, 0, 3)).reshape(9, 3072, HD)
    part, embed_near, qkv_near = conv_newest(cur, norm_gain, conv_weight, embed_weight, qkv)
    section_out, send = conv(
        info, cur, prev, part, norm_gain, conv_bias, embed_near, embed_bias, conv_weight
    )
    wq, wk, wv, rows, cols = fold(
        embed_near, embed_bias, mod_shift, mod_scale, k_gain, qkv_near
    )
    shards = (send, shift_band(send, 1), shift_band(send, 3), shift_band(send, 2))
    across = (shift_tm(send, dx=2), shift_tm(send, dx=2, swap=True))
    query, xr, pair = queries_of(info, shards, across, wq, rows, q_gain)
    far_own = shift_tm(xr, swap=True)
    q1, q3, q2 = shift_tm(query, dz=1), shift_tm(query, dz=3), shift_tm(query, dz=2)
    pairs = (pair, shift_band(pair, 1), shift_band(pair, 3), shift_band(pair, 2))
    a1 = after(shift_tm(xr, dx=1), q2, pairs[3])
    a3 = after(shift_tm(xr, dx=3), pairs[1], pairs[2])
    near = (xr, a1, a3)
    far = (far_own, shift_tm(a1, swap=True), shift_tm(a3, swap=True))
    o2, key_t, value = attend_first(info, q2, near, far, pairs, wk, wv, rows, cols)
    p2 = shift_tm(o2, dz=2)
    o1, o3 = attend_next((1, 3), info, (q1, q3), key_t, value)
    p1, p3 = shift_tm(o1, dz=3), shift_tm(o3, dz=1)
    (o0,) = attend_next((0,), info, (query,), key_t, value, p2)
    parts = (o0, p1, p3, p2)
    attended = jnp.transpose(merge(parts), (1, 0, 2))
    return (section_out, attended)


def solution(mesh):
    return jax.shard_map(
        per_device,
        mesh=mesh,
        in_specs=(
            P("tm", "band", None, None),
            P(),
            P(),
            P(),
            P(),
            P(),
            P(),
            P(),
            P(),
            P(None, None, "band", None),
            P(),
            P(),
        ),
        out_specs=(P("tm", "band", None, None), P("tm", "band", None)),
        check_vma=False,
    )
```

```python
import functools

import jax
import jax.numpy as jnp
from jax import lax
from jax.experimental import pallas as pl
from jax.experimental.pallas import tpu as pltpu
from jax.sharding import PartitionSpec as P

EPSILON = 1e-06
NONE = -1e30
NX, NZ, NC, NB = 4, 4, 2, 4
HD = 128
FACTOR = 1.4426950408889634 / HD**0.5
HEADS = 3
SHARD = 128
FRAME = 256
OWN = 512
KEYS = 4096
F32 = jnp.float32
BF16 = jnp.bfloat16
MIB = 1024 * 1024


def params(mib):
    return pltpu.CompilerParams(vmem_limit_bytes=mib * MIB)


def fetch(sources, targets, sems, base=0):
    copies = [
        pltpu.make_async_copy(source, target, sems.at[base + at])
        for at, (source, target) in enumerate(zip(sources, targets))
    ]
    for copy in copies:
        copy.start()
    return copies


SMEM = pl.BlockSpec(memory_space=pltpu.SMEM)
VMEM = pl.BlockSpec(memory_space=pltpu.VMEM)
HBM = pl.BlockSpec(memory_space=pltpu.HBM)
ANY = pl.BlockSpec(memory_space=pl.ANY)


def pinned(*arrays):
    return [pltpu.with_memory_space_constraint(array, pltpu.HBM) for array in arrays]


def in_vmem(*arrays):
    return [pltpu.with_memory_space_constraint(array, pltpu.VMEM) for array in arrays]


def clip_of_frame(info_ref, frame):
    first, last, end = 0, 0, 0
    for clip in range(4):
        start, end = end, end + info_ref[clip]
        inside = (frame >= start) & (frame < end)
        first = jnp.where(inside, start, first)
        last = jnp.where(inside, end, last)
    return first, last


def place_of(info_ref):
    place = info_ref[4]
    return place // (NZ * NC), place // NC % NZ, place % NC


def split_bf16(value, count):
    parts = []
    for _ in range(count):
        part = value.astype(BF16).astype(F32)
        parts.append(part)
        value = value - part
    return parts


def after(array, *others):
    def kernel(source, *refs):
        (copy,) = fetch([source], [refs[-2]], refs[-1])
        copy.wait()

    return pl.pallas_call(
        kernel,
        in_specs=[ANY] * (1 + len(others)),
        out_specs=ANY,
        out_shape=jax.ShapeDtypeStruct(array.shape, array.dtype),
        scratch_shapes=[pltpu.SemaphoreType.DMA((1,))],
        compiler_params=params(2),
    )(array, *others)


def tm_index(x, z, c):
    return (x * NZ + z) * NC + c


def shift_tm(block, dx=0, dz=0, swap=False):
    route = []
    for x in range(NX):
        for z in range(NZ):
            for c in range(NC):
                target = tm_index((x + dx) % NX, (z + dz) % NZ, 1 - c if swap else c)
                route.append((tm_index(x, z, c), target))
    return lax.ppermute(block, "tm", route)


def shift_band(block, db):
    return lax.ppermute(block, "band", [(i, (i + db) % NB) for i in range(NB)])


def halo(block, dt, db):
    count = lax.axis_size("tm")
    route = []
    for t in range(count):
        for b in range(NB):
            if t + dt < count and 0 <= b + db < NB:
                route.append((t * NB + b, (t + dt) * NB + b + db))
    return lax.ppermute(block, ("tm", "band"), route)


def fold_kernel(
    embed_ref, bias_ref, shift_ref, scale_ref, gain_ref, qkv_ref, wq_ref, wk_ref, wv_ref, rows_ref, cols_ref,
    left,
):
    width = left.shape[1]
    gain = 1.0 + scale_ref[...]
    for lo in range(0, 512, 64):
        weight = embed_ref[lo : lo + 64, :].astype(F32)
        centred = weight - jnp.mean(weight, axis=-1, keepdims=True)
        left[lo : lo + 64, :] = (centred * gain).astype(BF16)
    bias = bias_ref[...]
    bias = (bias - jnp.mean(bias, axis=-1, keepdims=True)) * gain
    extra = jnp.zeros((16, width), F32)
    place = lax.broadcasted_iota(jnp.int32, (16, width), 0)
    for at, part in enumerate(split_bf16(bias, 3) + split_bf16(shift_ref[...], 3)):
        extra = jnp.where(place == at, part, extra)
    left[512:528, :] = extra.astype(BF16)
    where = lax.broadcasted_iota(jnp.int32, (8, HD), 0)
    cols_ref[2, 0:HD, :] = jnp.transpose(jnp.broadcast_to(gain_ref[...], (HD, HD)))
    for pair in ((0, 1), (2, 3), (4, 5), (6, 7), (8,)):
        right = jnp.concatenate([qkv_ref[i] for i in pair], axis=1)
        both = jnp.dot(left[...], right, preferred_element_type=F32)
        for at, block in enumerate(pair):
            part = both[:, at * HD : (at + 1) * HD]
            head = slice(block % HEADS * HD, (block % HEADS + 1) * HD)
            offset = part[512:513] + part[513:514] + part[514:515]
            moved = part[515:516] + part[516:517] + part[517:518]
            rows_ref[:, block * HD : (block + 1) * HD] = jnp.where(
                where == 0, offset, jnp.where(where == 1, moved, 0.0)
            )
            if block // HEADS == 0:
                wq_ref[:, head] = part[0:512].astype(BF16)
            elif block // HEADS == 1:
                wk_ref[head, :] = jnp.transpose(part[0:512]).astype(BF16)
                cols_ref[0, head, :] = jnp.transpose(jnp.broadcast_to(offset, (HD, HD)))
                cols_ref[1, head, :] = jnp.transpose(jnp.broadcast_to(moved, (HD, HD)))
            else:
                wv_ref[:, head] = part[0:512].astype(BF16)


def fold(embed_weight, embed_bias, mod_shift, mod_scale, k_gain, qkv):
    return pl.pallas_call(
        fold_kernel,
        in_specs=[VMEM] * 6,
        out_specs=[VMEM] * 5,
        out_shape=[
            jax.ShapeDtypeStruct((512, 384), BF16),
            jax.ShapeDtypeStruct((384, 512), BF16),
            jax.ShapeDtypeStruct((512, 384), BF16),
            jax.ShapeDtypeStruct((8, 1152), F32),
            jax.ShapeDtypeStruct((3, 384, HD), F32),
        ],
        scratch_shapes=[pltpu.VMEM((528, 3072), BF16)],
        compiler_params=params(16),
        cost_estimate=pl.CostEstimate(
            flops=2 * 528 * 3072 * 1152, bytes_accessed=12000000, transcendentals=0
        ),
    )(
        *in_vmem(embed_weight),
        embed_bias[None],
        mod_shift[None],
        mod_scale[None],
        k_gain[None],
        *in_vmem(qkv),
    )


def activate(cells, gain, act, slot, place):
    mean_square = jnp.mean(cells * cells, axis=-1, keepdims=True)
    scaled = cells * lax.rsqrt(mean_square + EPSILON) * gain
    active = (scaled * jax.nn.sigmoid(scaled)).astype(BF16).astype(F32)
    act[0, slot] = jnp.where(place == 0, 0.0, pltpu.roll(active, 1, 0))
    act[1, slot] = active
    act[2, slot] = jnp.where(place == 7, 0.0, pltpu.roll(active, 79, 0))


def newest_kernel(
    cur_ref, gain_hbm, weight_hbm, embed_hbm, qkv_hbm, part_ref, embed_out, qkv_out,
    act, gain_ref, weight_ref, sems,
):
    (gain_copy,) = fetch([gain_hbm], [gain_ref], sems)
    weight_copies = fetch(
        [weight_hbm.at[2, r] for r in range(3)], [weight_ref.at[r] for r in range(3)], sems, 1
    )
    copies = fetch((embed_hbm, qkv_hbm), (embed_out, qkv_out), sems, 4)
    place = lax.broadcasted_iota(jnp.int32, (80, 512), 0) % 8
    gain_copy.wait()
    for slot in range(2):
        activate(cur_ref[slot].astype(F32).reshape(80, 512), gain_ref[...], act, slot, place)
    total = jnp.zeros((SHARD, 512), F32)
    for tap_row in range(3):
        weight_copies[tap_row].wait()
        for tap_col in range(3):
            piece = jnp.concatenate(
                [act[tap_col, i, tap_row * 8 : tap_row * 8 + 64, :] for i in range(2)], axis=0
            ).astype(BF16)
            total = total + jnp.dot(
                piece, weight_ref[tap_row, tap_col], preferred_element_type=F32
            )
    part_ref[...] = total
    for copy in copies:
        copy.wait()


def conv_newest(cur, norm_gain, conv_weight, embed_weight, qkv):
    return pl.pallas_call(
        newest_kernel,
        in_specs=[VMEM] + [HBM] * 4,
        out_specs=[VMEM] + [ANY] * 2,
        out_shape=[
            jax.ShapeDtypeStruct((SHARD, 512), F32),
            jax.ShapeDtypeStruct(embed_weight.shape, BF16),
            jax.ShapeDtypeStruct(qkv.shape, BF16),
        ],
        scratch_shapes=[
            pltpu.VMEM((3, 2, 80, 512), F32),
            pltpu.VMEM((1, 512), F32),
            pltpu.VMEM((3, 3, 512, 512), BF16),
            pltpu.SemaphoreType.DMA((6,)),
        ],
        compiler_params=params(16),
        cost_estimate=pl.CostEstimate(
            flops=2 * 128 * 4608 * 512, bytes_accessed=15000000, transcendentals=0
        ),
    )(*in_vmem(cur), *pinned(norm_gain[None], conv_weight, embed_weight, qkv))


def conv_kernel(
    info_ref, cur_ref, prev_ref, part_ref, embed_ref, gain_hbm, bias_hbm, embed_bias_hbm, weight_hbm,
    out_ref, send_ref,
    act, gain_ref, bias_ref, embed_bias_ref, weight_ref, sems,
):
    copies = fetch(
        (gain_hbm, bias_hbm, embed_bias_hbm), (gain_ref, bias_ref, embed_bias_ref), sems
    )
    taps = [(t, r) for t in range(2) for r in range(3)]
    weight_copies = fetch(
        [weight_hbm.at[tap] for tap in taps], [weight_ref.at[tap] for tap in taps], sems, 3
    )
    first_frame = info_ref[4] * 2
    slots = []
    for i in range(2):
        clip_first, _ = clip_of_frame(info_ref, first_frame + i)
        slots.append(
            [jnp.maximum(first_frame + i - 2 + t, clip_first) - first_frame + 2 for t in range(2)]
        )
    place = lax.broadcasted_iota(jnp.int32, (80, 512), 0) % 8
    for copy in copies:
        copy.wait()
    for slot in range(4):
        cells = (prev_ref if slot < 2 else cur_ref)[slot % 2].astype(F32).reshape(80, 512)
        activate(cells, gain_ref[...], act, slot, place)
    inputs = jnp.concatenate(
        [cur_ref[i, 1:9].astype(F32).reshape(64, 512) for i in range(2)], axis=0
    )
    total = inputs + bias_ref[...] + part_ref[...]
    for at, (tap_time, tap_row) in enumerate(taps):
        weight_copies[at].wait()
        for tap_col in range(3):
            piece = jnp.concatenate(
                [
                    act[tap_col, slots[i][tap_time], tap_row * 8 : tap_row * 8 + 64, :]
                    for i in range(2)
                ],
                axis=0,
            ).astype(BF16)
            total = total + jnp.dot(
                piece, weight_ref[tap_time, tap_row, tap_col], preferred_element_type=F32
            )
    section = total.astype(BF16)
    out_ref[...] = section.reshape(out_ref.shape)
    send_ref[0:SHARD, :] = section
    embedded = jnp.dot(section, embed_ref[...], preferred_element_type=F32) + embed_bias_ref[...]
    center = embedded - jnp.mean(embedded, axis=-1, keepdims=True)
    spread = jnp.mean(center * center, axis=-1, keepdims=True)
    scale = lax.rsqrt(spread + EPSILON)
    across = jnp.transpose(jnp.broadcast_to(scale, (SHARD, SHARD)))[0:16]
    high, low = split_bf16(across, 2)
    tail = jnp.concatenate([high, low, jnp.zeros((16, 256), F32)], axis=1)
    place = lax.broadcasted_iota(jnp.int32, (16, 512), 0)
    send_ref[SHARD : SHARD + 16, :] = jnp.where(place == 0, tail, 0.0).astype(BF16)


def conv(info, cur, prev, part, norm_gain, conv_bias, embed_near, embed_bias, conv_weight):
    return pl.pallas_call(
        conv_kernel,
        in_specs=[SMEM] + [VMEM] * 4 + [HBM] * 4,
        out_specs=[VMEM] * 2,
        out_shape=[
            jax.ShapeDtypeStruct((2, 8, 8, 512), BF16),
            jax.ShapeDtypeStruct((SHARD + 16, 512), BF16),
        ],
        scratch_shapes=[
            pltpu.VMEM((3, 4, 80, 512), F32),
            pltpu.VMEM((1, 512), F32),
            pltpu.VMEM((1, 512), F32),
            pltpu.VMEM((1, 3072), F32),
            pltpu.VMEM((2, 3, 3, 512, 512), BF16),
            pltpu.SemaphoreType.DMA((9,)),
        ],
        compiler_params=params(24),
        cost_estimate=pl.CostEstimate(
            flops=2 * 128 * 13824 * 512, bytes_accessed=12000000, transcendentals=0
        ),
    )(
        info,
        *in_vmem(cur, prev, part, embed_near),
        *pinned(norm_gain[None], conv_bias[None], embed_bias[None], conv_weight),
    )


def normed(values, gain):
    mean_square = jnp.mean(values * values, axis=-1, keepdims=True)
    return (values * lax.rsqrt(mean_square + EPSILON) * gain).astype(BF16)


def gather_rows(shards, first_row, band, out_ref):
    across = []
    sources = []
    for back, ref in zip((0, 1, 3, 2), shards):
        source = lax.rem(band + (NB - back), NB)
        sources.append(source)
        across.append(ref[first_row + SHARD : first_row + SHARD + 16, :].astype(F32)[0:1])
        for i in range(2):
            rows = pl.ds(pl.multiple_of(i * FRAME + source * 64, 64), 64)
            out_ref[rows, :] = ref[first_row + i * 64 : first_row + (i + 1) * 64, :]
    lines = []
    for term in range(2):
        pieces = []
        for i in range(2):
            for b in range(NB):
                lanes = slice(term * HD + i * 64, term * HD + (i + 1) * 64)
                piece = across[0][:, lanes]
                for source, extra in zip(sources[1:], across[1:]):
                    piece = jnp.where(source == b, extra[:, lanes], piece)
                pieces.append(piece)
        lines.append(jnp.concatenate(pieces, axis=1))
    place = lax.broadcasted_iota(jnp.int32, (16, 512), 0)
    tail = jnp.where(place == 0, lines[0], jnp.where(place == 1, lines[1], 0.0))
    out_ref[OWN : OWN + 16, :] = tail.astype(BF16)
    return sources, across


def query_kernel(
    band_ref, s0, s1, s3, s2, weight_ref, rows_ref, gain_ref, needed, q_ref, xr_ref
):
    shards = (s0, s1, s3, s2)
    sources, across = gather_rows(shards, 0, band_ref[5], xr_ref)
    for ref, source, extra in zip(shards, sources, across):
        scale = jnp.transpose(jnp.broadcast_to(extra[:, 0:HD] + extra[:, HD : 2 * HD], (HD, HD)))
        projected = (
            jnp.dot(ref[0:SHARD, :], weight_ref[...], preferred_element_type=F32)
            + rows_ref[0:1, 0:384]
        )
        for head in range(HEADS):
            lanes = slice(head * HD, (head + 1) * HD)
            values = normed(projected[:, lanes] * scale + rows_ref[1:2, lanes], gain_ref[...])
            for i in range(2):
                rows = pl.ds(pl.multiple_of(i * FRAME + source * 64, 64), 64)
                q_ref[head, rows, :] = values[i * 64 : (i + 1) * 64]


def queries_of(info, shards, weight, rows, gain, needed):
    return pl.pallas_call(
        query_kernel,
        in_specs=[SMEM] + [VMEM] * 7 + [ANY],
        out_specs=[VMEM] * 2,
        out_shape=[
            jax.ShapeDtypeStruct((HEADS, OWN, HD), BF16),
            jax.ShapeDtypeStruct((OWN + 16, 512), BF16),
        ],
        compiler_params=params(8),
        cost_estimate=pl.CostEstimate(
            flops=2 * 512 * 512 * 384, bytes_accessed=2000000, transcendentals=0
        ),
    )(info, *in_vmem(*shards, weight, rows), gain[None] * FACTOR, needed)


def assemble(info, shards):
    def kernel(info_ref, s0, s1, s3, s2, out_ref):
        gather_rows((s0, s1, s3, s2), 0, info_ref[5], out_ref)

    return pl.pallas_call(
        kernel,
        in_specs=[SMEM] + [VMEM] * 4,
        out_specs=VMEM,
        out_shape=jax.ShapeDtypeStruct((OWN + 16, 512), BF16),
        compiler_params=params(4),
    )(info, *in_vmem(*shards))


def store_rows(o_ref, base, results):
    lane = lax.broadcasted_iota(jnp.int32, (FRAME, HD), 1)
    marks = jnp.zeros((FRAME, HD), F32)
    for head, (mixed, peak, weight_sum) in enumerate(results):
        some = weight_sum > 0.0
        safe = jnp.where(some, weight_sum, 1.0)
        o_ref[pl.ds(pl.multiple_of(head * OWN + base, FRAME), FRAME), :] = (mixed / safe).astype(
            BF16
        )
        level = jnp.where(some, peak + jnp.log2(safe), NONE)
        marks = jnp.where(lane == head, level, marks)
    for half in range(2):
        turned = jnp.transpose(marks[half * HD : (half + 1) * HD])[0:8]
        first, second, third = split_bf16(turned, 3)
        at = pl.multiple_of(HEADS * OWN + (base // HD + half) * 32, 32)
        tail = jnp.concatenate([first, second, third, jnp.zeros((8, HD), F32)], axis=0)
        o_ref[pl.ds(at, 32), :] = tail.astype(BF16)


LONG = 12
SHORT = 4


def attend_group(info_ref, group, q_ref, o_ref, key_t, value):
    x_here, z_here, core = place_of(info_ref)
    group_frame = x_here * 16 + lax.rem(z_here + NZ - group, NZ) * 4 + core * 2

    def bounds(i):
        ends = []
        for edge in clip_of_frame(info_ref, group_frame + i):
            inside = [jnp.clip(edge - 16 * x - 4 * z_here, 0, 4) for x in range(NX)]
            ends.append(inside[0] + inside[1] + inside[2] + inside[3])
        return ends[0], ends[1] - ends[0]

    def rows_of(start, frames, base, shown=None):
        width = frames * FRAME
        start = pl.multiple_of(start * FRAME, FRAME)

        def scores_of(head):
            return jnp.dot(
                q_ref[head, pl.ds(base, FRAME), :],
                key_t[head, :, pl.ds(start, width)],
                preferred_element_type=F32,
            )

        scores = scores_of(0)
        results = []
        for head in range(HEADS):
            ahead = scores_of(head + 1) if head + 1 < HEADS else None
            if shown is not None:
                scores = jnp.where(shown, scores, NONE)
            top = jnp.max(scores, axis=-1, keepdims=True)
            weights = jnp.exp2(scores - top)
            if shown is not None:
                weights = jnp.where(shown, weights, 0.0)
            weight_sum = jnp.sum(weights, axis=-1, keepdims=True)
            mixed = jnp.dot(
                weights.astype(BF16),
                value[head, pl.ds(start, width), :],
                preferred_element_type=F32,
            )
            results.append((mixed, top, weight_sum))
            scores = ahead
        store_rows(o_ref, base, results)

    def one_frame(i, carry):
        first, count = bounds(i)
        base = pl.multiple_of(i * FRAME, FRAME)

        @pl.when(count == LONG)
        def _():
            rows_of(first, LONG, base)

        @pl.when(count != LONG)
        def _():
            start = jnp.minimum(first, KEYS // FRAME - SHORT)
            lane = lax.broadcasted_iota(jnp.int32, (FRAME, SHORT * FRAME), 1)
            low = (first - start) * FRAME
            rows_of(start, SHORT, base, (lane >= low) & (lane < low + count * FRAME))

        return carry

    lax.fori_loop(0, 2, one_frame, 0)


def project_block(ref, start, wk_ref, wv_ref, rows_ref, cols_ref, key_t, value):
    cells = ref[0:OWN, :]
    extra = ref[OWN : OWN + 16, :].astype(F32)
    scale = extra[0:1] + extra[1:2]
    keys = lax.dot_general(
        wk_ref[...], cells, (((1,), (1,)), ((), ())), preferred_element_type=F32
    )
    for head in range(HEADS):
        lanes = slice(head * HD, (head + 1) * HD)
        offset = jnp.concatenate([cols_ref[0, lanes, :]] * 4, axis=1)
        moved = jnp.concatenate([cols_ref[1, lanes, :]] * 4, axis=1)
        gain = jnp.concatenate([cols_ref[2, 0:HD, :]] * 4, axis=1)
        part = (keys[lanes] + offset) * scale + moved
        mean_square = jnp.mean(part * part, axis=0, keepdims=True)
        key_t[head, :, pl.ds(start, OWN)] = (
            part * lax.rsqrt(mean_square + EPSILON) * gain
        ).astype(BF16)
    down = jnp.concatenate(
        [
            jnp.transpose(jnp.broadcast_to(scale[:, j * HD : (j + 1) * HD], (HD, HD)))
            for j in range(4)
        ],
        axis=0,
    )
    values = jnp.dot(cells, wv_ref[...], preferred_element_type=F32) + rows_ref[0:1, 768:1152]
    for head in range(HEADS):
        lanes = slice(head * HD, (head + 1) * HD)
        value[head, pl.ds(start, OWN), :] = (
            values[:, lanes] * down + rows_ref[1:2, 768 + head * HD : 768 + (head + 1) * HD]
        ).astype(BF16)


def first_kernel(
    info_ref, q_hbm, a0, b0, a1, b1, a3, b3, a2, b2, wk_hbm, wv_hbm, rows_hbm, cols_hbm,
    o2, key_out, value_out, key_t, value, blocks, q2, wk_ref, wv_ref, rows_ref, cols_ref,
    sems,
):
    x_here, _, core = place_of(info_ref)
    weight_copies = fetch(
        (wk_hbm, wv_hbm, rows_hbm, cols_hbm), (wk_ref, wv_ref, rows_ref, cols_ref), sems
    )
    block_copies = fetch(
        (a0, b0, a1, b1, a3, b3, a2, b2), [blocks.at[i] for i in range(8)], sems, 4
    )
    (query_copy,) = fetch([q_hbm], [q2], sems, 12)
    for copy in weight_copies:
        copy.wait()
    for at in range(8):
        if at % 4 == 0:
            for copy in block_copies[at : at + 4]:
                copy.wait()
        source = lax.rem(x_here + (NX - (0, 1, 3, 2)[at // 2]), NX)
        core_at = core if at % 2 == 0 else 1 - core
        start = pl.multiple_of((source * 2 + core_at) * OWN, OWN)
        project_block(blocks.at[at], start, wk_ref, wv_ref, rows_ref, cols_ref, key_t, value)
    copies = fetch((key_t, value), (key_out, value_out), sems, 13)
    query_copy.wait()
    attend_group(info_ref, 2, q2, o2, key_t, value)
    for copy in copies:
        copy.wait()


PARTIAL = jax.ShapeDtypeStruct((HEADS * OWN + 128, HD), BF16)


def attend_first(info, query, near, far, wk, wv, rows, cols):
    return pl.pallas_call(
        first_kernel,
        in_specs=[SMEM] + [ANY] * 13,
        out_specs=[VMEM, ANY, ANY],
        out_shape=[
            PARTIAL,
            jax.ShapeDtypeStruct((HEADS, HD, KEYS), BF16),
            jax.ShapeDtypeStruct((HEADS, KEYS, HD), BF16),
        ],
        scratch_shapes=[
            pltpu.VMEM((HEADS, HD, KEYS), BF16),
            pltpu.VMEM((HEADS, KEYS, HD), BF16),
            pltpu.VMEM((8, OWN + 16, 512), BF16),
            pltpu.VMEM((HEADS, OWN, HD), BF16),
            pltpu.VMEM((384, 512), BF16),
            pltpu.VMEM((512, 384), BF16),
            pltpu.VMEM((8, 1152), F32),
            pltpu.VMEM((3, 384, HD), F32),
            pltpu.SemaphoreType.DMA((15,)),
        ],
        compiler_params=params(34),
        cost_estimate=pl.CostEstimate(
            flops=15000000000, bytes_accessed=10000000, transcendentals=0
        ),
    )(
        info,
        query,
        *[block for pair in zip(near, far) for block in pair],
        wk,
        wv,
        rows,
        cols,
    )


def next_kernel(groups, info_ref, key_t, value, *refs):
    count = len(groups)
    sources, refs = refs[:count], refs[-(count + 3) :]
    outs, queries, partial, sems = refs[:count], refs[count], refs[count + 1], refs[count + 2]
    for copy in fetch(sources, [queries.at[n] for n in range(count)], sems):
        copy.wait()

    def one_group(n, carry):
        group = groups[0] + n * 2
        attend_group(info_ref, group, queries.at[n], partial.at[n], key_t, value)
        return carry

    lax.fori_loop(0, count, one_group, 0)
    for copy in fetch([partial.at[n] for n in range(count)], outs, sems, count):
        copy.wait()


def attend_next(groups, info, queries, key_t, value, *needed):
    key_t, value = [
        pltpu.with_memory_space_constraint(array, pltpu.VMEM) for array in (key_t, value)
    ]
    return pl.pallas_call(
        functools.partial(next_kernel, groups),
        in_specs=[SMEM, VMEM, VMEM] + [ANY] * (len(groups) + len(needed)),
        out_specs=[ANY] * len(groups),
        out_shape=[PARTIAL] * len(groups),
        scratch_shapes=[
            pltpu.VMEM((len(groups), HEADS, OWN, HD), BF16),
            pltpu.VMEM((len(groups), *PARTIAL.shape), BF16),
            pltpu.SemaphoreType.DMA((2 * len(groups),)),
        ],
        compiler_params=params(28),
        cost_estimate=pl.CostEstimate(
            flops=8000000000 * len(groups), bytes_accessed=8000000, transcendentals=0
        ),
    )(info, key_t, value, *queries, *needed)


def merge_kernel(p0, p1, p2, p3, out_ref):
    parts = (p0, p1, p2, p3)
    for at in range(4):
        base = HEADS * OWN + at * 32
        levels = []
        for ref in parts:
            marks = ref[base : base + 32, :].astype(F32)
            levels.append(marks[0:8] + marks[8:16] + marks[16:24])
        top = functools.reduce(jnp.maximum, levels)
        shares = [jnp.exp2(level - top) for level in levels]
        weight_sum = functools.reduce(jnp.add, shares)
        stacked = jnp.concatenate([share / weight_sum for share in shares], axis=0)
        columns = jnp.transpose(
            jnp.concatenate([stacked, jnp.zeros((HD - 32, HD), F32)], axis=0)
        )
        for head in range(HEADS):
            rows = slice(head * OWN + at * HD, head * OWN + (at + 1) * HD)
            mixed = functools.reduce(
                jnp.add,
                [
                    ref[rows, :].astype(F32) * columns[:, i * 8 + head : i * 8 + head + 1]
                    for i, ref in enumerate(parts)
                ],
            )
            out_ref[head, at * HD : (at + 1) * HD, :] = mixed.astype(BF16)


def merge(parts):
    return pl.pallas_call(
        merge_kernel,
        in_specs=[VMEM] * 4,
        out_specs=VMEM,
        out_shape=jax.ShapeDtypeStruct((HEADS, OWN, HD), BF16),
        compiler_params=params(8),
    )(*in_vmem(*parts))


def per_device(
    section_in,
    norm_gain,
    conv_weight,
    conv_bias,
    lengths,
    embed_weight,
    embed_bias,
    mod_shift,
    mod_scale,
    qkv_weight,
    q_gain,
    k_gain,
):
    info = jnp.concatenate(
        [lengths, jnp.stack([lax.axis_index("tm"), lax.axis_index("band")])]
    ).astype(jnp.int32)
    above = halo(section_in[:, 7:8], 0, 1)
    below = halo(section_in[:, 0:1], 0, -1)
    cur = jnp.concatenate([above, section_in, below], axis=1)
    prev = halo(cur, 1, 0)
    qkv = jnp.transpose(qkv_weight, (1, 2, 0, 3)).reshape(9, 3072, HD)
    part, embed_near, qkv_near = conv_newest(cur, norm_gain, conv_weight, embed_weight, qkv)
    section_out, send = conv(
        info, cur, prev, part, norm_gain, conv_bias, embed_near, embed_bias, conv_weight
    )
    wq, wk, wv, rows, cols = fold(
        embed_near, embed_bias, mod_shift, mod_scale, k_gain, qkv_near
    )
    shards = (send, shift_band(send, 1), shift_band(send, 3), shift_band(send, 2))
    across = shift_tm(send, dx=2)
    query, xr = queries_of(info, shards, wq, rows, q_gain, across)
    far_own = shift_tm(xr, swap=True)
    q1, q3, q2 = shift_tm(query, dz=1), shift_tm(query, dz=3), shift_tm(query, dz=2)
    g1, g3, g2 = shift_band(across, 1), shift_band(across, 3), shift_band(across, 2)
    a1 = after(shift_tm(xr, dx=1), q2, g2)
    a3 = after(shift_tm(xr, dx=3), g1, g3)
    a2 = assemble(info, (across, g1, g3, g2))
    near = (xr, a1, a3, a2)
    far = (far_own,) + tuple(shift_tm(part, swap=True) for part in near[1:])
    o2, key_t, value = attend_first(info, q2, near, far, wk, wv, rows, cols)
    p2 = shift_tm(o2, dz=2)
    o1, o3 = attend_next((1, 3), info, (q1, q3), key_t, value)
    p1, p3 = shift_tm(o1, dz=3), shift_tm(o3, dz=1)
    (o0,) = attend_next((0,), info, (query,), key_t, value, p2)
    parts = (o0, p1, p3, p2)
    attended = jnp.transpose(merge(parts), (1, 0, 2))
    return (section_out, attended)


def solution(mesh):
    return jax.shard_map(
        per_device,
        mesh=mesh,
        in_specs=(
            P("tm", "band", None, None),
            P(),
            P(),
            P(),
            P(),
            P(),
            P(),
            P(),
            P(),
            P(None, None, "band", None),
            P(),
            P(),
        ),
        out_specs=(P("tm", "band", None, None), P("tm", "band", None)),
        check_vma=False,
    )
```

```python
import functools

import jax
import jax.numpy as jnp
from jax import lax
from jax.experimental import pallas as pl
from jax.experimental.pallas import tpu as pltpu
from jax.sharding import PartitionSpec as P

EPSILON = 1e-06
NONE = -1e30
NX, NZ, NC, NB = 4, 4, 2, 4
HD = 128
FACTOR = 1.4426950408889634 / HD**0.5
HEADS = 3
SHARD = 128
FRAME = 256
OWN = 512
KEYS = 4096
F32 = jnp.float32
BF16 = jnp.bfloat16
MIB = 1024 * 1024


def params(mib):
    return pltpu.CompilerParams(vmem_limit_bytes=mib * MIB)


def fetch(sources, targets, sems, base=0):
    copies = [
        pltpu.make_async_copy(source, target, sems.at[base + at])
        for at, (source, target) in enumerate(zip(sources, targets))
    ]
    for copy in copies:
        copy.start()
    return copies


SMEM = pl.BlockSpec(memory_space=pltpu.SMEM)
VMEM = pl.BlockSpec(memory_space=pltpu.VMEM)
HBM = pl.BlockSpec(memory_space=pltpu.HBM)
ANY = pl.BlockSpec(memory_space=pl.ANY)


def pinned(*arrays):
    return [pltpu.with_memory_space_constraint(array, pltpu.HBM) for array in arrays]


def in_vmem(*arrays):
    return [pltpu.with_memory_space_constraint(array, pltpu.VMEM) for array in arrays]


def clip_of_frame(info_ref, frame):
    first, last, end = 0, 0, 0
    for clip in range(4):
        start, end = end, end + info_ref[clip]
        inside = (frame >= start) & (frame < end)
        first = jnp.where(inside, start, first)
        last = jnp.where(inside, end, last)
    return first, last


def place_of(info_ref):
    place = info_ref[4]
    return place // (NZ * NC), place // NC % NZ, place % NC


def split_bf16(value, count):
    parts = []
    for _ in range(count):
        part = value.astype(BF16).astype(F32)
        parts.append(part)
        value = value - part
    return parts


def after(array, *others):
    def kernel(source, *refs):
        (copy,) = fetch([source], [refs[-2]], refs[-1])
        copy.wait()

    return pl.pallas_call(
        kernel,
        in_specs=[ANY] * (1 + len(others)),
        out_specs=ANY,
        out_shape=jax.ShapeDtypeStruct(array.shape, array.dtype),
        scratch_shapes=[pltpu.SemaphoreType.DMA((1,))],
        compiler_params=params(2),
    )(array, *others)


def tm_index(x, z, c):
    return (x * NZ + z) * NC + c


def shift_tm(block, dx=0, dz=0, swap=False):
    route = []
    for x in range(NX):
        for z in range(NZ):
            for c in range(NC):
                target = tm_index((x + dx) % NX, (z + dz) % NZ, 1 - c if swap else c)
                route.append((tm_index(x, z, c), target))
    return lax.ppermute(block, "tm", route)


def shift_band(block, db):
    return lax.ppermute(block, "band", [(i, (i + db) % NB) for i in range(NB)])


def halo(block, dt, db):
    count = lax.axis_size("tm")
    route = []
    for t in range(count):
        for b in range(NB):
            if t + dt < count and 0 <= b + db < NB:
                route.append((t * NB + b, (t + dt) * NB + b + db))
    return lax.ppermute(block, ("tm", "band"), route)


def fold_kernel(
    embed_ref, bias_ref, shift_ref, scale_ref, gain_ref, qkv_ref, wq_ref, wk_ref, wv_ref, rows_ref, cols_ref,
    left,
):
    width = left.shape[1]
    gain = 1.0 + scale_ref[...]
    for lo in range(0, 512, 64):
        weight = embed_ref[lo : lo + 64, :].astype(F32)
        centred = weight - jnp.mean(weight, axis=-1, keepdims=True)
        left[lo : lo + 64, :] = (centred * gain).astype(BF16)
    bias = bias_ref[...]
    bias = (bias - jnp.mean(bias, axis=-1, keepdims=True)) * gain
    extra = jnp.zeros((16, width), F32)
    place = lax.broadcasted_iota(jnp.int32, (16, width), 0)
    for at, part in enumerate(split_bf16(bias, 3) + split_bf16(shift_ref[...], 3)):
        extra = jnp.where(place == at, part, extra)
    left[512:528, :] = extra.astype(BF16)
    where = lax.broadcasted_iota(jnp.int32, (8, HD), 0)
    cols_ref[2, 0:HD, :] = jnp.transpose(jnp.broadcast_to(gain_ref[...], (HD, HD)))
    for pair in ((0, 1), (2, 3), (4, 5), (6, 7), (8,)):
        right = jnp.concatenate([qkv_ref[i] for i in pair], axis=1)
        both = jnp.dot(left[...], right, preferred_element_type=F32)
        for at, block in enumerate(pair):
            part = both[:, at * HD : (at + 1) * HD]
            head = slice(block % HEADS * HD, (block % HEADS + 1) * HD)
            offset = part[512:513] + part[513:514] + part[514:515]
            moved = part[515:516] + part[516:517] + part[517:518]
            rows_ref[:, block * HD : (block + 1) * HD] = jnp.where(
                where == 0, offset, jnp.where(where == 1, moved, 0.0)
            )
            if block // HEADS == 0:
                wq_ref[:, head] = part[0:512].astype(BF16)
            elif block // HEADS == 1:
                wk_ref[head, :] = jnp.transpose(part[0:512]).astype(BF16)
                cols_ref[0, head, :] = jnp.transpose(jnp.broadcast_to(offset, (HD, HD)))
                cols_ref[1, head, :] = jnp.transpose(jnp.broadcast_to(moved, (HD, HD)))
            else:
                wv_ref[:, head] = part[0:512].astype(BF16)


def fold(embed_weight, embed_bias, mod_shift, mod_scale, k_gain, qkv):
    return pl.pallas_call(
        fold_kernel,
        in_specs=[VMEM] * 6,
        out_specs=[VMEM] * 5,
        out_shape=[
            jax.ShapeDtypeStruct((512, 384), BF16),
            jax.ShapeDtypeStruct((384, 512), BF16),
            jax.ShapeDtypeStruct((512, 384), BF16),
            jax.ShapeDtypeStruct((8, 1152), F32),
            jax.ShapeDtypeStruct((3, 384, HD), F32),
        ],
        scratch_shapes=[pltpu.VMEM((528, 3072), BF16)],
        compiler_params=params(16),
        cost_estimate=pl.CostEstimate(
            flops=2 * 528 * 3072 * 1152, bytes_accessed=12000000, transcendentals=0
        ),
    )(
        *in_vmem(embed_weight),
        embed_bias[None],
        mod_shift[None],
        mod_scale[None],
        k_gain[None],
        *in_vmem(qkv),
    )


def activate(cells, gain, act, slot, place):
    mean_square = jnp.mean(cells * cells, axis=-1, keepdims=True)
    scaled = cells * lax.rsqrt(mean_square + EPSILON) * gain
    active = (scaled * jax.nn.sigmoid(scaled)).astype(BF16).astype(F32)
    act[0, slot] = jnp.where(place == 0, 0.0, pltpu.roll(active, 1, 0))
    act[1, slot] = active
    act[2, slot] = jnp.where(place == 7, 0.0, pltpu.roll(active, 79, 0))


def newest_kernel(
    cur_ref, gain_hbm, weight_hbm, qkv_hbm, part_ref, qkv_out,
    act, gain_ref, weight_ref, sems,
):
    (gain_copy,) = fetch([gain_hbm], [gain_ref], sems)
    weight_copies = fetch(
        [weight_hbm.at[2, r] for r in range(3)], [weight_ref.at[r] for r in range(3)], sems, 1
    )
    copies = fetch([qkv_hbm], [qkv_out], sems, 4)
    place = lax.broadcasted_iota(jnp.int32, (80, 512), 0) % 8
    gain_copy.wait()
    for slot in range(2):
        activate(cur_ref[slot].astype(F32).reshape(80, 512), gain_ref[...], act, slot, place)
    total = jnp.zeros((SHARD, 512), F32)
    for tap_row in range(3):
        weight_copies[tap_row].wait()
        for tap_col in range(3):
            piece = jnp.concatenate(
                [act[tap_col, i, tap_row * 8 : tap_row * 8 + 64, :] for i in range(2)], axis=0
            ).astype(BF16)
            total = total + jnp.dot(
                piece, weight_ref[tap_row, tap_col], preferred_element_type=F32
            )
    part_ref[...] = total
    for copy in copies:
        copy.wait()


def conv_newest(cur, norm_gain, conv_weight, qkv):
    return pl.pallas_call(
        newest_kernel,
        in_specs=[VMEM] + [HBM] * 3,
        out_specs=[VMEM, ANY],
        out_shape=[
            jax.ShapeDtypeStruct((SHARD, 512), F32),
            jax.ShapeDtypeStruct(qkv.shape, BF16),
        ],
        scratch_shapes=[
            pltpu.VMEM((3, 2, 80, 512), F32),
            pltpu.VMEM((1, 512), F32),
            pltpu.VMEM((3, 3, 512, 512), BF16),
            pltpu.SemaphoreType.DMA((5,)),
        ],
        compiler_params=params(16),
        cost_estimate=pl.CostEstimate(
            flops=2 * 128 * 4608 * 512, bytes_accessed=15000000, transcendentals=0
        ),
    )(*in_vmem(cur), *pinned(norm_gain[None], conv_weight, qkv))


def conv_kernel(
    info_ref, cur_ref, prev_ref, part_ref, gain_hbm, bias_hbm, embed_bias_hbm, weight_hbm, embed_hbm,
    out_ref, send_ref, embed_out,
    embed_ref, act, gain_ref, bias_ref, embed_bias_ref, weight_ref, sems,
):
    copies = fetch(
        (gain_hbm, bias_hbm, embed_bias_hbm), (gain_ref, bias_ref, embed_bias_ref), sems
    )
    taps = [(t, r) for t in range(2) for r in range(3)]
    weight_copies = fetch(
        [weight_hbm.at[tap] for tap in taps], [weight_ref.at[tap] for tap in taps], sems, 3
    )
    (embed_copy,) = fetch([embed_hbm], [embed_ref], sems, 9)
    first_frame = info_ref[4] * 2
    slots = []
    for i in range(2):
        clip_first, _ = clip_of_frame(info_ref, first_frame + i)
        slots.append(
            [jnp.maximum(first_frame + i - 2 + t, clip_first) - first_frame + 2 for t in range(2)]
        )
    place = lax.broadcasted_iota(jnp.int32, (80, 512), 0) % 8
    for copy in copies:
        copy.wait()
    for slot in range(4):
        cells = (prev_ref if slot < 2 else cur_ref)[slot % 2].astype(F32).reshape(80, 512)
        activate(cells, gain_ref[...], act, slot, place)
    inputs = jnp.concatenate(
        [cur_ref[i, 1:9].astype(F32).reshape(64, 512) for i in range(2)], axis=0
    )
    total = inputs + bias_ref[...] + part_ref[...]
    for at, (tap_time, tap_row) in enumerate(taps):
        weight_copies[at].wait()
        for tap_col in range(3):
            piece = jnp.concatenate(
                [
                    act[tap_col, slots[i][tap_time], tap_row * 8 : tap_row * 8 + 64, :]
                    for i in range(2)
                ],
                axis=0,
            ).astype(BF16)
            total = total + jnp.dot(
                piece, weight_ref[tap_time, tap_row, tap_col], preferred_element_type=F32
            )
    section = total.astype(BF16)
    embed_copy.wait()
    (embed_sent,) = fetch([embed_ref], [embed_out], sems, 10)
    out_ref[...] = section.reshape(out_ref.shape)
    send_ref[0:SHARD, :] = section
    embedded = jnp.dot(section, embed_ref[...], preferred_element_type=F32) + embed_bias_ref[...]
    center = embedded - jnp.mean(embedded, axis=-1, keepdims=True)
    spread = jnp.mean(center * center, axis=-1, keepdims=True)
    scale = lax.rsqrt(spread + EPSILON)
    across = jnp.transpose(jnp.broadcast_to(scale, (SHARD, SHARD)))[0:16]
    high, low = split_bf16(across, 2)
    tail = jnp.concatenate([high, low, jnp.zeros((16, 256), F32)], axis=1)
    place = lax.broadcasted_iota(jnp.int32, (16, 512), 0)
    send_ref[SHARD : SHARD + 16, :] = jnp.where(place == 0, tail, 0.0).astype(BF16)
    embed_sent.wait()


def conv(info, cur, prev, part, norm_gain, conv_bias, embed_weight, embed_bias, conv_weight):
    return pl.pallas_call(
        conv_kernel,
        in_specs=[SMEM] + [VMEM] * 3 + [HBM] * 5,
        out_specs=[VMEM] * 2 + [ANY],
        out_shape=[
            jax.ShapeDtypeStruct((2, 8, 8, 512), BF16),
            jax.ShapeDtypeStruct((SHARD + 16, 512), BF16),
            jax.ShapeDtypeStruct(embed_weight.shape, BF16),
        ],
        scratch_shapes=[
            pltpu.VMEM(embed_weight.shape, BF16),
            pltpu.VMEM((3, 4, 80, 512), F32),
            pltpu.VMEM((1, 512), F32),
            pltpu.VMEM((1, 512), F32),
            pltpu.VMEM((1, 3072), F32),
            pltpu.VMEM((2, 3, 3, 512, 512), BF16),
            pltpu.SemaphoreType.DMA((11,)),
        ],
        compiler_params=params(28),
        cost_estimate=pl.CostEstimate(
            flops=2 * 128 * 13824 * 512, bytes_accessed=12000000, transcendentals=0
        ),
    )(
        info,
        *in_vmem(cur, prev, part),
        *pinned(norm_gain[None], conv_bias[None], embed_bias[None], conv_weight, embed_weight),
    )


def normed(values, gain):
    mean_square = jnp.mean(values * values, axis=-1, keepdims=True)
    return (values * lax.rsqrt(mean_square + EPSILON) * gain).astype(BF16)


def gather_rows(shards, first_row, band, out_ref):
    across = []
    sources = []
    for back, ref in zip((0, 1, 3, 2), shards):
        source = lax.rem(band + (NB - back), NB)
        sources.append(source)
        across.append(ref[first_row + SHARD : first_row + SHARD + 16, :].astype(F32)[0:1])
        for i in range(2):
            rows = pl.ds(pl.multiple_of(i * FRAME + source * 64, 64), 64)
            out_ref[rows, :] = ref[first_row + i * 64 : first_row + (i + 1) * 64, :]
    lines = []
    for term in range(2):
        pieces = []
        for i in range(2):
            for b in range(NB):
                lanes = slice(term * HD + i * 64, term * HD + (i + 1) * 64)
                piece = across[0][:, lanes]
                for source, extra in zip(sources[1:], across[1:]):
                    piece = jnp.where(source == b, extra[:, lanes], piece)
                pieces.append(piece)
        lines.append(jnp.concatenate(pieces, axis=1))
    place = lax.broadcasted_iota(jnp.int32, (16, 512), 0)
    tail = jnp.where(place == 0, lines[0], jnp.where(place == 1, lines[1], 0.0))
    out_ref[OWN : OWN + 16, :] = tail.astype(BF16)
    return sources, across


def query_kernel(
    band_ref, s0, s1, s3, s2, weight_ref, rows_ref, gain_ref, needed, q_ref, xr_ref
):
    shards = (s0, s1, s3, s2)
    sources, across = gather_rows(shards, 0, band_ref[5], xr_ref)
    for ref, source, extra in zip(shards, sources, across):
        scale = jnp.transpose(jnp.broadcast_to(extra[:, 0:HD] + extra[:, HD : 2 * HD], (HD, HD)))
        projected = (
            jnp.dot(ref[0:SHARD, :], weight_ref[...], preferred_element_type=F32)
            + rows_ref[0:1, 0:384]
        )
        for head in range(HEADS):
            lanes = slice(head * HD, (head + 1) * HD)
            values = normed(projected[:, lanes] * scale + rows_ref[1:2, lanes], gain_ref[...])
            for i in range(2):
                rows = pl.ds(pl.multiple_of(i * FRAME + source * 64, 64), 64)
                q_ref[head, rows, :] = values[i * 64 : (i + 1) * 64]


def queries_of(info, shards, weight, rows, gain, needed):
    return pl.pallas_call(
        query_kernel,
        in_specs=[SMEM] + [VMEM] * 7 + [ANY],
        out_specs=[VMEM] * 2,
        out_shape=[
            jax.ShapeDtypeStruct((HEADS, OWN, HD), BF16),
            jax.ShapeDtypeStruct((OWN + 16, 512), BF16),
        ],
        compiler_params=params(8),
        cost_estimate=pl.CostEstimate(
            flops=2 * 512 * 512 * 384, bytes_accessed=2000000, transcendentals=0
        ),
    )(info, *in_vmem(*shards, weight, rows), gain[None] * FACTOR, needed)


def assemble(info, shards):
    def kernel(info_ref, s0, s1, s3, s2, out_ref):
        gather_rows((s0, s1, s3, s2), 0, info_ref[5], out_ref)

    return pl.pallas_call(
        kernel,
        in_specs=[SMEM] + [VMEM] * 4,
        out_specs=VMEM,
        out_shape=jax.ShapeDtypeStruct((OWN + 16, 512), BF16),
        compiler_params=params(4),
    )(info, *in_vmem(*shards))


def store_rows(o_ref, base, results):
    lane = lax.broadcasted_iota(jnp.int32, (FRAME, HD), 1)
    marks = jnp.zeros((FRAME, HD), F32)
    for head, (mixed, peak, weight_sum) in enumerate(results):
        some = weight_sum > 0.0
        safe = jnp.where(some, weight_sum, 1.0)
        o_ref[pl.ds(pl.multiple_of(head * OWN + base, FRAME), FRAME), :] = (mixed / safe).astype(
            BF16
        )
        level = jnp.where(some, peak + jnp.log2(safe), NONE)
        marks = jnp.where(lane == head, level, marks)
    for half in range(2):
        turned = jnp.transpose(marks[half * HD : (half + 1) * HD])[0:8]
        first, second, third = split_bf16(turned, 3)
        at = pl.multiple_of(HEADS * OWN + (base // HD + half) * 32, 32)
        tail = jnp.concatenate([first, second, third, jnp.zeros((8, HD), F32)], axis=0)
        o_ref[pl.ds(at, 32), :] = tail.astype(BF16)


LONG = 12
SHORT = 4


def attend_group(info_ref, group, q_ref, o_ref, key_t, value):
    x_here, z_here, core = place_of(info_ref)
    group_frame = x_here * 16 + lax.rem(z_here + NZ - group, NZ) * 4 + core * 2

    def bounds(i):
        ends = []
        for edge in clip_of_frame(info_ref, group_frame + i):
            inside = [jnp.clip(edge - 16 * x - 4 * z_here, 0, 4) for x in range(NX)]
            ends.append(inside[0] + inside[1] + inside[2] + inside[3])
        return ends[0], ends[1] - ends[0]

    def rows_of(start, frames, base, shown=None):
        width = frames * FRAME
        start = pl.multiple_of(start * FRAME, FRAME)

        def scores_of(head):
            return jnp.dot(
                q_ref[head, pl.ds(base, FRAME), :],
                key_t[head, :, pl.ds(start, width)],
                preferred_element_type=F32,
            )

        scores = scores_of(0)
        results = []
        for head in range(HEADS):
            ahead = scores_of(head + 1) if head + 1 < HEADS else None
            if shown is not None:
                scores = jnp.where(shown, scores, NONE)
            top = jnp.max(scores, axis=-1, keepdims=True)
            weights = jnp.exp2(scores - top)
            if shown is not None:
                weights = jnp.where(shown, weights, 0.0)
            weight_sum = jnp.sum(weights, axis=-1, keepdims=True)
            mixed = jnp.dot(
                weights.astype(BF16),
                value[head, pl.ds(start, width), :],
                preferred_element_type=F32,
            )
            results.append((mixed, top, weight_sum))
            scores = ahead
        store_rows(o_ref, base, results)

    def one_frame(i, carry):
        first, count = bounds(i)
        base = pl.multiple_of(i * FRAME, FRAME)

        @pl.when(count == LONG)
        def _():
            rows_of(first, LONG, base)

        @pl.when(count != LONG)
        def _():
            start = jnp.minimum(first, KEYS // FRAME - SHORT)
            lane = lax.broadcasted_iota(jnp.int32, (FRAME, SHORT * FRAME), 1)
            low = (first - start) * FRAME
            rows_of(start, SHORT, base, (lane >= low) & (lane < low + count * FRAME))

        return carry

    lax.fori_loop(0, 2, one_frame, 0)


def project_block(ref, start, wk_ref, wv_ref, rows_ref, cols_ref, key_t, value):
    cells = ref[0:OWN, :]
    extra = ref[OWN : OWN + 16, :].astype(F32)
    scale = extra[0:1] + extra[1:2]
    keys = lax.dot_general(
        wk_ref[...], cells, (((1,), (1,)), ((), ())), preferred_element_type=F32
    )
    for head in range(HEADS):
        lanes = slice(head * HD, (head + 1) * HD)
        offset = jnp.concatenate([cols_ref[0, lanes, :]] * 4, axis=1)
        moved = jnp.concatenate([cols_ref[1, lanes, :]] * 4, axis=1)
        gain = jnp.concatenate([cols_ref[2, 0:HD, :]] * 4, axis=1)
        part = (keys[lanes] + offset) * scale + moved
        mean_square = jnp.mean(part * part, axis=0, keepdims=True)
        key_t[head, :, pl.ds(start, OWN)] = (
            part * lax.rsqrt(mean_square + EPSILON) * gain
        ).astype(BF16)
    down = jnp.concatenate(
        [
            jnp.transpose(jnp.broadcast_to(scale[:, j * HD : (j + 1) * HD], (HD, HD)))
            for j in range(4)
        ],
        axis=0,
    )
    values = jnp.dot(cells, wv_ref[...], preferred_element_type=F32) + rows_ref[0:1, 768:1152]
    for head in range(HEADS):
        lanes = slice(head * HD, (head + 1) * HD)
        value[head, pl.ds(start, OWN), :] = (
            values[:, lanes] * down + rows_ref[1:2, 768 + head * HD : 768 + (head + 1) * HD]
        ).astype(BF16)


def first_kernel(
    info_ref, q_hbm, a0, b0, a1, b1, a3, b3, a2, b2, wk_hbm, wv_hbm, rows_hbm, cols_hbm,
    o2, key_out, value_out, key_t, value, blocks, q2, wk_ref, wv_ref, rows_ref, cols_ref,
    sems,
):
    x_here, _, core = place_of(info_ref)
    weight_copies = fetch(
        (wk_hbm, wv_hbm, rows_hbm, cols_hbm), (wk_ref, wv_ref, rows_ref, cols_ref), sems
    )
    block_copies = fetch(
        (a0, b0, a1, b1, a3, b3, a2, b2), [blocks.at[i] for i in range(8)], sems, 4
    )
    (query_copy,) = fetch([q_hbm], [q2], sems, 12)
    for copy in weight_copies:
        copy.wait()
    for at in range(8):
        if at % 4 == 0:
            for copy in block_copies[at : at + 4]:
                copy.wait()
        source = lax.rem(x_here + (NX - (0, 1, 3, 2)[at // 2]), NX)
        core_at = core if at % 2 == 0 else 1 - core
        start = pl.multiple_of((source * 2 + core_at) * OWN, OWN)
        project_block(blocks.at[at], start, wk_ref, wv_ref, rows_ref, cols_ref, key_t, value)
    copies = fetch((key_t, value), (key_out, value_out), sems, 13)
    query_copy.wait()
    attend_group(info_ref, 2, q2, o2, key_t, value)
    for copy in copies:
        copy.wait()


PARTIAL = jax.ShapeDtypeStruct((HEADS * OWN + 128, HD), BF16)


def attend_first(info, query, near, far, wk, wv, rows, cols):
    return pl.pallas_call(
        first_kernel,
        in_specs=[SMEM] + [ANY] * 13,
        out_specs=[VMEM, ANY, ANY],
        out_shape=[
            PARTIAL,
            jax.ShapeDtypeStruct((HEADS, HD, KEYS), BF16),
            jax.ShapeDtypeStruct((HEADS, KEYS, HD), BF16),
        ],
        scratch_shapes=[
            pltpu.VMEM((HEADS, HD, KEYS), BF16),
            pltpu.VMEM((HEADS, KEYS, HD), BF16),
            pltpu.VMEM((8, OWN + 16, 512), BF16),
            pltpu.VMEM((HEADS, OWN, HD), BF16),
            pltpu.VMEM((384, 512), BF16),
            pltpu.VMEM((512, 384), BF16),
            pltpu.VMEM((8, 1152), F32),
            pltpu.VMEM((3, 384, HD), F32),
            pltpu.SemaphoreType.DMA((15,)),
        ],
        compiler_params=params(34),
        cost_estimate=pl.CostEstimate(
            flops=15000000000, bytes_accessed=10000000, transcendentals=0
        ),
    )(
        info,
        query,
        *[block for pair in zip(near, far) for block in pair],
        wk,
        wv,
        rows,
        cols,
    )


def next_kernel(groups, info_ref, key_t, value, *refs):
    count = len(groups)
    sources, refs = refs[:count], refs[-(count + 3) :]
    outs, queries, partial, sems = refs[:count], refs[count], refs[count + 1], refs[count + 2]
    for copy in fetch(sources, [queries.at[n] for n in range(count)], sems):
        copy.wait()

    def one_group(n, carry):
        group = groups[0] + n * 2
        attend_group(info_ref, group, queries.at[n], partial.at[n], key_t, value)
        return carry

    lax.fori_loop(0, count, one_group, 0)
    for copy in fetch([partial.at[n] for n in range(count)], outs, sems, count):
        copy.wait()


def attend_next(groups, info, queries, key_t, value, *needed):
    key_t, value = [
        pltpu.with_memory_space_constraint(array, pltpu.VMEM) for array in (key_t, value)
    ]
    return pl.pallas_call(
        functools.partial(next_kernel, groups),
        in_specs=[SMEM, VMEM, VMEM] + [ANY] * (len(groups) + len(needed)),
        out_specs=[ANY] * len(groups),
        out_shape=[PARTIAL] * len(groups),
        scratch_shapes=[
            pltpu.VMEM((len(groups), HEADS, OWN, HD), BF16),
            pltpu.VMEM((len(groups), *PARTIAL.shape), BF16),
            pltpu.SemaphoreType.DMA((2 * len(groups),)),
        ],
        compiler_params=params(28),
        cost_estimate=pl.CostEstimate(
            flops=8000000000 * len(groups), bytes_accessed=8000000, transcendentals=0
        ),
    )(info, key_t, value, *queries, *needed)


def merge_kernel(p0, p1, p2, p3, out_ref):
    parts = (p0, p1, p2, p3)
    for at in range(4):
        base = HEADS * OWN + at * 32
        levels = []
        for ref in parts:
            marks = ref[base : base + 32, :].astype(F32)
            levels.append(marks[0:8] + marks[8:16] + marks[16:24])
        top = functools.reduce(jnp.maximum, levels)
        shares = [jnp.exp2(level - top) for level in levels]
        weight_sum = functools.reduce(jnp.add, shares)
        stacked = jnp.concatenate([share / weight_sum for share in shares], axis=0)
        columns = jnp.transpose(
            jnp.concatenate([stacked, jnp.zeros((HD - 32, HD), F32)], axis=0)
        )
        for head in range(HEADS):
            rows = slice(head * OWN + at * HD, head * OWN + (at + 1) * HD)
            mixed = functools.reduce(
                jnp.add,
                [
                    ref[rows, :].astype(F32) * columns[:, i * 8 + head : i * 8 + head + 1]
                    for i, ref in enumerate(parts)
                ],
            )
            out_ref[head, at * HD : (at + 1) * HD, :] = mixed.astype(BF16)


def merge(parts):
    return pl.pallas_call(
        merge_kernel,
        in_specs=[VMEM] * 4,
        out_specs=VMEM,
        out_shape=jax.ShapeDtypeStruct((HEADS, OWN, HD), BF16),
        compiler_params=params(8),
    )(*in_vmem(*parts))


def per_device(
    section_in,
    norm_gain,
    conv_weight,
    conv_bias,
    lengths,
    embed_weight,
    embed_bias,
    mod_shift,
    mod_scale,
    qkv_weight,
    q_gain,
    k_gain,
):
    info = jnp.concatenate(
        [lengths, jnp.stack([lax.axis_index("tm"), lax.axis_index("band")])]
    ).astype(jnp.int32)
    above = halo(section_in[:, 7:8], 0, 1)
    below = halo(section_in[:, 0:1], 0, -1)
    cur = jnp.concatenate([above, section_in, below], axis=1)
    prev = halo(cur, 1, 0)
    qkv = jnp.transpose(qkv_weight, (1, 2, 0, 3)).reshape(9, 3072, HD)
    part, qkv_near = conv_newest(cur, norm_gain, conv_weight, qkv)
    section_out, send, embed_near = conv(
        info, cur, prev, part, norm_gain, conv_bias, embed_weight, embed_bias, conv_weight
    )
    wq, wk, wv, rows, cols = fold(
        embed_near, embed_bias, mod_shift, mod_scale, k_gain, qkv_near
    )
    shards = (send, shift_band(send, 1), shift_band(send, 3), shift_band(send, 2))
    across = shift_tm(send, dx=2)
    query, xr = queries_of(info, shards, wq, rows, q_gain, across)
    far_own = shift_tm(xr, swap=True)
    q1, q3, q2 = shift_tm(query, dz=1), shift_tm(query, dz=3), shift_tm(query, dz=2)
    g1, g3, g2 = shift_band(across, 1), shift_band(across, 3), shift_band(across, 2)
    a1 = after(shift_tm(xr, dx=1), q2, g2)
    a3 = after(shift_tm(xr, dx=3), g1, g3)
    a2 = assemble(info, (across, g1, g3, g2))
    near = (xr, a1, a3, a2)
    far = (far_own,) + tuple(shift_tm(part, swap=True) for part in near[1:])
    o2, key_t, value = attend_first(info, q2, near, far, wk, wv, rows, cols)
    p2 = shift_tm(o2, dz=2)
    o1, o3 = attend_next((1, 3), info, (q1, q3), key_t, value)
    p1, p3 = shift_tm(o1, dz=3), shift_tm(o3, dz=1)
    (o0,) = attend_next((0,), info, (query,), key_t, value, p2)
    parts = (o0, p1, p3, p2)
    attended = jnp.transpose(merge(parts), (1, 0, 2))
    return (section_out, attended)


def solution(mesh):
    return jax.shard_map(
        per_device,
        mesh=mesh,
        in_specs=(
            P("tm", "band", None, None),
            P(),
            P(),
            P(),
            P(),
            P(),
            P(),
            P(),
            P(),
            P(None, None, "band", None),
            P(),
            P(),
        ),
        out_specs=(P("tm", "band", None, None), P("tm", "band", None)),
        check_vma=False,
    )
```
